32 devices in a mesh: dp: 8 (over y, x, core), shard: 4 (over z).
Axes of the slice: x: 2, y: 2, z: 4, core: 2. Of those that a mesh axis runs over, the one named last changes fastest.
Arguments:
- tokens: bfloat16 [2, 8192, 1024], P(None, ('dp', 'shard')), may hold values from -6 to 6
- positions: int32 [2, 8192], P(None, ('dp', 'shard')), may hold values from -1 to 255, as said below
- cotangent: bfloat16 [2, 8192, 1024], P(None, ('dp', 'shard')), may hold values from -6 to 6
- norm_gain: bfloat16 [1024], P(('dp', 'shard')), may hold values from 0.099609375 to 1.8984375
- in_weight: bfloat16 [1024, 3072], P(('dp', 'shard')), may hold values from -0.1875 to 0.1875
- conv_weight: bfloat16 [3, 1024], P(None, ('dp', 'shard')), may hold values from -3 to 3
- out_weight: bfloat16 [1024, 1024], P(('dp', 'shard')), may hold values from -0.1875 to 0.1875
- ffn_gain: bfloat16 [1024], P(('dp', 'shard')), may hold values from 0.099609375 to 1.8984375
- gate_weight: bfloat16 [1024, 4608], P(('dp', 'shard')), may hold values from -0.1875 to 0.1875
- up_weight: bfloat16 [1024, 4608], P(('dp', 'shard')), may hold values from -0.1875 to 0.1875
- down_weight: bfloat16 [4608, 1024], P(('dp', 'shard')), may hold values from -0.125 to 0.125
Outputs:
- block_out: bfloat16 [2, 8192, 1024], P(None, ('dp', 'shard'))
- input_grad: bfloat16 [2, 8192, 1024], P(None, ('dp', 'shard'))
- grad_norm_gain: float32 [1024], P(('dp', 'shard'))
- grad_in_weight: float32 [1024, 3072], P(('dp', 'shard'))
- grad_conv_weight: float32 [3, 1024], P(None, ('dp', 'shard'))
- grad_out_weight: float32 [1024, 1024], P(('dp', 'shard'))
- grad_ffn_gain: float32 [1024], P(('dp', 'shard'))
- grad_gate_weight: float32 [1024, 4608], P(('dp', 'shard'))
- grad_up_weight: float32 [1024, 4608], P(('dp', 'shard'))
- grad_down_weight: float32 [4608, 1024], P(('dp', 'shard'))
The draws below stay inside these ranges and needn't reach their ends.
Inputs may be any that keep to these rules, and one draw needn't show every extreme that they name: `positions`: each device's 256 rows of a micro-batch hold whole sequences one after another, each starting at a block boundary with place 0 and taking whole blocks of 128 rows, its last block padded with -1; padding blocks follow the sequences. In every micro-batch some device holds one sequence of exactly 256 rows.
All inputs are finite; a program needn't handle non-finite values.
Results may differ from the reference program's by a relative error of at most 0.0096.
Values may be sent and summed in bfloat16 or wider, within the bound.
No kernel may reach another device: no remote copies, remote signals or barrier semaphores. Data moves between devices by JAX's collectives and lax.ppermute only.
A program may use at most 256 MiB of HBM per device.

```python
import jax
import jax.numpy as jnp
from jax import lax

D = 1024
FF = 4608
CONV = 3
BLOCK = 128
BLK_DEV = 2
MICRO = 2
ROWS_DEV = 256
ROWS = 8192


def draw_positions(key, part):
    key = jax.random.fold_in(key, 11)
    devices_all = ROWS // ROWS_DEV
    keys = jax.random.split(key, 4)
    full_device = jax.random.randint(keys[0], (MICRO, 1), 0, devices_all)
    device_ids = jnp.arange(devices_all, dtype=jnp.int32)[None, :]
    forced = device_ids == full_device
    least_blocks = max(BLK_DEV // 2, 1)
    live_blocks = jax.random.randint(keys[1], (MICRO, devices_all), least_blocks, BLK_DEV + 1)
    live_blocks = jnp.where(forced, BLK_DEV, live_blocks)
    block_ids = jnp.arange(BLK_DEV, dtype=jnp.int32)
    starts = jax.random.randint(keys[2], (MICRO, devices_all, BLK_DEV), 0, 2)
    starts = jnp.where(block_ids == 0, 1, starts)
    starts = jnp.where(forced[:, :, None] & (block_ids > 0), 0, starts)
    first_block = lax.cummax(block_ids * starts, axis=2)
    next_start = jnp.concatenate([starts[:, :, 1:], jnp.ones_like(starts[:, :, :1])], axis=2)
    last_block = (next_start == 1) | (block_ids == live_blocks[:, :, None] - 1)
    tails = jax.random.randint(keys[3], (MICRO, devices_all, BLK_DEV), 1, BLOCK + 1)
    tails = jnp.where(forced[:, :, None], BLOCK, tails)
    offsets = jnp.arange(BLOCK, dtype=jnp.int32)
    places = (block_ids - first_block)[:, :, :, None] * BLOCK + offsets
    alive = (block_ids < live_blocks[:, :, None])[:, :, :, None] & ((~last_block)[:, :, :, None] | (offsets < tails[:, :, :, None]))
    places = jnp.where(alive, places, -1)
    return places.reshape(MICRO, ROWS).astype(jnp.int32)


def spiked(array, rng, source, target, parts, factor):
    owner, partner = [(jnp.arange(array.shape[dim]) // (array.shape[dim] // parts)).reshape([-1 if axis == dim else 1 for axis in range(array.ndim)]) for dim in (source, target)]
    chosen = jax.random.permutation(rng, parts)[partner]
    strong = (owner == chosen) | (owner == (partner + parts // 2) % parts)
    return jnp.where(strong, factor * array, array)


def shard_levels(stream_key, extent, cuts, smallest, top_value):
    level = 1.0
    for dim, blocks in cuts:
        draws = jax.random.uniform(jax.random.fold_in(jax.random.fold_in(stream_key, 6), dim), (blocks,), jnp.float32, smallest / len(cuts), top_value / len(cuts))
        level = level * jnp.repeat(jnp.exp(draws), extent[dim] // blocks).reshape((-1,) + (1,) * (len(extent) - 1 - dim))
    return level


def centred(key, dims, width, bound, cuts=(), kind=jnp.bfloat16):
    drawn = width * jax.random.normal(key, dims, jnp.float32)
    if cuts:
        drawn = drawn * shard_levels(key, dims, cuts, -0.22, 0.18)
    return jnp.clip(drawn, -bound, bound).astype(kind)


def noise_with(stream_key, extent, spread, reach, cuts, heavy, kind=jnp.bfloat16):
    entries = spread * jax.random.normal(stream_key, extent, jnp.float32)
    if cuts:
        entries = entries * shard_levels(stream_key, extent, cuts, -0.22, 0.18)
    return jnp.clip(spiked(entries, jax.random.fold_in(stream_key, 3), *heavy), -reach, reach).astype(kind)


def setup_inputs(seed: int = 0) -> dict:
    seeds = jax.random.split(jax.random.key(seed), 12)
    tokens = noise_with(seeds[0], (MICRO, ROWS, D), 1.0, 6.0, ((1, 32),), (1, 2, 32, 2.75))
    positions = draw_positions(jax.random.fold_in(seeds[11], 71), 0)
    cotangent = centred(seeds[2], (MICRO, ROWS, D), 1.0, 6.0, ((1, 32),))
    norm_gain = jnp.clip(1.0 + 0.18 * jax.random.normal(seeds[3], (D,), jnp.float32), 0.099609375, 1.8984375).astype(jnp.bfloat16)
    in_weight = centred(seeds[4], (D, 3 * D), D ** -0.5, 0.1875, ((0, 32),))
    conv_weight = centred(seeds[5], (CONV, D), 0.6, 3.0, ((1, 32),))
    out_weight = centred(seeds[6], (D, D), D ** -0.5, 0.1875, ((0, 32),))
    ffn_gain = jnp.clip(1.0 + 0.18 * jax.random.normal(seeds[7], (D,), jnp.float32), 0.099609375, 1.8984375).astype(jnp.bfloat16)
    gate_weight = centred(seeds[8], (D, FF), D ** -0.5, 0.1875, ((0, 32),))
    up_weight = centred(seeds[9], (D, FF), D ** -0.5, 0.1875, ((0, 32),))
    down_weight = centred(seeds[10], (FF, D), (FF // 2) ** -0.5, 0.125, ((0, 32),))
    return dict(tokens=tokens, positions=positions, cotangent=cotangent, norm_gain=norm_gain, in_weight=in_weight, conv_weight=conv_weight, out_weight=out_weight, ffn_gain=ffn_gain, gate_weight=gate_weight, up_weight=up_weight, down_weight=down_weight)


EPSILON = 1e-05

@jax.custom_vjp
def low(v):
    return lax.optimization_barrier(v.astype(jnp.bfloat16)).astype(jnp.float32)

@jax.custom_vjp
def low_back(v):
    return v

def low_keep(v):
    return (low(v), None)

def low_pass(kept, grad):
    return (grad,)

def back_keep(v):
    return (v, None)

def back_low(kept, grad):
    return (low(grad),)
low.defvjp(low_keep, low_pass)
low_back.defvjp(back_keep, back_low)

def normed(values, scales):
    return values * lax.rsqrt(lax.optimization_barrier(jnp.mean(values * values, axis=-1, keepdims=True)) + EPSILON) * scales

def product(left_side, right_side):
    return jnp.dot(left_side, right_side, precision=lax.Precision.HIGHEST, preferred_element_type=jnp.float32)

def causal_conv(mixed_rows, kernel, places):
    zero_row = jnp.zeros((1, mixed_rows.shape[1]), mixed_rows.dtype)
    earlier = jnp.concatenate([zero_row, mixed_rows[:-1]], axis=0)
    earliest = jnp.concatenate([zero_row, zero_row, mixed_rows[:-2]], axis=0)
    first_mask = (places >= 1).astype(mixed_rows.dtype)[:, None]
    second_mask = (places >= 2).astype(mixed_rows.dtype)[:, None]
    return kernel[0] * mixed_rows + kernel[1] * earlier * first_mask + kernel[2] * earliest * second_mask

def conv_block(inputs, weights, places):
    norm_gain, in_weight, conv_weight, out_weight, ffn_gain, gate_weight, up_weight, down_weight = weights
    features = inputs.shape[1]
    live_rows = (places >= 0).astype(inputs.dtype)[:, None]
    first_normed = low(normed(inputs, norm_gain))
    projected = low_back(product(first_normed, in_weight))
    b_part = projected[:, :features]
    c_part = projected[:, features:2 * features]
    x_part = projected[:, 2 * features:]
    mixer_in = low(c_part * causal_conv(b_part * x_part, conv_weight, places))
    mixer_out = low_back(product(mixer_in, out_weight))
    middle = inputs + live_rows * mixer_out
    second_normed = low(normed(middle, ffn_gain))
    gate_value = low_back(product(second_normed, gate_weight))
    up_value = low_back(product(second_normed, up_weight))
    hidden = low(jax.nn.silu(gate_value) * up_value)
    ffn_out = low_back(product(hidden, down_weight))
    return middle + live_rows * ffn_out

def reference(tokens, positions, cotangent, norm_gain, in_weight, conv_weight, out_weight, ffn_gain, gate_weight, up_weight, down_weight):
    weights = tuple((weight.astype(jnp.float32) for weight in (norm_gain, in_weight, conv_weight, out_weight, ffn_gain, gate_weight, up_weight, down_weight)))
    slices = MICRO * (ROWS // ROWS_DEV)
    inputs = tokens.astype(jnp.float32).reshape(slices, ROWS_DEV, D)
    cotangents = cotangent.astype(jnp.float32).reshape(slices, ROWS_DEV, D)
    places = positions.reshape(slices, ROWS_DEV)

    def scan_step(totals, sliced):
        rows_in, rows_cot, rows_pos = sliced
        result, pullback = jax.vjp(lambda values, params: conv_block(values, params, rows_pos), rows_in, weights)
        in_gradient, weight_grads = pullback(rows_cot)
        totals = jax.tree.map(lambda running, gradient: running + gradient, totals, weight_grads)
        return (totals, (result, in_gradient))
    zero_grads = jax.tree.map(jnp.zeros_like, weights)
    totals, (results, in_gradients) = lax.scan(scan_step, zero_grads, (inputs, cotangents, places))
    block_out = results.reshape(MICRO, ROWS, D).astype(jnp.bfloat16)
    input_grad = in_gradients.reshape(MICRO, ROWS, D).astype(jnp.bfloat16)
    return (block_out, input_grad, totals[0], totals[1], totals[2], totals[3], totals[4], totals[5], totals[6], totals[7])
```

```python
from functools import reduce

import jax
import jax.numpy as jnp
from jax import lax
from jax.experimental import pallas as pl
from jax.experimental.pallas import tpu as pltpu
from jax.sharding import Mesh, PartitionSpec as P

EPSILON = 1e-05
TEAM = 4
EXTRA_ROWS = 16
ROW_TILE = 256
bf16 = jnp.bfloat16
f32 = jnp.float32


def forward_dot(left_side, right_side):
    return jnp.dot(left_side, right_side, preferred_element_type=f32)


def rows_dot(left_side, right_side):
    return lax.dot_general(
        left_side, right_side, (((0,), (0,)), ((), ())), preferred_element_type=f32
    )


def back_dot(left_side, right_side):
    return lax.dot_general(
        left_side, right_side, (((1,), (1,)), ((), ())), preferred_element_type=f32
    )


def swap_core(values):
    return lax.ppermute(values, "c", [(0, 1), (1, 0)])


def swap_chip(values):
    return lax.ppermute(values, "x", [(0, 1), (1, 0)])


def swap_both(values):
    return lax.ppermute(values, ("x", "c"), [(i, i ^ 3) for i in range(TEAM)])


def reorder(blocks):
    odd_core = lax.axis_index("c") == 1
    odd_chip = lax.axis_index("x") == 1
    b0, b1, b2, b3 = blocks
    b0, b1 = jnp.where(odd_core, b1, b0), jnp.where(odd_core, b0, b1)
    b2, b3 = jnp.where(odd_core, b3, b2), jnp.where(odd_core, b2, b3)
    b0, b2 = jnp.where(odd_chip, b2, b0), jnp.where(odd_chip, b0, b2)
    b1, b3 = jnp.where(odd_chip, b3, b1), jnp.where(odd_chip, b1, b3)
    return [b0, b1, b2, b3]


def exchange(blocks):
    near = reorder(blocks)
    came = [near[0], swap_core(near[1]), swap_chip(near[2]), swap_both(near[3])]
    return reorder(came)


def team_rows(rows):
    across = swap_chip(rows)
    return jnp.concatenate([rows, swap_core(rows), across, swap_core(across)], axis=0)


def team_sum(partial):
    count = partial.shape[0] // TEAM
    sent = jnp.concatenate([partial[count : 2 * count], partial[3 * count :]], axis=0)
    came = swap_core(sent).astype(f32)
    own = partial[:count].astype(f32) + came[:count]
    other = partial[2 * count : 3 * count].astype(f32) + came[count:]
    return own + swap_chip(other.astype(bf16)).astype(f32)


def take(blocks, index):
    return lax.dynamic_index_in_dim(blocks, index, axis=0, keepdims=False)


def swap_group(values):
    return lax.ppermute(values, "g", [(0, 1), (1, 0)])


def line_gather(block):
    place = lax.axis_index("s")
    right, left = [block], [block]
    for step in range(1, 4):
        right.append(lax.ppermute(right[-1], "s", [(i, i + 1) for i in range(step - 1, 3)]))
        left.append(lax.ppermute(left[-1], "s", [(i + 1, i) for i in range(4 - step)]))
    blocks = [block] + [jnp.where(place >= k, right[k], left[4 - k]) for k in range(1, 4)]
    return blocks, [lax.rem(place + 4 - k, 4) for k in range(4)]


def line_scatter(blocks):
    place = lax.axis_index("s")
    total = take(blocks, place).astype(f32)
    for sign in (1, -1):
        came = None
        for step in range(1, 4):
            sent = take(blocks, jnp.clip(place + sign * (4 - step), 0, 3))
            if came is not None:
                sent = (sent.astype(f32) + came.astype(f32)).astype(bf16)
            if sign == 1:
                pairs = [(i, i + 1) for i in range(step)]
            else:
                pairs = [(i, i - 1) for i in range(4 - step, 4)]
            came = lax.ppermute(sent, "s", pairs)
        total = total + came.astype(f32)
    return total


def gather_first(shard, unpack):
    groups, slots = lax.axis_size("g"), lax.axis_size("s")
    if groups == 2 and slots == 4:
        low = lax.axis_index("g") == 0
        other = swap_group(shard)
        both = jnp.stack([jnp.where(low, shard, other), jnp.where(low, other, shard)])
        results = [jnp.zeros((2, 4) + part.shape, part.dtype) for part in unpack(shard)]
        for block, source in zip(*line_gather(both)):
            results = [
                lax.dynamic_update_slice(
                    whole, part[:, None], (0, source) + (0,) * (part.ndim - 1)
                )
                for whole, part in zip(results, jax.vmap(unpack)(block))
            ]
        return results
    every = lax.all_gather(shard, ("g", "s"), axis=0, tiled=False)
    results = jax.vmap(unpack)(every)
    return [part.reshape((groups, slots) + part.shape[1:]) for part in results]


def scatter_first(part):
    groups, slots = part.shape[:2]
    if groups == 2 and slots == 4:
        row = lax.axis_index("g")
        came = swap_group(take(part, 1 - row))
        return line_scatter((take(part, row).astype(f32) + came.astype(f32)).astype(bf16))
    flat = part.reshape((groups * slots,) + part.shape[2:]).astype(f32)
    return lax.psum_scatter(flat, ("g", "s"), scatter_dimension=0, tiled=False)


def scatter_rest(part):
    if part.shape[0] > 8:
        part = part.astype(f32)
    return lax.psum_scatter(part, ("g", "s"), scatter_dimension=0, tiled=False)


def feed_forward_kernel(
    normed_ref,
    grad_ref,
    gate_ref,
    up_ref,
    down_ref,
    hidden_ref,
    gate_grad_ref,
    up_grad_ref,
    out_ref,
    normed_grad_ref,
):
    gate_value = forward_dot(normed_ref[...], gate_ref[...])
    up_value = forward_dot(normed_ref[...], up_ref[...])
    sigmoid = jax.nn.sigmoid(gate_value)
    silu = gate_value * sigmoid
    hidden = (silu * up_value).astype(bf16)
    hidden_ref[...] = hidden
    hidden_grad = back_dot(grad_ref[...], down_ref[...])
    gate_grad = hidden_grad * up_value * (sigmoid * (1 + gate_value * (1 - sigmoid)))
    gate_grad = gate_grad.astype(bf16)
    up_grad = (hidden_grad * silu).astype(bf16)
    gate_grad_ref[...] = gate_grad
    up_grad_ref[...] = up_grad
    normed_grad = back_dot(gate_grad, gate_ref[...]) + back_dot(up_grad, up_ref[...])
    normed_grad_ref[...] = normed_grad.astype(bf16)
    out_ref[...] = forward_dot(hidden, down_ref[...]).astype(bf16)


def feed_forward(normed, grad, gate_full, up_full, down_full):
    rows, features = normed.shape
    width = gate_full.shape[1]
    tile = min(ROW_TILE, rows)

    def row_block(columns):
        return pl.BlockSpec((tile, columns), lambda i: (i, 0))

    def whole(shape):
        return pl.BlockSpec(shape, lambda i: (0, 0))

    wide = jax.ShapeDtypeStruct((rows, width), bf16)
    model = jax.ShapeDtypeStruct((rows, features), bf16)
    return pl.pallas_call(
        feed_forward_kernel,
        grid=(rows // tile,),
        in_specs=[
            row_block(features),
            row_block(features),
            whole(gate_full.shape),
            whole(up_full.shape),
            whole(down_full.shape),
        ],
        out_specs=[row_block(width)] * 3 + [row_block(features)] * 2,
        out_shape=[wide] * 3 + [model] * 2,
        compiler_params=pltpu.CompilerParams(vmem_limit_bytes=52 * 1024 * 1024),
        cost_estimate=pl.CostEstimate(
            flops=12 * rows * features * width,
            bytes_accessed=6 * features * width + 6 * rows * width + 8 * rows * features,
            transcendentals=rows * width,
        ),
    )(normed, grad, gate_full, up_full, down_full)


def shifted_down(rows, step):
    return jnp.concatenate(
        [jnp.zeros((step, rows.shape[1]), rows.dtype), rows[:-step]], axis=0
    )


def shifted_up(rows, step):
    return jnp.concatenate(
        [rows[step:], jnp.zeros((step, rows.shape[1]), rows.dtype)], axis=0
    )


def inverse_rms(values):
    return lax.rsqrt(jnp.mean(values * values, axis=-1, keepdims=True) + EPSILON)


def norm_back(values, scale, weighted):
    return scale * weighted - values * (
        scale * scale * scale * jnp.mean(weighted * values, axis=-1, keepdims=True)
    )


def per_device(
    tokens,
    positions,
    cotangent,
    norm_gain,
    in_weight,
    conv_weight,
    out_weight,
    ffn_gain,
    gate_weight,
    up_weight,
    down_weight,
):
    micro, micro_rows, features = tokens.shape
    share = in_weight.shape[0]
    hidden_share = down_weight.shape[0]
    hidden_width = gate_weight.shape[1]
    taps = conv_weight.shape[0]
    groups = lax.axis_size("g")
    slots = lax.axis_size("s")
    chan_run = slots * share
    hid_run = slots * hidden_share
    chan = groups * chan_run
    hid = groups * hid_run

    def by_place(weight, parts, run):
        split = weight.reshape(share, parts, groups, TEAM, run)
        return jnp.transpose(split, (3, 0, 1, 2, 4)).reshape(TEAM, share, parts * groups * run)

    def side_by_side(block, width):
        return jnp.concatenate(
            [block[..., j * share : (j + 1) * share, :width] for j in range(TEAM)], axis=-1
        )

    def stacked(block, width):
        return jnp.concatenate(
            [block[..., j * width : (j + 1) * width] for j in range(TEAM)], axis=-2
        )

    in_blocks = by_place(in_weight, 3, chan_run)
    in_mine = jnp.concatenate(exchange([in_blocks[j] for j in range(TEAM)]), axis=0)
    gains = jnp.concatenate([norm_gain, ffn_gain]).reshape(1, 2 * share)
    near_gains = team_rows(gains)
    gains_row = jnp.concatenate(reorder([near_gains[j : j + 1] for j in range(TEAM)]), axis=1)
    pair_blocks = jnp.concatenate(
        [by_place(gate_weight, 1, hid_run), by_place(up_weight, 1, hid_run)], axis=2
    )
    pair_mine = jnp.concatenate(exchange([pair_blocks[j] for j in range(TEAM)]), axis=0)

    def as_row(values):
        return jnp.pad(values, ((0, 0), (0, features - values.shape[1])))

    first_pack = jnp.concatenate(
        [
            jnp.concatenate([in_mine, stacked(out_weight, chan)], axis=1),
            as_row(conv_weight.reshape(1, taps * share)),
            as_row(gains_row),
            jnp.zeros((EXTRA_ROWS - 2, features), bf16),
        ],
        axis=0,
    )
    tall = TEAM * share

    def first_unpack(block):
        return [
            block[:tall, : 3 * chan].reshape(TEAM, share, 3 * chan),
            side_by_side(block[:tall, 3 * chan :], chan),
            block[tall, : taps * share].reshape(taps, share),
            block[tall + 1, : 2 * tall].reshape(TEAM, 2, share),
        ]

    in_all, out_all, conv_all, gains_all = gather_first(first_pack, first_unpack)

    full = 2 * hid // features
    rest = 2 * hid - full * features

    def rest_pack(pair, down):
        blocks = [pair[..., k * features : (k + 1) * features] for k in range(full)]
        if rest:
            blocks.append(side_by_side(pair[..., full * features :], rest))
        return jnp.concatenate(blocks + [down], axis=-2)

    def rest_unpack(packed):
        blocks = [packed[..., k * tall : (k + 1) * tall, :] for k in range(full)]
        base = full * tall
        if rest:
            blocks.append(stacked(packed[..., base : base + share, :], rest))
            base += share
        return jnp.concatenate(blocks, axis=-1), packed[..., base:, :]

    rest_all = lax.all_gather(
        rest_pack(pair_mine, down_weight), ("g", "s"), axis=0, tiled=False
    )
    pair_all, down_all = rest_unpack(rest_all)

    def natural(gathered):
        width = gathered.shape[-1]
        split = gathered.reshape(groups, slots, TEAM, share, width)
        return jnp.transpose(split, (0, 2, 1, 3, 4)).reshape(features, width)

    in_full = jnp.transpose(in_all, (0, 2, 1, 3, 4)).reshape(features, 3 * chan)
    out_full = out_all.reshape(chan, features)
    conv_full = jnp.transpose(conv_all, (2, 0, 1, 3)).reshape(taps, chan).astype(f32)
    gains_full = jnp.transpose(gains_all, (3, 0, 2, 1, 4)).reshape(2, features).astype(f32)
    norm_full, ffn_full = gains_full[0], gains_full[1]
    gate_full = natural(pair_all[..., :hid])
    up_full = natural(pair_all[..., hid:])
    down_full = down_all.reshape(hid, features)

    each = range(micro)
    team_tokens = [team_rows(tokens[m]) for m in each]
    team_places = [team_rows(positions[m][:, None]) for m in each]
    live = [(positions[m] >= 0).astype(f32)[:, None] for m in each]
    upstream = [cotangent[m].astype(f32) for m in each]
    ffn_grad = [team_rows((live[m] * upstream[m]).astype(bf16)) for m in each]
    inputs = [tokens[m].astype(f32) for m in each]

    def mixer(m):
        values = team_tokens[m].astype(f32)
        first_normed = (values * inverse_rms(values) * norm_full).astype(bf16)
        projected = forward_dot(first_normed, in_full)
        b_part = projected[:, :chan]
        c_part = projected[:, chan : 2 * chan]
        x_part = projected[:, 2 * chan :]
        mixed = b_part * x_part
        mask_one = (team_places[m] >= 1).astype(f32)
        mask_two = (team_places[m] >= 2).astype(f32)
        mixed_one = mask_one * shifted_down(mixed, 1)
        mixed_two = mask_two * shifted_down(mixed, 2)
        convolved = conv_full[0] * mixed + conv_full[1] * mixed_one + conv_full[2] * mixed_two
        mixer_in = (c_part * convolved).astype(bf16)
        middle = inputs[m] + live[m] * team_sum(forward_dot(mixer_in, out_full).astype(bf16))
        second_scale = inverse_rms(middle)
        second_normed = team_rows((middle * second_scale * ffn_full).astype(bf16))
        kept = (first_normed, b_part, c_part, x_part, mixed, mixed_one, mixed_two)
        return kept + (mask_one, mask_two, convolved, mixer_in), middle, second_scale, second_normed

    def feed(m, second_normed):
        return feed_forward(second_normed, ffn_grad[m], gate_full, up_full, down_full)

    def mixer_back(m, kept, middle, second_scale, normed_grad):
        first_normed, b_part, c_part, x_part, mixed, mixed_one, mixed_two = kept[:7]
        mask_one, mask_two, convolved, mixer_in = kept[7:]
        second_weighted = ffn_full * team_sum(normed_grad)
        middle_grad = upstream[m] + norm_back(middle, second_scale, second_weighted)
        mixer_grad = team_rows((live[m] * middle_grad).astype(bf16))
        mixer_in_grad = back_dot(mixer_grad, out_full)
        c_grad = mixer_in_grad * convolved
        conv_grad = mixer_in_grad * c_part
        mixed_grad = (
            conv_full[0] * conv_grad
            + conv_full[1] * shifted_up(mask_one * conv_grad, 1)
            + conv_full[2] * shifted_up(mask_two * conv_grad, 2)
        )
        projected_grad = jnp.concatenate(
            [mixed_grad * x_part, c_grad, mixed_grad * b_part], axis=1
        ).astype(bf16)
        grad_conv = jnp.stack(
            [
                jnp.sum(conv_grad * mixed, axis=0),
                jnp.sum(conv_grad * mixed_one, axis=0),
                jnp.sum(conv_grad * mixed_two, axis=0),
            ]
        )
        return middle_grad, mixer_grad, projected_grad, grad_conv

    def by_owner(grad):
        width = grad.shape[-1]
        split = grad.astype(bf16).reshape(groups, TEAM, slots, share, width)
        return jnp.transpose(split, (0, 2, 1, 3, 4)).reshape(groups, slots, tall, width)

    def total(terms):
        return reduce(jnp.add, terms)

    kept, middle, second_scale, second_normed = zip(*[mixer(m) for m in each])
    hidden, gate_grad, up_grad, out_part, normed_grad = zip(
        *[feed(m, second_normed[m]) for m in each]
    )
    middle_grad, mixer_grad, projected_grad, conv_parts = zip(
        *[mixer_back(m, kept[m], middle[m], second_scale[m], normed_grad[m]) for m in each]
    )

    pair_part = jnp.concatenate(
        [
            by_owner(total([rows_dot(second_normed[m], gate_grad[m]) for m in each])),
            by_owner(total([rows_dot(second_normed[m], up_grad[m]) for m in each])),
        ],
        axis=3,
    )
    down_part = total([rows_dot(hidden[m], ffn_grad[m]) for m in each]).astype(bf16)
    owners = groups * slots
    rest_part = rest_pack(
        pair_part.reshape(owners, tall, 2 * hid),
        down_part.reshape(owners, hidden_share, features),
    )
    pair_sum, down_sum = rest_unpack(scatter_rest(rest_part))

    in_part = by_owner(total([rows_dot(kept[m][0], projected_grad[m]) for m in each]))
    out_grad_part = total([rows_dot(kept[m][10], mixer_grad[m]) for m in each]).astype(bf16)
    out_grad_part = stacked(out_grad_part.reshape(groups, slots, share, features), chan)
    conv_rows = jnp.transpose(
        total(conv_parts).reshape(taps, groups, slots, share), (1, 2, 0, 3)
    ).reshape(groups, slots, 1, taps * share)
    conv_rows = jnp.pad(
        conv_rows.astype(bf16),
        ((0, 0), (0, 0), (0, EXTRA_ROWS - 1), (0, features - taps * share)),
    )
    first_sum = scatter_first(
        jnp.concatenate(
            [jnp.concatenate([in_part, out_grad_part], axis=3), conv_rows], axis=2
        )
    )

    block_out = jnp.stack(
        [(middle[m] + live[m] * team_sum(out_part[m])).astype(bf16) for m in each]
    )
    input_grads = []
    for m in each:
        weighted = norm_full * team_sum(back_dot(projected_grad[m], in_full).astype(bf16))
        scale = inverse_rms(inputs[m])
        input_grads.append(
            (middle_grad[m] + norm_back(inputs[m], scale, weighted)).astype(bf16)
        )

    def own_rows(summed, parts, run):
        blocks = [
            summed[j * share : (j + 1) * share].astype(bf16) for j in range(TEAM)
        ]
        came = [block.reshape(share, parts, groups, 1, run) for block in exchange(blocks)]
        joined = jnp.concatenate(came, axis=3)
        return joined.reshape(share, parts * groups * TEAM * run).astype(f32)

    pair_rows = own_rows(pair_sum, 2, hid_run)
    gate_rows = pair_rows[:, :hidden_width]
    up_rows = pair_rows[:, hidden_width:]
    in_rows = own_rows(first_sum[:tall, : 3 * chan], 3, chan_run)
    grad_out = side_by_side(first_sum[:tall, 3 * chan :], chan).astype(f32)
    grad_conv = first_sum[tall, : taps * share].reshape(taps, share).astype(f32)
    grad_norm_gain = jnp.sum(in_weight.astype(f32) * in_rows, axis=1) / norm_gain.astype(f32)
    grad_ffn_gain = jnp.sum(
        gate_weight.astype(f32) * gate_rows + up_weight.astype(f32) * up_rows, axis=1
    ) / ffn_gain.astype(f32)
    return (
        block_out,
        jnp.stack(input_grads),
        grad_norm_gain,
        in_rows,
        grad_conv,
        grad_out,
        grad_ffn_gain,
        gate_rows,
        up_rows,
        down_sum.astype(f32),
    )


def solution(mesh):
    groups = mesh.shape["dp"] // TEAM
    teams = Mesh(
        mesh.devices.reshape(groups, 2, 2, mesh.shape["shard"]), ("g", "x", "c", "s")
    )
    every = ("g", "x", "c", "s")
    return jax.shard_map(
        per_device,
        mesh=teams,
        in_specs=(
            P(None, every, None),
            P(None, every),
            P(None, every, None),
            P(every),
            P(every, None),
            P(None, every),
            P(every, None),
            P(every),
            P(every, None),
            P(every, None),
            P(every, None),
        ),
        out_specs=(
            P(None, every, None),
            P(None, every, None),
            P(every),
            P(every, None),
            P(None, every),
            P(every, None),
            P(every),
            P(every, None),
            P(every, None),
            P(every, None),
        ),
        check_vma=False,
    )
```

```python
from functools import partial, reduce

import jax
import jax.numpy as jnp
from jax import lax
from jax.experimental import pallas as pl
from jax.experimental.pallas import tpu as pltpu
from jax.sharding import Mesh, PartitionSpec as P

EPSILON = 1e-05
TEAM = 4
CREW = 8
EXTRA_ROWS = 16
ROW_TILE = 512
bf16 = jnp.bfloat16
f32 = jnp.float32


def forward_dot(left_side, right_side):
    return jnp.dot(left_side, right_side, preferred_element_type=f32)


def rows_dot(left_side, right_side):
    return lax.dot_general(
        left_side, right_side, (((0,), (0,)), ((), ())), preferred_element_type=f32
    )


def back_dot(left_side, right_side):
    return lax.dot_general(
        left_side, right_side, (((1,), (1,)), ((), ())), preferred_element_type=f32
    )


def swap_core(values):
    return lax.ppermute(values, "c", [(0, 1), (1, 0)])


def swap_chip(values):
    return lax.ppermute(values, "x", [(0, 1), (1, 0)])


def swap_row(values):
    return lax.ppermute(values, "y", [(0, 1), (1, 0)])


def swap_far(values, distance):
    axes = ("y", "x", "c")
    return lax.ppermute(values, axes, [(i, i ^ distance) for i in range(CREW)])


def after(values, token):
    return values + (token.ravel()[0] * 0).astype(values.dtype)


def reorder(blocks):
    blocks = list(blocks)
    for bit, axis in ((1, "c"), (2, "x"), (4, "y"))[: len(blocks).bit_length() - 1]:
        odd = lax.axis_index(axis) == 1
        blocks = [jnp.where(odd, blocks[j ^ bit], blocks[j]) for j in range(len(blocks))]
    return blocks


def exchange(blocks):
    near = reorder(blocks)
    return reorder(near[:1] + [swap_far(near[j], j) for j in range(1, len(near))])


def team_rows(rows):
    across = swap_chip(rows)
    return jnp.concatenate([rows, swap_core(rows), across, swap_core(across)], axis=0)


def team_sum(terms):
    count = terms.shape[0] // TEAM
    sent = jnp.concatenate([terms[count : 2 * count], terms[3 * count :]], axis=0)
    came = swap_core(sent).astype(f32)
    own = terms[:count].astype(f32) + came[:count]
    other = terms[2 * count : 3 * count].astype(f32) + came[count:]
    return own + swap_chip(other.astype(bf16)).astype(f32)


def take(blocks, index):
    return lax.dynamic_index_in_dim(blocks, index, axis=0, keepdims=False)


def scatter_first(part):
    groups, slots = part.shape[:2]
    if groups == 2:
        row = lax.axis_index("y")
        came = swap_row(take(part, 1 - row))
        summed = (take(part, row).astype(f32) + came.astype(f32)).astype(bf16)
        return lax.psum_scatter(summed, "s", scatter_dimension=0, tiled=False)
    flat = part.reshape((groups * slots,) + part.shape[2:]).astype(f32)
    return lax.psum_scatter(flat, ("g", "y", "s"), scatter_dimension=0, tiled=False)


def scatter_rest(part):
    if lax.axis_size("g") > 1:
        return lax.psum_scatter(
            part.astype(f32), ("g", "s"), scatter_dimension=0, tiled=False
        )
    return lax.psum_scatter(part, "s", scatter_dimension=0, tiled=False)


def feed_forward_kernel(
    normed_ref,
    grad_ref,
    gate_ref,
    up_ref,
    down_ref,
    hidden_ref,
    gate_grad_ref,
    up_grad_ref,
    out_ref,
    normed_grad_ref,
):
    gate_value = forward_dot(normed_ref[...], gate_ref[...])
    up_value = forward_dot(normed_ref[...], up_ref[...])
    sigmoid = jax.nn.sigmoid(gate_value)
    silu = gate_value * sigmoid
    hidden = (silu * up_value).astype(bf16)
    hidden_ref[...] = hidden
    hidden_grad = back_dot(grad_ref[...], down_ref[...])
    gate_grad = hidden_grad * up_value * (sigmoid * (1 + gate_value * (1 - sigmoid)))
    gate_grad = gate_grad.astype(bf16)
    up_grad = (hidden_grad * silu).astype(bf16)
    gate_grad_ref[...] = gate_grad
    up_grad_ref[...] = up_grad
    normed_grad = back_dot(gate_grad, gate_ref[...]) + back_dot(up_grad, up_ref[...])
    normed_grad_ref[...] = normed_grad.astype(bf16)
    out_ref[...] = forward_dot(hidden, down_ref[...]).astype(bf16)


def feed_forward(normed, grad, gate_full, up_full, down_full):
    rows, features = normed.shape
    width = gate_full.shape[1]
    tile = min(ROW_TILE, rows)

    def row_block(columns):
        return pl.BlockSpec((tile, columns), lambda i: (i, 0))

    def whole(shape):
        return pl.BlockSpec(shape, lambda i: (0, 0))

    wide = jax.ShapeDtypeStruct((rows, width), bf16)
    model = jax.ShapeDtypeStruct((rows, features), bf16)
    return pl.pallas_call(
        feed_forward_kernel,
        grid=(rows // tile,),
        in_specs=[
            row_block(features),
            row_block(features),
            whole(gate_full.shape),
            whole(up_full.shape),
            whole(down_full.shape),
        ],
        out_specs=[row_block(width)] * 3 + [row_block(features)] * 2,
        out_shape=[wide] * 3 + [model] * 2,
        compiler_params=pltpu.CompilerParams(vmem_limit_bytes=52 * 1024 * 1024),
        cost_estimate=pl.CostEstimate(
            flops=12 * rows * features * width,
            bytes_accessed=6 * features * width + 6 * rows * width + 8 * rows * features,
            transcendentals=rows * width,
        ),
    )(normed, grad, gate_full, up_full, down_full)


def crew_rows(rows):
    half = rows.shape[1] // 2
    left, right = rows[:, :half], rows[:, half:]
    left_x = swap_chip(left)
    right_y = swap_row(right)
    left_y = swap_row(jnp.concatenate([left, left_x], axis=0))
    right_x = swap_chip(jnp.concatenate([right, right_y], axis=0))
    count = rows.shape[0]
    core = jnp.concatenate(
        [
            rows,
            jnp.concatenate([left_x, right_x[:count]], axis=1),
            jnp.concatenate([left_y[:count], right_y], axis=1),
            jnp.concatenate([left_y[count:], right_x[count:]], axis=1),
        ],
        axis=0,
    )
    return jnp.concatenate([core, swap_core(core)], axis=0)


def crew_sum(terms):
    count = terms.shape[0] // CREW
    half = terms.shape[1] // 2
    came = swap_core(terms[4 * count :])
    both = terms[: 4 * count].astype(f32) + came.astype(f32)
    own, x_rows, y_rows, xy_rows = [both[k * count : (k + 1) * count] for k in range(4)]
    sent_y = jnp.concatenate([y_rows[:, :half], xy_rows[:, :half]], axis=0).astype(bf16)
    sent_x = jnp.concatenate([x_rows[:, half:], xy_rows[:, half:]], axis=0).astype(bf16)
    came_y = swap_row(sent_y).astype(f32)
    came_x = swap_chip(sent_x).astype(f32)
    last_x = swap_chip((x_rows[:, :half] + came_y[count:]).astype(bf16)).astype(f32)
    last_y = swap_row((y_rows[:, half:] + came_x[count:]).astype(bf16)).astype(f32)
    left = own[:, :half] + came_y[:count] + last_x
    right = own[:, half:] + came_x[:count] + last_y
    return jnp.concatenate([left, right], axis=1), sent_y


def weight_grad_kernel(steps, count, *refs):
    token_ref, operands, outs, sums = refs[0], refs[1:-6], refs[-6:-3], refs[-3:]
    del token_ref
    step = pl.program_id(0)

    @pl.when(step == 0)
    def _():
        for total in sums:
            total[...] = jnp.zeros_like(total)

    for m in range(count):
        normed, grad, hidden, gate_grad, up_grad = operands[5 * m : 5 * m + 5]

        @pl.when(step // steps == m)
        def _():
            sums[0][...] += rows_dot(normed[...], gate_grad[...])
            sums[1][...] += rows_dot(normed[...], up_grad[...])
            sums[2][...] += rows_dot(hidden[...], grad[...])

    @pl.when(step == count * steps - 1)
    def _():
        for out, total in zip(outs, sums):
            out[...] = total[...].astype(out.dtype)


def weight_grads(token, operands):
    count = len(operands)
    rows, features = operands[0][0].shape
    width = operands[0][2].shape[1]
    tile = min(ROW_TILE, rows)
    steps = rows // tile

    def row_block(m, columns):
        return pl.BlockSpec(
            (tile, columns), lambda i: (jnp.clip(i - m * steps, 0, steps - 1), 0)
        )

    def whole(shape):
        return pl.BlockSpec(shape, lambda i: (0, 0))

    shapes = [(features, width), (features, width), (width, features)]
    columns = (features, features, width, width, width)
    return pl.pallas_call(
        partial(weight_grad_kernel, steps, count),
        grid=(count * steps,),
        in_specs=[whole(token.shape)]
        + [row_block(m, size) for m in range(count) for size in columns],
        out_specs=[whole(shape) for shape in shapes],
        out_shape=[jax.ShapeDtypeStruct(shape, bf16) for shape in shapes],
        scratch_shapes=[pltpu.VMEM(shape, f32) for shape in shapes],
        compiler_params=pltpu.CompilerParams(vmem_limit_bytes=52 * 1024 * 1024),
        cost_estimate=pl.CostEstimate(
            flops=6 * count * rows * features * width,
            bytes_accessed=count * rows * (4 * features + 6 * width) + 6 * features * width,
            transcendentals=0,
        ),
    )(token, *[value for group in operands for value in group])


def shifted_down(rows, step):
    return jnp.concatenate(
        [jnp.zeros((step, rows.shape[1]), rows.dtype), rows[:-step]], axis=0
    )


def shifted_up(rows, step):
    return jnp.concatenate(
        [rows[step:], jnp.zeros((step, rows.shape[1]), rows.dtype)], axis=0
    )


def inverse_rms(values):
    return lax.rsqrt(jnp.mean(values * values, axis=-1, keepdims=True) + EPSILON)


def norm_back(values, scale, weighted):
    return scale * weighted - values * (
        scale * scale * scale * jnp.mean(weighted * values, axis=-1, keepdims=True)
    )


def per_device(
    tokens,
    positions,
    cotangent,
    norm_gain,
    in_weight,
    conv_weight,
    out_weight,
    ffn_gain,
    gate_weight,
    up_weight,
    down_weight,
):
    micro, micro_rows, features = tokens.shape
    share = in_weight.shape[0]
    hidden_share = down_weight.shape[0]
    hidden_width = gate_weight.shape[1]
    taps = conv_weight.shape[0]
    outer = lax.axis_size("g")
    groups = outer * lax.axis_size("y")
    slots = lax.axis_size("s")
    chan_run = slots * share
    hid_run = slots * hidden_share
    chan = groups * chan_run
    hid = outer * hid_run

    def by_place(weight, parts, team, run):
        count = weight.shape[1] // (parts * team * run)
        split = weight.reshape(share, parts, count, team, run)
        return jnp.transpose(split, (3, 0, 1, 2, 4)).reshape(team, share, parts * count * run)

    def side_by_side(block, width):
        return jnp.concatenate(
            [block[..., j * share : (j + 1) * share, :width] for j in range(features // width)],
            axis=-1,
        )

    def stacked(block, width):
        return jnp.concatenate(
            [block[..., j * width : (j + 1) * width] for j in range(features // width)], axis=-2
        )

    in_blocks = by_place(in_weight, 3, TEAM, chan_run)
    in_mine = jnp.concatenate(exchange([in_blocks[j] for j in range(TEAM)]), axis=0)
    gains = jnp.concatenate([norm_gain, ffn_gain]).reshape(1, 2 * share)
    near_gains = team_rows(gains)
    gains_row = jnp.concatenate(reorder([near_gains[j : j + 1] for j in range(TEAM)]), axis=1)
    pair_blocks = jnp.concatenate(
        [by_place(gate_weight, 1, CREW, hid_run), by_place(up_weight, 1, CREW, hid_run)], axis=2
    )
    pair_mine = jnp.concatenate(exchange([pair_blocks[j] for j in range(CREW)]), axis=0)

    def as_row(values):
        return jnp.pad(values, ((0, 0), (0, features - values.shape[1])))

    first_pack = jnp.concatenate(
        [
            jnp.concatenate([in_mine, stacked(out_weight, chan)], axis=1),
            as_row(conv_weight.reshape(1, taps * share)),
            as_row(gains_row),
            jnp.zeros((EXTRA_ROWS - 2, features), bf16),
        ],
        axis=0,
    )
    tall = TEAM * share

    def first_unpack(block):
        return [
            block[:tall, : 3 * chan].reshape(TEAM, share, 3 * chan),
            side_by_side(block[:tall, 3 * chan :], chan),
            block[tall, : taps * share].reshape(taps, share),
            block[tall + 1, : 2 * tall].reshape(TEAM, 2, share),
        ]

    first_all = lax.all_gather(first_pack, ("g", "y", "s"), axis=0, tiled=False)
    in_all, out_all, conv_all, gains_all = [
        part.reshape((groups, slots) + part.shape[1:]) for part in jax.vmap(first_unpack)(first_all)
    ]

    full = 2 * hid // features
    rest = 2 * hid - full * features
    rest_tall = CREW * share

    def rest_pack(pair, down):
        blocks = [pair[..., k * features : (k + 1) * features] for k in range(full)]
        if rest:
            blocks.append(side_by_side(pair[..., full * features :], rest))
        return jnp.concatenate(blocks + [down], axis=-2)

    def rest_unpack(packed):
        blocks = [packed[..., k * rest_tall : (k + 1) * rest_tall, :] for k in range(full)]
        base = full * rest_tall
        if rest:
            blocks.append(stacked(packed[..., base : base + share, :], rest))
            base += share
        return jnp.concatenate(blocks, axis=-1), packed[..., base:, :]

    rest_all = lax.all_gather(
        rest_pack(pair_mine, down_weight), ("g", "s"), axis=0, tiled=False
    )
    pair_all, down_all = rest_unpack(rest_all)

    def natural(gathered):
        width = gathered.shape[-1]
        split = gathered.reshape(outer, slots, CREW, share, width)
        return jnp.transpose(split, (0, 2, 1, 3, 4)).reshape(features, width)

    in_full = jnp.transpose(in_all, (0, 2, 1, 3, 4)).reshape(features, 3 * chan)
    out_full = out_all.reshape(chan, features)
    conv_full = jnp.transpose(conv_all, (2, 0, 1, 3)).reshape(taps, chan).astype(f32)
    gains_full = jnp.transpose(gains_all, (3, 0, 2, 1, 4)).reshape(2, features).astype(f32)
    norm_full, ffn_full = gains_full[0], gains_full[1]
    gate_full = natural(pair_all[..., :hid])
    up_full = natural(pair_all[..., hid:])
    down_full = down_all.reshape(hid, features)

    each = range(micro)
    team_tokens = [team_rows(tokens[m]) for m in each]
    team_places = [team_rows(positions[m][:, None]) for m in each]
    live = [(positions[m] >= 0).astype(f32)[:, None] for m in each]
    upstream = [cotangent[m].astype(f32) for m in each]
    ffn_grad = [crew_rows((live[m] * upstream[m]).astype(bf16)) for m in each]
    inputs = [tokens[m].astype(f32) for m in each]

    def mixer(m):
        values = team_tokens[m].astype(f32)
        first_normed = (values * inverse_rms(values) * norm_full).astype(bf16)
        projected = forward_dot(first_normed, in_full)
        b_part = projected[:, :chan]
        c_part = projected[:, chan : 2 * chan]
        x_part = projected[:, 2 * chan :]
        mixed = b_part * x_part
        mask_one = after((team_places[m] >= 1).astype(f32), ffn_grad[m][-1:])
        mask_two = (team_places[m] >= 2).astype(f32)
        mixed_one = mask_one * shifted_down(mixed, 1)
        mixed_two = mask_two * shifted_down(mixed, 2)
        convolved = conv_full[0] * mixed + conv_full[1] * mixed_one + conv_full[2] * mixed_two
        mixer_in = (c_part * convolved).astype(bf16)
        middle = inputs[m] + live[m] * team_sum(forward_dot(mixer_in, out_full).astype(bf16))
        second_scale = inverse_rms(middle)
        second_normed = crew_rows((middle * second_scale * ffn_full).astype(bf16))
        kept = (first_normed, b_part, c_part, x_part, mixed, mixed_one, mixed_two)
        return kept + (mask_one, mask_two, convolved, mixer_in), middle, second_scale, second_normed

    def feed(m, second_normed):
        return feed_forward(second_normed, ffn_grad[m], gate_full, up_full, down_full)

    def mixer_back(m, kept, middle, second_scale, normed_sum):
        first_normed, b_part, c_part, x_part, mixed, mixed_one, mixed_two = kept[:7]
        mask_one, mask_two, convolved, mixer_in = kept[7:]
        second_weighted = ffn_full * normed_sum
        middle_grad = upstream[m] + norm_back(middle, second_scale, second_weighted)
        mixer_grad = team_rows((live[m] * middle_grad).astype(bf16))
        mixer_in_grad = back_dot(mixer_grad, out_full)
        c_grad = mixer_in_grad * convolved
        conv_grad = mixer_in_grad * c_part
        mixed_grad = (
            conv_full[0] * conv_grad
            + conv_full[1] * shifted_up(mask_one * conv_grad, 1)
            + conv_full[2] * shifted_up(mask_two * conv_grad, 2)
        )
        projected_grad = jnp.concatenate(
            [mixed_grad * x_part, c_grad, mixed_grad * b_part], axis=1
        ).astype(bf16)
        grad_conv = jnp.stack(
            [
                jnp.sum(conv_grad * mixed, axis=0),
                jnp.sum(conv_grad * mixed_one, axis=0),
                jnp.sum(conv_grad * mixed_two, axis=0),
            ]
        )
        return middle_grad, mixer_grad, projected_grad, grad_conv

    def by_owner(grad, team):
        width = grad.shape[-1]
        count = features // (team * slots * share)
        split = grad.astype(bf16).reshape(count, team, slots, share, width)
        return jnp.transpose(split, (0, 2, 1, 3, 4)).reshape(count, slots, team * share, width)

    def total(terms):
        return reduce(jnp.add, terms)

    kept, middle, second_scale, second_normed = zip(*[mixer(m) for m in each])
    hidden, gate_grad, up_grad, out_part, normed_grad = zip(
        *[feed(m, second_normed[m]) for m in each]
    )
    normed_sum, sent = zip(*[crew_sum(normed_grad[m]) for m in each])

    gate_part, up_part, down_part = weight_grads(
        sum([sent[m][:16, :128] for m in each]),
        [
            (second_normed[m], ffn_grad[m], hidden[m], gate_grad[m], up_grad[m])
            for m in each
        ],
    )
    pair_part = jnp.concatenate([by_owner(gate_part, CREW), by_owner(up_part, CREW)], axis=3)
    owners = outer * slots
    rest_part = rest_pack(
        pair_part.reshape(owners, rest_tall, 2 * hid),
        down_part.reshape(owners, hidden_share, features),
    )
    middle_grad, mixer_grad, projected_grad, conv_parts = zip(
        *[mixer_back(m, kept[m], middle[m], second_scale[m], normed_sum[m]) for m in each]
    )
    pair_sum, down_sum = rest_unpack(scatter_rest(rest_part))

    in_part = by_owner(total([rows_dot(kept[m][0], projected_grad[m]) for m in each]), TEAM)
    out_grad_part = total([rows_dot(kept[m][10], mixer_grad[m]) for m in each]).astype(bf16)
    out_grad_part = stacked(out_grad_part.reshape(groups, slots, share, features), chan)
    conv_rows = jnp.transpose(
        total(conv_parts).reshape(taps, groups, slots, share), (1, 2, 0, 3)
    ).reshape(groups, slots, 1, taps * share)
    conv_rows = jnp.pad(
        conv_rows.astype(bf16),
        ((0, 0), (0, 0), (0, EXTRA_ROWS - 1), (0, features - taps * share)),
    )
    first_sum = scatter_first(
        jnp.concatenate(
            [jnp.concatenate([in_part, out_grad_part], axis=3), conv_rows], axis=2
        )
    )

    block_out = jnp.stack(
        [
            (
                middle[m] + live[m] * crew_sum(after(out_part[m], mixer_grad[-1][-1:]))[0]
            ).astype(bf16)
            for m in each
        ]
    )
    input_grads = []
    for m in each:
        weighted = norm_full * team_sum(back_dot(projected_grad[m], in_full).astype(bf16))
        scale = inverse_rms(inputs[m])
        input_grads.append(
            (middle_grad[m] + norm_back(inputs[m], scale, weighted)).astype(bf16)
        )

    def own_rows(summed, parts, team, run):
        blocks = [summed[j * share : (j + 1) * share].astype(bf16) for j in range(team)]
        came = [block.reshape(share, parts, -1, 1, run) for block in exchange(blocks)]
        joined = jnp.concatenate(came, axis=3)
        return joined.reshape(share, -1).astype(f32)

    pair_rows = own_rows(pair_sum, 2, CREW, hid_run)
    gate_rows = pair_rows[:, :hidden_width]
    up_rows = pair_rows[:, hidden_width:]
    in_rows = own_rows(first_sum[:tall, : 3 * chan], 3, TEAM, chan_run)
    grad_out = side_by_side(first_sum[:tall, 3 * chan :], chan).astype(f32)
    grad_conv = first_sum[tall, : taps * share].reshape(taps, share).astype(f32)
    grad_norm_gain = jnp.sum(in_weight.astype(f32) * in_rows, axis=1) / norm_gain.astype(f32)
    grad_ffn_gain = jnp.sum(
        gate_weight.astype(f32) * gate_rows + up_weight.astype(f32) * up_rows, axis=1
    ) / ffn_gain.astype(f32)
    return (
        block_out,
        jnp.stack(input_grads),
        grad_norm_gain,
        in_rows,
        grad_conv,
        grad_out,
        grad_ffn_gain,
        gate_rows,
        up_rows,
        down_sum.astype(f32),
    )


def solution(mesh):
    every = ("g", "y", "x", "c", "s")
    outer = mesh.shape["dp"] // CREW
    teams = Mesh(mesh.devices.reshape(outer, 2, 2, 2, mesh.shape["shard"]), every)
    return jax.shard_map(
        per_device,
        mesh=teams,
        in_specs=(
            P(None, every, None),
            P(None, every),
            P(None, every, None),
            P(every),
            P(every, None),
            P(None, every),
            P(every, None),
            P(every),
            P(every, None),
            P(every, None),
            P(every, None),
        ),
        out_specs=(
            P(None, every, None),
            P(None, every, None),
            P(every),
            P(every, None),
            P(None, every),
            P(every, None),
            P(every),
            P(every, None),
            P(every, None),
            P(every, None),
        ),
        check_vma=False,
    )
```

```python
from functools import partial

import jax
import jax.numpy as jnp
from jax import lax
from jax.experimental import pallas as pl
from jax.experimental.pallas import tpu as pltpu
from jax.sharding import Mesh, PartitionSpec as P

EPSILON = 1e-05
TEAM = 4
CREW = 8
EXTRA_ROWS = 16
ROW_TILE = 512
bf16 = jnp.bfloat16
f32 = jnp.float32


def forward_dot(left_side, right_side):
    return jnp.dot(left_side, right_side, preferred_element_type=f32)


def rows_dot(left_side, right_side):
    return lax.dot_general(
        left_side, right_side, (((0,), (0,)), ((), ())), preferred_element_type=f32
    )


def back_dot(left_side, right_side):
    return lax.dot_general(
        left_side, right_side, (((1,), (1,)), ((), ())), preferred_element_type=f32
    )


def swap_core(values):
    return lax.ppermute(values, "c", [(0, 1), (1, 0)])


def swap_chip(values):
    return lax.ppermute(values, "x", [(0, 1), (1, 0)])


def swap_row(values):
    return lax.ppermute(values, "y", [(0, 1), (1, 0)])


def swap_far(values, distance):
    axes = ("y", "x", "c")
    return lax.ppermute(values, axes, [(i, i ^ distance) for i in range(CREW)])


def after(values, token):
    return values + (token.ravel()[0] * 0).astype(values.dtype)


def reorder(blocks):
    blocks = list(blocks)
    for bit, axis in ((1, "c"), (2, "x"), (4, "y"))[: len(blocks).bit_length() - 1]:
        odd = lax.axis_index(axis) == 1
        blocks = [jnp.where(odd, blocks[j ^ bit], blocks[j]) for j in range(len(blocks))]
    return blocks


def exchange(blocks):
    near = reorder(blocks)
    return reorder(near[:1] + [swap_far(near[j], j) for j in range(1, len(near))])


def team_rows(rows):
    across = swap_chip(rows)
    return jnp.concatenate([rows, swap_core(rows), across, swap_core(across)], axis=0)


def team_sum(terms):
    count = terms.shape[0] // TEAM
    sent = jnp.concatenate([terms[count : 2 * count], terms[3 * count :]], axis=0)
    came = swap_core(sent).astype(f32)
    own = terms[:count].astype(f32) + came[:count]
    other = terms[2 * count : 3 * count].astype(f32) + came[count:]
    return own + swap_chip(other.astype(bf16)).astype(f32)


def take(blocks, index):
    return lax.dynamic_index_in_dim(blocks, index, axis=0, keepdims=False)


def scatter_first(part):
    groups, slots = part.shape[:2]
    if groups == 2:
        row = lax.axis_index("y")
        came = swap_row(take(part, 1 - row))
        summed = (take(part, row).astype(f32) + came.astype(f32)).astype(bf16)
        return lax.psum_scatter(summed, "s", scatter_dimension=0, tiled=False), summed[0, :1]
    flat = part.reshape((groups * slots,) + part.shape[2:]).astype(f32)
    total = lax.psum_scatter(flat, ("g", "y", "s"), scatter_dimension=0, tiled=False)
    return total, total[:1]


def scatter_rest(part):
    if lax.axis_size("g") > 1:
        return lax.psum_scatter(
            part.astype(f32), ("g", "s"), scatter_dimension=0, tiled=False
        )
    return lax.psum_scatter(part, "s", scatter_dimension=0, tiled=False)


def feed_forward_kernel(*refs):
    pieces, (gate_ref, up_ref, down_ref) = refs[:10], refs[10:13]
    hidden_ref, gate_grad_ref, up_grad_ref, out_ref, normed_grad_ref = refs[13:18]
    step = pl.program_id(0)
    half = gate_ref.shape[0] // 2
    for target, (own, left_x, right_y, left_y, right_x) in zip(
        refs[18:], (pieces[:5], pieces[5:])
    ):
        count = own.shape[0]

        @pl.when(step == 0)
        def _():
            target[...] = own[...]

        @pl.when(step == 1)
        def _():
            target[:, :half] = left_x[...]
            target[:, half:] = right_x[:count, :]

        @pl.when(step == 2)
        def _():
            target[:, :half] = left_y[:count, :]
            target[:, half:] = right_y[...]

        @pl.when(step == 3)
        def _():
            target[:, :half] = left_y[count:, :]
            target[:, half:] = right_x[count:, :]

    normed_ref, grad_ref = refs[18:]
    gate_value = forward_dot(normed_ref[...], gate_ref[...])
    up_value = forward_dot(normed_ref[...], up_ref[...])
    sigmoid = jax.nn.sigmoid(gate_value)
    silu = gate_value * sigmoid
    hidden = (silu * up_value).astype(bf16)
    hidden_ref[...] = hidden
    hidden_grad = back_dot(grad_ref[...], down_ref[...])
    gate_grad = hidden_grad * up_value * (sigmoid * (1 + gate_value * (1 - sigmoid)))
    gate_grad = gate_grad.astype(bf16)
    up_grad = (hidden_grad * silu).astype(bf16)
    gate_grad_ref[...] = gate_grad
    up_grad_ref[...] = up_grad
    normed_grad = back_dot(gate_grad, gate_ref[...]) + back_dot(up_grad, up_ref[...])
    normed_grad_ref[...] = normed_grad.astype(bf16)
    out_ref[...] = forward_dot(hidden, down_ref[...]).astype(bf16)


def feed_forward(normed, grad, gate_full, up_full, down_full):
    count, features = normed[0].shape
    width = gate_full.shape[1]

    def row_block(columns):
        return pl.BlockSpec((count, columns), lambda i: (i, 0))

    def whole(values):
        return pl.BlockSpec(values.shape, lambda i: (0, 0), pipeline_mode=pl.Buffered(1))

    wide = jax.ShapeDtypeStruct((4 * count, width), bf16)
    model = jax.ShapeDtypeStruct((4 * count, features), bf16)
    operands = [*normed, *grad, gate_full, up_full, down_full]
    return pl.pallas_call(
        feed_forward_kernel,
        grid=(4,),
        in_specs=[whole(values) for values in operands],
        out_specs=[row_block(width)] * 3 + [row_block(features)] * 4,
        out_shape=[wide] * 3 + [model] * 4,
        compiler_params=pltpu.CompilerParams(vmem_limit_bytes=56 * 1024 * 1024),
        cost_estimate=pl.CostEstimate(
            flops=48 * count * features * width,
            bytes_accessed=6 * features * width + 24 * count * width + 48 * count * features,
            transcendentals=4 * count * width,
        ),
    )(*operands)


def crew_pieces(rows):
    half = rows.shape[1] // 2
    left, right = rows[:, :half], rows[:, half:]
    left_x = swap_chip(left)
    right_y = swap_row(right)
    left_y = swap_row(jnp.concatenate([left, left_x], axis=0))
    right_x = swap_chip(jnp.concatenate([right, right_y], axis=0))
    return [rows, left_x, right_y, left_y, right_x]


def crew_sum(mine, theirs, beside):
    count = mine.shape[0] // 4
    half = mine.shape[1] // 2
    both = mine.astype(f32) + swap_core(theirs).astype(f32)
    own, x_rows, y_rows, xy_rows = [both[k * count : (k + 1) * count] for k in range(4)]
    sent_y = jnp.concatenate([y_rows[:, :half], xy_rows[:, :half]], axis=0).astype(bf16)
    sent_x = jnp.concatenate([x_rows[:, half:], xy_rows[:, half:]], axis=0).astype(bf16)
    came_y = swap_row(sent_y).astype(f32)
    came_x = swap_chip(sent_x).astype(f32)
    token, made = beside(sent_y[:16, :128])
    if token is not None:
        came_y, came_x = after(came_y, token), after(came_x, token)
    last_x = swap_chip((x_rows[:, :half] + came_y[count:]).astype(bf16)).astype(f32)
    last_y = swap_row((y_rows[:, half:] + came_x[count:]).astype(bf16)).astype(f32)
    left = own[:, :half] + came_y[:count] + last_x
    right = own[:, half:] + came_x[:count] + last_y
    return jnp.concatenate([left, right], axis=1), made


def weight_grad_kernel(steps, count, share, *refs):
    operands, outs, sums = refs[1 : 1 + 5 * count], refs[1 + 5 * count : -3], refs[-3:]
    step = pl.program_id(0)

    @pl.when(step == 0)
    def _():
        for total in sums:
            total[...] = jnp.zeros_like(total)

    for m in range(count):
        normed, grad, hidden, gate_grad, up_grad = operands[5 * m : 5 * m + 5]

        @pl.when(step // steps == m)
        def _():
            sums[0][...] += rows_dot(normed[...], gate_grad[...])
            sums[1][...] += rows_dot(normed[...], up_grad[...])
            sums[2][...] += rows_dot(hidden[...], grad[...])

    @pl.when(step == count * steps - 1)
    def _():
        if len(outs) == 3:
            for out, total in zip(outs, sums):
                out[...] = total[...].astype(bf16)
            return
        (out,) = outs
        gate, up, down = sums
        features, width = gate.shape
        slots = out.shape[0]
        hidden_share = width // slots
        tall = CREW * share
        rest = 2 * width - features
        for s in range(slots):
            for place in range(CREW):
                rows = pl.ds((place * slots + s) * share, share)
                at = pl.ds(place * share, share)
                out[s, at, :width] = gate[rows, :].astype(bf16)
                out[s, at, width:] = up[rows, : features - width].astype(bf16)
                out[s, pl.ds(tall, share), place * rest : (place + 1) * rest] = up[
                    rows, features - width :
                ].astype(bf16)
            out[s, tall + share :, :] = down[pl.ds(s * hidden_share, hidden_share), :].astype(bf16)


def weight_grads(token, operands, share, slots, packed):
    count = len(operands)
    rows, features = operands[0][0].shape
    width = operands[0][2].shape[1]
    tile = min(ROW_TILE, rows)
    steps = rows // tile

    def row_block(m, columns):
        return pl.BlockSpec(
            (tile, columns), lambda i: (jnp.clip(i - m * steps, 0, steps - 1), 0)
        )

    sums = [(features, width), (features, width), (width, features)]
    columns = (features, features, width, width, width)
    shapes = [(slots, CREW * share + share + width // slots, features)] if packed else sums
    return pl.pallas_call(
        partial(weight_grad_kernel, steps, count, share),
        grid=(count * steps,),
        in_specs=[pl.BlockSpec(token.shape, lambda i: (0, 0))]
        + [row_block(m, size) for m in range(count) for size in columns],
        out_specs=[pl.BlockSpec(shape, lambda i, r=len(shape): (0,) * r) for shape in shapes],
        out_shape=[jax.ShapeDtypeStruct(shape, bf16) for shape in shapes],
        scratch_shapes=[pltpu.VMEM(size, f32) for size in sums],
        compiler_params=pltpu.CompilerParams(vmem_limit_bytes=52 * 1024 * 1024),
        cost_estimate=pl.CostEstimate(
            flops=6 * count * rows * features * width,
            bytes_accessed=count * rows * (4 * features + 6 * width) + 6 * features * width,
            transcendentals=0,
        ),
    )(token, *[value for group in operands for value in group])


def shifted_down(rows, step):
    return jnp.concatenate(
        [jnp.zeros((step, rows.shape[1]), rows.dtype), rows[:-step]], axis=0
    )


def shifted_up(rows, step):
    return jnp.concatenate(
        [rows[step:], jnp.zeros((step, rows.shape[1]), rows.dtype)], axis=0
    )


def inverse_rms(values):
    return lax.rsqrt(jnp.mean(values * values, axis=-1, keepdims=True) + EPSILON)


def norm_back(values, scale, weighted):
    return scale * weighted - values * (
        scale * scale * scale * jnp.mean(weighted * values, axis=-1, keepdims=True)
    )


def per_device(
    tokens,
    positions,
    cotangent,
    norm_gain,
    in_weight,
    conv_weight,
    out_weight,
    ffn_gain,
    gate_weight,
    up_weight,
    down_weight,
):
    shape = tokens.shape
    features = shape[2]
    rows = shape[0] * shape[1]
    share = in_weight.shape[0]
    hidden_share = down_weight.shape[0]
    hidden_width = gate_weight.shape[1]
    taps = conv_weight.shape[0]
    outer = lax.axis_size("g")
    groups = outer * lax.axis_size("y")
    slots = lax.axis_size("s")
    chan_run = slots * share
    hid_run = slots * hidden_share
    chan = groups * chan_run
    hid = outer * hid_run

    def by_place(weight, parts, team, run):
        count = weight.shape[1] // (parts * team * run)
        split = weight.reshape(share, parts, count, team, run)
        return jnp.transpose(split, (3, 0, 1, 2, 4)).reshape(team, share, parts * count * run)

    def side_by_side(block, width):
        return jnp.concatenate(
            [block[..., j * share : (j + 1) * share, :width] for j in range(features // width)],
            axis=-1,
        )

    def stacked(block, width):
        return jnp.concatenate(
            [block[..., j * width : (j + 1) * width] for j in range(features // width)], axis=-2
        )

    in_blocks = by_place(in_weight, 3, TEAM, chan_run)
    in_mine = jnp.concatenate(exchange([in_blocks[j] for j in range(TEAM)]), axis=0)
    gains = jnp.concatenate([norm_gain, ffn_gain]).reshape(1, 2 * share)
    near_gains = team_rows(gains)
    gains_row = jnp.concatenate(reorder([near_gains[j : j + 1] for j in range(TEAM)]), axis=1)
    def as_row(values):
        return jnp.pad(values, ((0, 0), (0, features - values.shape[1])))

    first_pack = jnp.concatenate(
        [
            jnp.concatenate([in_mine, stacked(out_weight, chan)], axis=1),
            as_row(conv_weight.reshape(1, taps * share)),
            as_row(gains_row),
            jnp.zeros((EXTRA_ROWS - 2, features), bf16),
        ],
        axis=0,
    )
    tall = TEAM * share

    def first_unpack(block):
        return [
            block[:tall, : 3 * chan].reshape(TEAM, share, 3 * chan),
            side_by_side(block[:tall, 3 * chan :], chan),
            block[tall, : taps * share].reshape(taps, share),
            block[tall + 1, : 2 * tall].reshape(TEAM, 2, share),
        ]

    pair_blocks = jnp.concatenate(
        [by_place(gate_weight, 1, CREW, hid_run), by_place(up_weight, 1, CREW, hid_run)], axis=2
    )
    pair_blocks = after(pair_blocks, first_pack[:1])
    pair_mine = jnp.concatenate(exchange([pair_blocks[j] for j in range(CREW)]), axis=0)

    first_all = lax.all_gather(first_pack, ("g", "y", "s"), axis=0, tiled=False)
    in_all, out_all, conv_all, gains_all = [
        part.reshape((groups, slots) + part.shape[1:]) for part in jax.vmap(first_unpack)(first_all)
    ]

    full = 2 * hid // features
    rest = 2 * hid - full * features
    rest_tall = CREW * share

    def rest_pack(pair, down):
        blocks = [pair[..., k * features : (k + 1) * features] for k in range(full)]
        if rest:
            blocks.append(side_by_side(pair[..., full * features :], rest))
        return jnp.concatenate(blocks + [down], axis=-2)

    def rest_unpack(packed):
        blocks = [packed[..., k * rest_tall : (k + 1) * rest_tall, :] for k in range(full)]
        base = full * rest_tall
        if rest:
            blocks.append(stacked(packed[..., base : base + share, :], rest))
            base += share
        return jnp.concatenate(blocks, axis=-1), packed[..., base:, :]

    rest_all = lax.all_gather(
        rest_pack(pair_mine, down_weight), ("g", "s"), axis=0, tiled=False
    )
    pair_all, down_all = rest_unpack(rest_all)

    def natural(gathered):
        width = gathered.shape[-1]
        split = gathered.reshape(outer, slots, CREW, share, width)
        return jnp.transpose(split, (0, 2, 1, 3, 4)).reshape(features, width)

    in_full = jnp.transpose(in_all, (0, 2, 1, 3, 4)).reshape(features, 3 * chan)
    out_full = out_all.reshape(chan, features)
    conv_full = jnp.transpose(conv_all, (2, 0, 1, 3)).reshape(taps, chan).astype(f32)
    gains_full = jnp.transpose(gains_all, (3, 0, 2, 1, 4)).reshape(2, features).astype(f32)
    norm_full, ffn_full = gains_full[0], gains_full[1]
    gate_full = natural(pair_all[..., :hid])
    up_full = natural(pair_all[..., hid:])
    down_full = down_all.reshape(hid, features)

    own_tokens = after(tokens.reshape(rows, features), first_pack[:1])
    places = positions.reshape(rows, 1)
    team_tokens = team_rows(own_tokens)
    team_places = team_rows(places)
    live = (places >= 0).astype(f32)
    upstream = cotangent.reshape(rows, features).astype(f32)
    ffn_pieces = crew_pieces((after(live, own_tokens[:1]) * upstream).astype(bf16))
    inputs = tokens.reshape(rows, features).astype(f32)

    values = team_tokens.astype(f32)
    first_normed = (values * inverse_rms(values) * norm_full).astype(bf16)
    projected = forward_dot(first_normed, in_full)
    b_part = projected[:, :chan]
    c_part = projected[:, chan : 2 * chan]
    x_part = projected[:, 2 * chan :]
    mixed = b_part * x_part
    mask_one = (team_places >= 1).astype(f32)
    mask_two = (team_places >= 2).astype(f32)
    mixed_one = mask_one * shifted_down(mixed, 1)
    mixed_two = mask_two * shifted_down(mixed, 2)
    convolved = conv_full[0] * mixed + conv_full[1] * mixed_one + conv_full[2] * mixed_two
    mixer_in = (c_part * convolved).astype(bf16)
    mixer_out = team_sum(forward_dot(mixer_in, out_full).astype(bf16))
    middle = inputs + after(live, ffn_pieces[3][-1:]) * mixer_out
    second_scale = inverse_rms(middle)
    second_pieces = crew_pieces((middle * second_scale * ffn_full).astype(bf16))

    runs = []
    for normed, grad in (
        (second_pieces, ffn_pieces),
        ([swap_core(v) for v in second_pieces], [swap_core(v) for v in ffn_pieces]),
    ):
        runs.append(feed_forward(normed, grad, gate_full, up_full, down_full))
    (_, _, _, out_mine, normed_mine, _, _), (_, _, _, out_theirs, normed_theirs, _, _) = runs
    owners = outer * slots

    def by_owner(grad, team):
        width = grad.shape[-1]
        count = features // (team * slots * share)
        split = grad.astype(bf16).reshape(count, team, slots, share, width)
        return jnp.transpose(split, (0, 2, 1, 3, 4)).reshape(count, slots, team * share, width)

    def rest_grads(token):
        groups_of = [(run[5], run[6], run[0], run[1], run[2]) for run in runs]
        if outer == 1 and share % 16 == 0 and hidden_share % 16 == 0:
            (packed,) = weight_grads(token, groups_of, share, owners, True)
            return packed[0, :1, :128], packed
        gate_part, up_part, down_part = weight_grads(token, groups_of, share, owners, False)
        pair_part = jnp.concatenate([by_owner(gate_part, CREW), by_owner(up_part, CREW)], axis=3)
        packed = rest_pack(
            pair_part.reshape(owners, rest_tall, 2 * hid),
            down_part.reshape(owners, hidden_share, features),
        )
        return packed[0, :1], packed

    normed_sum, rest_part = crew_sum(normed_mine, normed_theirs, rest_grads)
    second_weighted = ffn_full * normed_sum
    middle_grad = upstream + norm_back(middle, second_scale, second_weighted)

    mixer_grad = team_rows((live * middle_grad).astype(bf16))
    mixer_in_grad = back_dot(mixer_grad, out_full)
    c_grad = mixer_in_grad * convolved
    conv_grad = mixer_in_grad * c_part
    mixed_grad = (
        conv_full[0] * conv_grad
        + conv_full[1] * shifted_up(mask_one * conv_grad, 1)
        + conv_full[2] * shifted_up(mask_two * conv_grad, 2)
    )
    projected_grad = jnp.concatenate(
        [mixed_grad * x_part, c_grad, mixed_grad * b_part], axis=1
    ).astype(bf16)
    grad_conv_part = jnp.stack(
        [
            jnp.sum(conv_grad * mixed, axis=0),
            jnp.sum(conv_grad * mixed_one, axis=0),
            jnp.sum(conv_grad * mixed_two, axis=0),
        ]
    )
    pair_sum, down_sum = rest_unpack(scatter_rest(rest_part))

    in_part = by_owner(rows_dot(first_normed, projected_grad), TEAM)
    out_grad_part = rows_dot(mixer_in, mixer_grad).astype(bf16)
    out_grad_part = stacked(out_grad_part.reshape(groups, slots, share, features), chan)
    conv_rows = jnp.transpose(
        grad_conv_part.reshape(taps, groups, slots, share), (1, 2, 0, 3)
    ).reshape(groups, slots, 1, taps * share)
    conv_rows = jnp.pad(
        conv_rows.astype(bf16),
        ((0, 0), (0, 0), (0, EXTRA_ROWS - 1), (0, features - taps * share)),
    )
    first_sum, token = scatter_first(
        jnp.concatenate(
            [jnp.concatenate([in_part, out_grad_part], axis=3), conv_rows], axis=2
        )
    )

    first_weighted = norm_full * team_sum(back_dot(projected_grad, in_full).astype(bf16))
    input_grad = middle_grad + norm_back(inputs, inverse_rms(inputs), first_weighted)
    input_grad = input_grad.astype(bf16)
    out_sum, _ = crew_sum(after(out_mine, token), out_theirs, lambda sent: (None, None))
    block_out = (middle + live * out_sum).astype(bf16)

    def own_rows(summed, parts, team, run):
        blocks = [summed[j * share : (j + 1) * share].astype(bf16) for j in range(team)]
        came = [block.reshape(share, parts, -1, 1, run) for block in exchange(blocks)]
        joined = jnp.concatenate(came, axis=3)
        return joined.reshape(share, -1).astype(f32)

    pair_rows = own_rows(pair_sum, 2, CREW, hid_run)
    gate_rows = pair_rows[:, :hidden_width]
    up_rows = pair_rows[:, hidden_width:]
    in_rows = own_rows(first_sum[:tall, : 3 * chan], 3, TEAM, chan_run)
    grad_out = side_by_side(first_sum[:tall, 3 * chan :], chan).astype(f32)
    grad_conv = first_sum[tall, : taps * share].reshape(taps, share).astype(f32)
    grad_norm_gain = jnp.sum(in_weight.astype(f32) * in_rows, axis=1) / norm_gain.astype(f32)
    grad_ffn_gain = jnp.sum(
        gate_weight.astype(f32) * gate_rows + up_weight.astype(f32) * up_rows, axis=1
    ) / ffn_gain.astype(f32)
    return (
        block_out.reshape(shape),
        input_grad.reshape(shape),
        grad_norm_gain,
        in_rows,
        grad_conv,
        grad_out,
        grad_ffn_gain,
        gate_rows,
        up_rows,
        down_sum.astype(f32),
    )


def solution(mesh):
    every = ("g", "y", "x", "c", "s")
    outer = mesh.shape["dp"] // CREW
    teams = Mesh(mesh.devices.reshape(outer, 2, 2, 2, mesh.shape["shard"]), every)
    return jax.shard_map(
        per_device,
        mesh=teams,
        in_specs=(
            P(None, every, None),
            P(None, every),
            P(None, every, None),
            P(every),
            P(every, None),
            P(None, every),
            P(every, None),
            P(every),
            P(every, None),
            P(every, None),
            P(every, None),
        ),
        out_specs=(
            P(None, every, None),
            P(None, every, None),
            P(every),
            P(every, None),
            P(None, every),
            P(every, None),
            P(every),
            P(every, None),
            P(every, None),
            P(every, None),
        ),
        check_vma=False,
    )
```

```python
import jax
import jax.numpy as jnp
from jax import lax
from jax.experimental import pallas as pl
from jax.experimental.pallas import tpu as pltpu
from jax.sharding import Mesh, PartitionSpec as P

EPSILON = 1e-05
TEAM = 4
EXTRA_ROWS = 16
ROW_TILE = 512
bf16 = jnp.bfloat16
f32 = jnp.float32


def forward_dot(left_side, right_side):
    return jnp.dot(left_side, right_side, preferred_element_type=f32)


def rows_dot(left_side, right_side):
    return lax.dot_general(
        left_side, right_side, (((0,), (0,)), ((), ())), preferred_element_type=f32
    )


def back_dot(left_side, right_side):
    return lax.dot_general(
        left_side, right_side, (((1,), (1,)), ((), ())), preferred_element_type=f32
    )


def swap_core(values):
    return lax.ppermute(values, "c", [(0, 1), (1, 0)])


def swap_chip(values):
    return lax.ppermute(values, "x", [(0, 1), (1, 0)])


def swap_row(values):
    return lax.ppermute(values, "y", [(0, 1), (1, 0)])


def swap_far(values, distance):
    return lax.ppermute(values, ("x", "c"), [(i, i ^ distance) for i in range(TEAM)])


def after(values, token):
    return values + (token.ravel()[0] * 0).astype(values.dtype)


def reorder(blocks):
    blocks = list(blocks)
    for bit, axis in ((1, "c"), (2, "x")):
        odd = lax.axis_index(axis) == 1
        blocks = [jnp.where(odd, blocks[j ^ bit], blocks[j]) for j in range(len(blocks))]
    return blocks


def exchange(blocks):
    near = reorder(blocks)
    return reorder(near[:1] + [swap_far(near[j], j) for j in range(1, len(near))])


def team_rows(rows):
    across = swap_chip(rows)
    return jnp.concatenate([rows, swap_core(rows), across, swap_core(across)], axis=0)


def team_sum(terms):
    count = terms.shape[0] // TEAM
    sent = jnp.concatenate([terms[count : 2 * count], terms[3 * count :]], axis=0)
    came = swap_core(sent).astype(f32)
    own = terms[:count].astype(f32) + came[:count]
    other = terms[2 * count : 3 * count].astype(f32) + came[count:]
    return own + swap_chip(other.astype(bf16)).astype(f32)


def take(blocks, index):
    return lax.dynamic_index_in_dim(blocks, index, axis=0, keepdims=False)


def scatter_first(part):
    groups, slots = part.shape[:2]
    if groups == 2:
        row = lax.axis_index("y")
        came = swap_row(take(part, 1 - row))
        summed = (take(part, row).astype(f32) + came.astype(f32)).astype(bf16)
        return lax.psum_scatter(summed, "s", scatter_dimension=0, tiled=False), summed[0, :1]
    flat = part.reshape((groups * slots,) + part.shape[2:]).astype(f32)
    total = lax.psum_scatter(flat, ("g", "y", "s"), scatter_dimension=0, tiled=False)
    return total, total[:1]


def scatter_rest(part):
    wide = part if part.shape[0] <= 8 else part.astype(f32)
    return lax.psum_scatter(wide, ("g", "y", "s"), scatter_dimension=0, tiled=False)


def forward_kernel(normed_ref, pair_ref, hidden_ref, silu_ref, slope_ref):
    width = hidden_ref.shape[1]
    values = forward_dot(normed_ref[...], pair_ref[...])
    gate_value, up_value = values[:, :width], values[:, width:]
    sigmoid = jax.nn.sigmoid(gate_value)
    silu = gate_value * sigmoid
    hidden_ref[...] = (silu * up_value).astype(bf16)
    silu_ref[...] = silu.astype(bf16)
    slope_ref[...] = (up_value * (sigmoid * (1 + gate_value * (1 - sigmoid)))).astype(bf16)


def backward_kernel(
    grad_ref, hidden_ref, silu_ref, slope_ref, pair_ref, down_ref, pair_grad_ref, normed_ref, out_ref
):
    width = hidden_ref.shape[1]
    hidden_grad = back_dot(grad_ref[...], down_ref[...])
    pair_grad_ref[:, :width] = (hidden_grad * slope_ref[...].astype(f32)).astype(bf16)
    pair_grad_ref[:, width:] = (hidden_grad * silu_ref[...].astype(f32)).astype(bf16)
    normed_ref[...] = back_dot(pair_grad_ref[...], pair_ref[...]).astype(bf16)
    out_ref[...] = forward_dot(hidden_ref[...], down_ref[...]).astype(bf16)


def by_rows(kernel, rowed, whole, columns, flops, transcendentals):
    rows = rowed[0].shape[0]
    tile = min(ROW_TILE, rows)

    def row_block(count):
        return pl.BlockSpec((tile, count), lambda i: (i, 0))

    moved = sum(2 * value.size for value in rowed + whole) + 2 * rows * sum(columns)
    return pl.pallas_call(
        kernel,
        grid=(rows // tile,),
        in_specs=[row_block(value.shape[1]) for value in rowed]
        + [
            pl.BlockSpec(value.shape, lambda i: (0, 0), pipeline_mode=pl.Buffered(1))
            for value in whole
        ],
        out_specs=[row_block(count) for count in columns],
        out_shape=[jax.ShapeDtypeStruct((rows, count), bf16) for count in columns],
        compiler_params=pltpu.CompilerParams(vmem_limit_bytes=52 * 1024 * 1024),
        cost_estimate=pl.CostEstimate(
            flops=flops, bytes_accessed=moved, transcendentals=transcendentals
        ),
    )(*rowed, *whole)


def shifted_down(rows, step):
    return jnp.concatenate(
        [jnp.zeros((step, rows.shape[1]), rows.dtype), rows[:-step]], axis=0
    )


def shifted_up(rows, step):
    return jnp.concatenate(
        [rows[step:], jnp.zeros((step, rows.shape[1]), rows.dtype)], axis=0
    )


def inverse_rms(values):
    return lax.rsqrt(jnp.mean(values * values, axis=-1, keepdims=True) + EPSILON)


def norm_back(values, scale, weighted):
    return scale * weighted - values * (
        scale * scale * scale * jnp.mean(weighted * values, axis=-1, keepdims=True)
    )


def per_device(
    tokens,
    positions,
    cotangent,
    norm_gain,
    in_weight,
    conv_weight,
    out_weight,
    ffn_gain,
    gate_weight,
    up_weight,
    down_weight,
):
    shape = tokens.shape
    features = shape[2]
    rows = shape[0] * shape[1]
    share = in_weight.shape[0]
    hidden_share = down_weight.shape[0]
    hidden_width = gate_weight.shape[1]
    taps = conv_weight.shape[0]
    groups = lax.axis_size("g") * lax.axis_size("y")
    slots = lax.axis_size("s")
    chan_run = slots * share
    hid_run = slots * hidden_share
    chan = groups * chan_run
    hid = groups * hid_run

    def by_place(weight, parts, team, run):
        count = weight.shape[1] // (parts * team * run)
        split = weight.reshape(share, parts, count, team, run)
        return jnp.transpose(split, (3, 0, 1, 2, 4)).reshape(team, share, parts * count * run)

    def side_by_side(block, width):
        return jnp.concatenate(
            [block[..., j * share : (j + 1) * share, :width] for j in range(features // width)],
            axis=-1,
        )

    def stacked(block, width):
        return jnp.concatenate(
            [block[..., j * width : (j + 1) * width] for j in range(features // width)], axis=-2
        )

    in_blocks = by_place(in_weight, 3, TEAM, chan_run)
    in_mine = jnp.concatenate(exchange([in_blocks[j] for j in range(TEAM)]), axis=0)
    gains = jnp.concatenate([norm_gain, ffn_gain]).reshape(1, 2 * share)
    near_gains = team_rows(gains)
    gains_row = jnp.concatenate(reorder([near_gains[j : j + 1] for j in range(TEAM)]), axis=1)
    def as_row(values):
        return jnp.pad(values, ((0, 0), (0, features - values.shape[1])))

    first_pack = jnp.concatenate(
        [
            jnp.concatenate([in_mine, stacked(out_weight, chan)], axis=1),
            as_row(conv_weight.reshape(1, taps * share)),
            as_row(gains_row),
            jnp.zeros((EXTRA_ROWS - 2, features), bf16),
        ],
        axis=0,
    )
    tall = TEAM * share

    def first_unpack(block):
        return [
            block[:tall, : 3 * chan].reshape(TEAM, share, 3 * chan),
            side_by_side(block[:tall, 3 * chan :], chan),
            block[tall, : taps * share].reshape(taps, share),
            block[tall + 1, : 2 * tall].reshape(TEAM, 2, share),
        ]

    pair_blocks = jnp.concatenate(
        [by_place(gate_weight, 1, TEAM, hid_run), by_place(up_weight, 1, TEAM, hid_run)], axis=2
    )
    pair_mine = jnp.concatenate(exchange([pair_blocks[j] for j in range(TEAM)]), axis=0)

    first_all = lax.all_gather(first_pack, ("g", "y", "s"), axis=0, tiled=False)
    in_all, out_all, conv_all, gains_all = [
        part.reshape((groups, slots) + part.shape[1:]) for part in jax.vmap(first_unpack)(first_all)
    ]

    pair_all = lax.all_gather(pair_mine, ("g", "y", "s"), axis=0, tiled=False)
    down_full = lax.all_gather(down_weight, ("g", "y", "s"), axis=0, tiled=True)

    in_full = jnp.transpose(in_all, (0, 2, 1, 3, 4)).reshape(features, 3 * chan)
    out_full = out_all.reshape(chan, features)
    conv_full = jnp.transpose(conv_all, (2, 0, 1, 3)).reshape(taps, chan).astype(f32)
    gains_full = jnp.transpose(gains_all, (3, 0, 2, 1, 4)).reshape(2, features).astype(f32)
    norm_full, ffn_full = gains_full[0], gains_full[1]
    pair_full = jnp.transpose(
        pair_all.reshape(groups, slots, TEAM, share, 2 * hid), (0, 2, 1, 3, 4)
    ).reshape(features, 2 * hid)

    own_tokens = tokens.reshape(rows, features)
    places = positions.reshape(rows, 1)
    team_tokens = team_rows(own_tokens)
    team_places = team_rows(places)
    live = (places >= 0).astype(f32)
    upstream = cotangent.reshape(rows, features).astype(f32)
    ffn_grad = team_rows((live * upstream).astype(bf16))
    inputs = tokens.reshape(rows, features).astype(f32)

    values = team_tokens.astype(f32)
    early_full = after(norm_full, ffn_grad[-1:])
    first_normed = (values * inverse_rms(values) * early_full).astype(bf16)
    projected = forward_dot(first_normed, in_full)
    b_part = projected[:, :chan]
    c_part = projected[:, chan : 2 * chan]
    x_part = projected[:, 2 * chan :]
    mixed = b_part * x_part
    mask_one = (team_places >= 1).astype(f32)
    mask_two = (team_places >= 2).astype(f32)
    mixed_one = mask_one * shifted_down(mixed, 1)
    mixed_two = mask_two * shifted_down(mixed, 2)
    convolved = conv_full[0] * mixed + conv_full[1] * mixed_one + conv_full[2] * mixed_two
    mixer_in = (c_part * convolved).astype(bf16)
    mixer_out = team_sum(forward_dot(mixer_in, out_full).astype(bf16))
    middle = inputs + live * mixer_out
    second_scale = inverse_rms(middle)
    second_normed = team_rows((middle * second_scale * ffn_full).astype(bf16))

    team_count = TEAM * rows
    unit = 2 * team_count * features * hid
    hidden, silu, slope = by_rows(
        forward_kernel, [second_normed], [pair_full], [hid] * 3, 2 * unit, team_count * hid
    )
    owners = groups * slots
    down_part = rows_dot(hidden, ffn_grad).astype(bf16)
    grad_down = scatter_rest(down_part.reshape(owners, hidden_share, features))
    pair_grad, normed_part, out_part = by_rows(
        backward_kernel,
        [ffn_grad, hidden, silu, slope],
        [pair_full, down_full],
        [2 * hid, features, features],
        4 * unit,
        0,
    )

    def by_owner(grad, team):
        width = grad.shape[-1]
        count = features // (team * slots * share)
        split = grad.astype(bf16).reshape(count, team, slots, share, width)
        return jnp.transpose(split, (0, 2, 1, 3, 4)).reshape(count, slots, team * share, width)

    pair_part = by_owner(rows_dot(second_normed, pair_grad), TEAM)
    pair_sum = scatter_rest(pair_part.reshape(owners, tall, 2 * hid))
    normed_sum = team_sum(normed_part)
    second_weighted = ffn_full * normed_sum
    middle_grad = upstream + norm_back(middle, second_scale, second_weighted)

    mixer_grad = team_rows((live * middle_grad).astype(bf16))
    mixer_in_grad = back_dot(mixer_grad, out_full)
    c_grad = mixer_in_grad * convolved
    conv_grad = mixer_in_grad * c_part
    mixed_grad = (
        conv_full[0] * conv_grad
        + conv_full[1] * shifted_up(mask_one * conv_grad, 1)
        + conv_full[2] * shifted_up(mask_two * conv_grad, 2)
    )
    projected_grad = jnp.concatenate(
        [mixed_grad * x_part, c_grad, mixed_grad * b_part], axis=1
    ).astype(bf16)
    grad_conv_part = jnp.stack(
        [
            jnp.sum(conv_grad * mixed, axis=0),
            jnp.sum(conv_grad * mixed_one, axis=0),
            jnp.sum(conv_grad * mixed_two, axis=0),
        ]
    )
    in_part = by_owner(rows_dot(first_normed, projected_grad), TEAM)
    out_grad_part = rows_dot(mixer_in, mixer_grad).astype(bf16)
    out_grad_part = stacked(out_grad_part.reshape(groups, slots, share, features), chan)
    conv_rows = jnp.transpose(
        grad_conv_part.reshape(taps, groups, slots, share), (1, 2, 0, 3)
    ).reshape(groups, slots, 1, taps * share)
    conv_rows = jnp.pad(
        conv_rows.astype(bf16),
        ((0, 0), (0, 0), (0, EXTRA_ROWS - 1), (0, features - taps * share)),
    )
    first_sum, token = scatter_first(
        jnp.concatenate(
            [jnp.concatenate([in_part, out_grad_part], axis=3), conv_rows], axis=2
        )
    )

    first_weighted = norm_full * team_sum(back_dot(projected_grad, in_full).astype(bf16))
    input_grad = middle_grad + norm_back(inputs, inverse_rms(inputs), first_weighted)
    input_grad = input_grad.astype(bf16)
    out_sum = team_sum(after(out_part, token))
    block_out = (middle + live * out_sum).astype(bf16)

    def own_rows(summed, parts, team, run):
        blocks = [summed[j * share : (j + 1) * share].astype(bf16) for j in range(team)]
        came = [block.reshape(share, parts, -1, 1, run) for block in exchange(blocks)]
        joined = jnp.concatenate(came, axis=3)
        return joined.reshape(share, -1).astype(f32)

    pair_rows = own_rows(pair_sum, 2, TEAM, hid_run)
    gate_rows = pair_rows[:, :hidden_width]
    up_rows = pair_rows[:, hidden_width:]
    in_rows = own_rows(first_sum[:tall, : 3 * chan], 3, TEAM, chan_run)
    grad_out = side_by_side(first_sum[:tall, 3 * chan :], chan).astype(f32)
    grad_conv = first_sum[tall, : taps * share].reshape(taps, share).astype(f32)
    grad_norm_gain = jnp.sum(in_weight.astype(f32) * in_rows, axis=1) / norm_gain.astype(f32)
    grad_ffn_gain = jnp.sum(
        gate_weight.astype(f32) * gate_rows + up_weight.astype(f32) * up_rows, axis=1
    ) / ffn_gain.astype(f32)
    return (
        block_out.reshape(shape),
        input_grad.reshape(shape),
        grad_norm_gain,
        in_rows,
        grad_conv,
        grad_out,
        grad_ffn_gain,
        gate_rows,
        up_rows,
        grad_down.astype(f32),
    )


def solution(mesh):
    every = ("g", "y", "x", "c", "s")
    outer = mesh.shape["dp"] // (2 * TEAM)
    teams = Mesh(mesh.devices.reshape(outer, 2, 2, 2, mesh.shape["shard"]), every)
    return jax.shard_map(
        per_device,
        mesh=teams,
        in_specs=(
            P(None, every, None),
            P(None, every),
            P(None, every, None),
            P(every),
            P(every, None),
            P(None, every),
            P(every, None),
            P(every),
            P(every, None),
            P(every, None),
            P(every, None),
        ),
        out_specs=(
            P(None, every, None),
            P(None, every, None),
            P(every),
            P(every, None),
            P(None, every),
            P(every, None),
            P(every),
            P(every, None),
            P(every, None),
            P(every, None),
        ),
        check_vma=False,
    )
```

```python
import jax
import jax.numpy as jnp
from jax import lax
from jax.experimental import pallas as pl
from jax.experimental.pallas import tpu as pltpu
from jax.sharding import Mesh, PartitionSpec as P

EPSILON = 1e-05
TEAM = 4
EXTRA_ROWS = 16
ROW_TILE = 512
bf16 = jnp.bfloat16
f32 = jnp.float32


def forward_dot(left_side, right_side):
    return jnp.dot(left_side, right_side, preferred_element_type=f32)


def rows_dot(left_side, right_side):
    return lax.dot_general(
        left_side, right_side, (((0,), (0,)), ((), ())), preferred_element_type=f32
    )


def back_dot(left_side, right_side):
    return lax.dot_general(
        left_side, right_side, (((1,), (1,)), ((), ())), preferred_element_type=f32
    )


def swap_core(values):
    return lax.ppermute(values, "c", [(0, 1), (1, 0)])


def swap_chip(values):
    return lax.ppermute(values, "x", [(0, 1), (1, 0)])


def swap_row(values):
    return lax.ppermute(values, "y", [(0, 1), (1, 0)])


def swap_far(values, distance):
    return lax.ppermute(values, ("x", "c"), [(i, i ^ distance) for i in range(TEAM)])


def after(values, token):
    return values + (token.ravel()[0] * 0).astype(values.dtype)


def reorder(blocks):
    blocks = list(blocks)
    for bit, axis in ((1, "c"), (2, "x")):
        odd = lax.axis_index(axis) == 1
        blocks = [jnp.where(odd, blocks[j ^ bit], blocks[j]) for j in range(len(blocks))]
    return blocks


def exchange(blocks):
    near = reorder(blocks)
    return reorder(near[:1] + [swap_far(near[j], j) for j in range(1, len(near))])


def team_pieces(rows):
    across = swap_chip(rows)
    return [rows, swap_core(rows), across, swap_core(across)]


def team_rows(rows):
    return jnp.concatenate(team_pieces(rows), axis=0)


def team_sum(terms, token=None):
    count = terms.shape[0] // TEAM
    sent = jnp.concatenate([terms[count : 2 * count], terms[3 * count :]], axis=0)
    came = swap_core(sent).astype(f32)
    own = terms[:count].astype(f32) + came[:count]
    other = terms[2 * count : 3 * count].astype(f32) + came[count:]
    came = swap_chip(other.astype(bf16)).astype(f32)
    return own + (came if token is None else after(came, token))


def take(blocks, index):
    return lax.dynamic_index_in_dim(blocks, index, axis=0, keepdims=False)


def scatter_first(part):
    groups, slots = part.shape[:2]
    if groups == 2:
        row = lax.axis_index("y")
        came = swap_row(take(part, 1 - row))
        summed = (take(part, row).astype(f32) + came.astype(f32)).astype(bf16)
        return lax.psum_scatter(summed, "s", scatter_dimension=0, tiled=False)
    flat = part.reshape((groups * slots,) + part.shape[2:]).astype(f32)
    return lax.psum_scatter(flat, ("g", "y", "s"), scatter_dimension=0, tiled=False)


def scatter_rest(part):
    wide = part if part.shape[0] <= 8 else part.astype(f32)
    return lax.psum_scatter(wide, ("g", "y", "s"), scatter_dimension=0, tiled=False)


def forward_kernel(*refs):
    pieces, pair_ref = refs[: 2 * TEAM], refs[2 * TEAM]
    hidden_ref, silu_ref, slope_ref, normed_ref, grad_ref = refs[2 * TEAM + 1 :]
    for k in range(TEAM):

        @pl.when(pl.program_id(0) == k)
        def _():
            normed_ref[...] = pieces[k][...]
            grad_ref[...] = pieces[TEAM + k][...]

    width = hidden_ref.shape[1]
    values = forward_dot(normed_ref[...], pair_ref[...])
    gate_value, up_value = values[:, :width], values[:, width:]
    sigmoid = jax.nn.sigmoid(gate_value)
    silu = gate_value * sigmoid
    hidden_ref[...] = (silu * up_value).astype(bf16)
    silu_ref[...] = silu.astype(bf16)
    slope_ref[...] = (up_value * (sigmoid * (1 + gate_value * (1 - sigmoid)))).astype(bf16)


def backward_kernel(
    grad_ref,
    hidden_ref,
    silu_ref,
    slope_ref,
    pair_ref,
    down_ref,
    token_ref,
    pair_grad_ref,
    normed_ref,
    out_ref,
):
    del token_ref
    width = hidden_ref.shape[1]
    hidden_grad = back_dot(grad_ref[...], down_ref[...])
    pair_grad_ref[:, :width] = (hidden_grad * slope_ref[...].astype(f32)).astype(bf16)
    pair_grad_ref[:, width:] = (hidden_grad * silu_ref[...].astype(f32)).astype(bf16)
    normed_ref[...] = back_dot(pair_grad_ref[...], pair_ref[...]).astype(bf16)
    out_ref[...] = forward_dot(hidden_ref[...], down_ref[...]).astype(bf16)


def by_rows(kernel, tile, steps, rowed, whole, tokens, columns, flops, transcendentals):
    rows = steps * tile

    def row_block(count):
        return pl.BlockSpec((tile, count), lambda i: (i, 0))

    moved = sum(2 * value.size for value in rowed + whole) + 2 * rows * sum(columns)
    return pl.pallas_call(
        kernel,
        grid=(steps,),
        in_specs=[row_block(value.shape[1]) for value in rowed]
        + [
            pl.BlockSpec(value.shape, lambda i: (0, 0), pipeline_mode=pl.Buffered(1))
            for value in whole
        ]
        + [pl.BlockSpec(memory_space=pl.ANY)] * len(tokens),
        out_specs=[row_block(count) for count in columns],
        out_shape=[jax.ShapeDtypeStruct((rows, count), bf16) for count in columns],
        compiler_params=pltpu.CompilerParams(vmem_limit_bytes=52 * 1024 * 1024),
        cost_estimate=pl.CostEstimate(
            flops=flops, bytes_accessed=moved, transcendentals=transcendentals
        ),
    )(*rowed, *whole, *tokens)


def shifted_down(rows, step):
    return jnp.concatenate(
        [jnp.zeros((step, rows.shape[1]), rows.dtype), rows[:-step]], axis=0
    )


def shifted_up(rows, step):
    return jnp.concatenate(
        [rows[step:], jnp.zeros((step, rows.shape[1]), rows.dtype)], axis=0
    )


def inverse_rms(values):
    return lax.rsqrt(jnp.mean(values * values, axis=-1, keepdims=True) + EPSILON)


def norm_back(values, scale, weighted):
    return scale * weighted - values * (
        scale * scale * scale * jnp.mean(weighted * values, axis=-1, keepdims=True)
    )


def per_device(
    tokens,
    positions,
    cotangent,
    norm_gain,
    in_weight,
    conv_weight,
    out_weight,
    ffn_gain,
    gate_weight,
    up_weight,
    down_weight,
):
    shape = tokens.shape
    features = shape[2]
    rows = shape[0] * shape[1]
    share = in_weight.shape[0]
    hidden_share = down_weight.shape[0]
    hidden_width = gate_weight.shape[1]
    taps = conv_weight.shape[0]
    groups = lax.axis_size("g") * lax.axis_size("y")
    slots = lax.axis_size("s")
    chan_run = slots * share
    hid_run = slots * hidden_share
    chan = groups * chan_run
    hid = groups * hid_run

    def by_place(weight, parts, team, run):
        count = weight.shape[1] // (parts * team * run)
        split = weight.reshape(share, parts, count, team, run)
        return jnp.transpose(split, (3, 0, 1, 2, 4)).reshape(team, share, parts * count * run)

    def side_by_side(block, width):
        return jnp.concatenate(
            [block[..., j * share : (j + 1) * share, :width] for j in range(features // width)],
            axis=-1,
        )

    def stacked(block, width):
        return jnp.concatenate(
            [block[..., j * width : (j + 1) * width] for j in range(features // width)], axis=-2
        )

    in_blocks = by_place(in_weight, 3, TEAM, chan_run)
    in_mine = jnp.concatenate(exchange([in_blocks[j] for j in range(TEAM)]), axis=0)
    gains = jnp.concatenate([norm_gain, ffn_gain]).reshape(1, 2 * share)
    near_gains = team_rows(gains)
    gains_row = jnp.concatenate(reorder([near_gains[j : j + 1] for j in range(TEAM)]), axis=1)
    def as_row(values):
        return jnp.pad(values, ((0, 0), (0, features - values.shape[1])))

    first_pack = jnp.concatenate(
        [
            jnp.concatenate([in_mine, stacked(out_weight, chan)], axis=1),
            as_row(conv_weight.reshape(1, taps * share)),
            as_row(gains_row),
            jnp.zeros((EXTRA_ROWS - 2, features), bf16),
        ],
        axis=0,
    )
    tall = TEAM * share

    def first_unpack(block):
        return [
            block[:tall, : 3 * chan].reshape(TEAM, share, 3 * chan),
            side_by_side(block[:tall, 3 * chan :], chan),
            block[tall, : taps * share].reshape(taps, share),
            block[tall + 1, : 2 * tall].reshape(TEAM, 2, share),
        ]

    pair_blocks = jnp.concatenate(
        [by_place(gate_weight, 1, TEAM, hid_run), by_place(up_weight, 1, TEAM, hid_run)], axis=2
    )
    pair_mine = jnp.concatenate(exchange([pair_blocks[j] for j in range(TEAM)]), axis=0)

    first_all = lax.all_gather(first_pack, ("g", "y", "s"), axis=0, tiled=False)
    in_all, out_all, conv_all, gains_all = [
        part.reshape((groups, slots) + part.shape[1:]) for part in jax.vmap(first_unpack)(first_all)
    ]

    pair_all = lax.all_gather(pair_mine, ("g", "y", "s"), axis=0, tiled=False)
    down_full = lax.all_gather(down_weight, ("g", "y", "s"), axis=0, tiled=True)

    in_full = jnp.transpose(in_all, (0, 2, 1, 3, 4)).reshape(features, 3 * chan)
    out_full = out_all.reshape(chan, features)
    conv_full = jnp.transpose(conv_all, (2, 0, 1, 3)).reshape(taps, chan).astype(f32)
    gains_full = jnp.transpose(gains_all, (3, 0, 2, 1, 4)).reshape(2, features).astype(f32)
    norm_full, ffn_full = gains_full[0], gains_full[1]
    pair_full = jnp.transpose(
        pair_all.reshape(groups, slots, TEAM, share, 2 * hid), (0, 2, 1, 3, 4)
    ).reshape(features, 2 * hid)

    own_tokens = tokens.reshape(rows, features)
    places = positions.reshape(rows, 1)
    team_tokens = team_rows(own_tokens)
    team_places = team_rows(places)
    live = (places >= 0).astype(f32)
    upstream = cotangent.reshape(rows, features).astype(f32)
    ffn_pieces = team_pieces((live * upstream).astype(bf16))
    inputs = tokens.reshape(rows, features).astype(f32)

    values = team_tokens.astype(f32)
    early_full = after(norm_full, ffn_pieces[3][-1:])
    first_normed = (values * inverse_rms(values) * early_full).astype(bf16)
    projected = forward_dot(first_normed, in_full)
    b_part = projected[:, :chan]
    c_part = projected[:, chan : 2 * chan]
    x_part = projected[:, 2 * chan :]
    mixed = b_part * x_part
    mask_one = (team_places >= 1).astype(f32)
    mask_two = (team_places >= 2).astype(f32)
    mixed_one = mask_one * shifted_down(mixed, 1)
    mixed_two = mask_two * shifted_down(mixed, 2)
    convolved = conv_full[0] * mixed + conv_full[1] * mixed_one + conv_full[2] * mixed_two
    mixer_in = (c_part * convolved).astype(bf16)
    mixer_out = team_sum(forward_dot(mixer_in, out_full).astype(bf16))
    middle = inputs + live * mixer_out
    second_scale = inverse_rms(middle)
    second_pieces = team_pieces((middle * second_scale * ffn_full).astype(bf16))

    team_count = TEAM * rows
    unit = 2 * team_count * features * hid
    hidden, silu, slope, second_normed, ffn_grad = by_rows(
        forward_kernel,
        rows,
        TEAM,
        [],
        second_pieces + ffn_pieces + [pair_full],
        [],
        [hid] * 3 + [features] * 2,
        2 * unit,
        team_count * hid,
    )
    owners = groups * slots
    down_part = rows_dot(hidden, ffn_grad).astype(bf16)
    grad_down = scatter_rest(down_part.reshape(owners, hidden_share, features))
    pair_grad, normed_part, out_part = by_rows(
        backward_kernel,
        ROW_TILE,
        team_count // ROW_TILE,
        [ffn_grad, hidden, silu, slope],
        [pair_full, down_full],
        [down_part],
        [2 * hid, features, features],
        4 * unit,
        0,
    )

    def by_owner(grad, team):
        width = grad.shape[-1]
        count = features // (team * slots * share)
        split = grad.astype(bf16).reshape(count, team, slots, share, width)
        return jnp.transpose(split, (0, 2, 1, 3, 4)).reshape(count, slots, team * share, width)

    pair_part = by_owner(rows_dot(second_normed, pair_grad), TEAM)
    pair_sum = scatter_rest(pair_part.reshape(owners, tall, 2 * hid))
    normed_sum = team_sum(normed_part, pair_part[0, 0, :1])
    second_weighted = ffn_full * normed_sum
    middle_grad = upstream + norm_back(middle, second_scale, second_weighted)

    mixer_grad = team_rows((live * middle_grad).astype(bf16))
    mixer_in_grad = back_dot(mixer_grad, out_full)
    c_grad = mixer_in_grad * convolved
    conv_grad = mixer_in_grad * c_part
    mixed_grad = (
        conv_full[0] * conv_grad
        + conv_full[1] * shifted_up(mask_one * conv_grad, 1)
        + conv_full[2] * shifted_up(mask_two * conv_grad, 2)
    )
    projected_grad = jnp.concatenate(
        [mixed_grad * x_part, c_grad, mixed_grad * b_part], axis=1
    ).astype(bf16)
    grad_conv_part = jnp.stack(
        [
            jnp.sum(conv_grad * mixed, axis=0),
            jnp.sum(conv_grad * mixed_one, axis=0),
            jnp.sum(conv_grad * mixed_two, axis=0),
        ]
    )
    in_part = by_owner(rows_dot(first_normed, projected_grad), TEAM)
    out_grad_part = rows_dot(mixer_in, mixer_grad).astype(bf16)
    out_grad_part = stacked(out_grad_part.reshape(groups, slots, share, features), chan)
    conv_rows = jnp.transpose(
        grad_conv_part.reshape(taps, groups, slots, share), (1, 2, 0, 3)
    ).reshape(groups, slots, 1, taps * share)
    conv_rows = jnp.pad(
        conv_rows.astype(bf16),
        ((0, 0), (0, 0), (0, EXTRA_ROWS - 1), (0, features - taps * share)),
    )
    first_sum = scatter_first(
        jnp.concatenate(
            [jnp.concatenate([in_part, out_grad_part], axis=3), conv_rows], axis=2
        )
    )

    first_weighted = norm_full * team_sum(back_dot(projected_grad, in_full).astype(bf16))
    input_grad = middle_grad + norm_back(inputs, inverse_rms(inputs), first_weighted)
    input_grad = input_grad.astype(bf16)
    out_sum = team_sum(after(out_part, mixer_grad[-1:]))
    block_out = (middle + live * out_sum).astype(bf16)

    def own_rows(summed, parts, team, run):
        blocks = [summed[j * share : (j + 1) * share].astype(bf16) for j in range(team)]
        came = [block.reshape(share, parts, -1, 1, run) for block in exchange(blocks)]
        joined = jnp.concatenate(came, axis=3)
        return joined.reshape(share, -1).astype(f32)

    pair_rows = own_rows(pair_sum, 2, TEAM, hid_run)
    gate_rows = pair_rows[:, :hidden_width]
    up_rows = pair_rows[:, hidden_width:]
    in_rows = own_rows(first_sum[:tall, : 3 * chan], 3, TEAM, chan_run)
    grad_out = side_by_side(first_sum[:tall, 3 * chan :], chan).astype(f32)
    grad_conv = first_sum[tall, : taps * share].reshape(taps, share).astype(f32)
    grad_norm_gain = jnp.sum(in_weight.astype(f32) * in_rows, axis=1) / norm_gain.astype(f32)
    grad_ffn_gain = jnp.sum(
        gate_weight.astype(f32) * gate_rows + up_weight.astype(f32) * up_rows, axis=1
    ) / ffn_gain.astype(f32)
    return (
        block_out.reshape(shape),
        input_grad.reshape(shape),
        grad_norm_gain,
        in_rows,
        grad_conv,
        grad_out,
        grad_ffn_gain,
        gate_rows,
        up_rows,
        grad_down.astype(f32),
    )


def solution(mesh):
    every = ("g", "y", "x", "c", "s")
    outer = mesh.shape["dp"] // (2 * TEAM)
    teams = Mesh(mesh.devices.reshape(outer, 2, 2, 2, mesh.shape["shard"]), every)
    return jax.shard_map(
        per_device,
        mesh=teams,
        in_specs=(
            P(None, every, None),
            P(None, every),
            P(None, every, None),
            P(every),
            P(every, None),
            P(None, every),
            P(every, None),
            P(every),
            P(every, None),
            P(every, None),
            P(every, None),
        ),
        out_specs=(
            P(None, every, None),
            P(None, every, None),
            P(every),
            P(every, None),
            P(None, every),
            P(every, None),
            P(every),
            P(every, None),
            P(every, None),
            P(every, None),
        ),
        check_vma=False,
    )
```

```python
import jax
import jax.numpy as jnp
from jax import lax
from jax.experimental import pallas as pl
from jax.experimental.pallas import tpu as pltpu
from jax.sharding import Mesh, PartitionSpec as P

EPSILON = 1e-05
TEAM = 4
EXTRA_ROWS = 16
ROW_TILE = 512
bf16 = jnp.bfloat16
f32 = jnp.float32


def forward_dot(left_side, right_side):
    return jnp.dot(left_side, right_side, preferred_element_type=f32)


def rows_dot(left_side, right_side):
    return lax.dot_general(
        left_side, right_side, (((0,), (0,)), ((), ())), preferred_element_type=f32
    )


def back_dot(left_side, right_side):
    return lax.dot_general(
        left_side, right_side, (((1,), (1,)), ((), ())), preferred_element_type=f32
    )


def swap_core(values):
    return lax.ppermute(values, "c", [(0, 1), (1, 0)])


def swap_chip(values):
    return lax.ppermute(values, "x", [(0, 1), (1, 0)])


def swap_row(values):
    return lax.ppermute(values, "y", [(0, 1), (1, 0)])


def swap_far(values, distance):
    return lax.ppermute(values, ("x", "c"), [(i, i ^ distance) for i in range(TEAM)])


def after(values, token):
    return values + (token.ravel()[0] * 0).astype(values.dtype)


def reorder(blocks):
    blocks = list(blocks)
    for bit, axis in ((1, "c"), (2, "x")):
        odd = lax.axis_index(axis) == 1
        blocks = [jnp.where(odd, blocks[j ^ bit], blocks[j]) for j in range(len(blocks))]
    return blocks


def exchange(blocks):
    near = reorder(blocks)
    return reorder(near[:1] + [swap_far(near[j], j) for j in range(1, len(near))])


def team_pieces(rows):
    across = swap_chip(rows)
    return [rows, swap_core(rows), across, swap_core(across)]


def team_rows(rows):
    return jnp.concatenate(team_pieces(rows), axis=0)


def team_sum(terms, token=None):
    count = terms.shape[0] // TEAM
    sent = jnp.concatenate([terms[count : 2 * count], terms[3 * count :]], axis=0)
    came = swap_core(sent).astype(f32)
    own = terms[:count].astype(f32) + came[:count]
    other = terms[2 * count : 3 * count].astype(f32) + came[count:]
    came = swap_chip(other.astype(bf16)).astype(f32)
    return own + (came if token is None else after(came, token))


def take(blocks, index):
    return lax.dynamic_index_in_dim(blocks, index, axis=0, keepdims=False)


def scatter(part, token=None):
    groups, slots = part.shape[:2]
    if groups == 2:
        row = lax.axis_index("y")
        came = swap_row(take(part, 1 - row)).astype(f32)
        if token is not None:
            came = after(came, token)
        summed = (take(part, row).astype(f32) + came).astype(bf16)
        return lax.psum_scatter(summed, "s", scatter_dimension=0, tiled=False)
    flat = part.reshape((groups * slots,) + part.shape[2:]).astype(f32)
    return lax.psum_scatter(flat, ("g", "y", "s"), scatter_dimension=0, tiled=False)


def forward_kernel(*refs):
    pieces, pair_ref = refs[: 2 * TEAM], refs[2 * TEAM]
    hidden_ref, silu_ref, slope_ref, normed_ref, grad_ref = refs[2 * TEAM + 1 :]
    for k in range(TEAM):

        @pl.when(pl.program_id(0) == k)
        def _():
            normed_ref[...] = pieces[k][...]
            grad_ref[...] = pieces[TEAM + k][...]

    width = hidden_ref.shape[1]
    values = forward_dot(normed_ref[...], pair_ref[...])
    gate_value, up_value = values[:, :width], values[:, width:]
    sigmoid = jax.nn.sigmoid(gate_value)
    silu = gate_value * sigmoid
    hidden_ref[...] = (silu * up_value).astype(bf16)
    silu_ref[...] = silu.astype(bf16)
    slope_ref[...] = (up_value * (sigmoid * (1 + gate_value * (1 - sigmoid)))).astype(bf16)


def backward_kernel(
    grad_ref,
    hidden_ref,
    silu_ref,
    slope_ref,
    pair_ref,
    down_ref,
    token_ref,
    pair_grad_ref,
    normed_ref,
    out_ref,
):
    del token_ref
    width = hidden_ref.shape[1]
    hidden_grad = back_dot(grad_ref[...], down_ref[...])
    pair_grad_ref[:, :width] = (hidden_grad * slope_ref[...].astype(f32)).astype(bf16)
    pair_grad_ref[:, width:] = (hidden_grad * silu_ref[...].astype(f32)).astype(bf16)
    normed_ref[...] = back_dot(pair_grad_ref[...], pair_ref[...]).astype(bf16)
    out_ref[...] = forward_dot(hidden_ref[...], down_ref[...]).astype(bf16)


def by_rows(kernel, tile, steps, rowed, whole, tokens, columns, flops, transcendentals):
    rows = steps * tile

    def row_block(count):
        return pl.BlockSpec((tile, count), lambda i: (i, 0))

    moved = sum(2 * value.size for value in rowed + whole) + 2 * rows * sum(columns)
    return pl.pallas_call(
        kernel,
        grid=(steps,),
        in_specs=[row_block(value.shape[1]) for value in rowed]
        + [
            pl.BlockSpec(value.shape, lambda i: (0, 0), pipeline_mode=pl.Buffered(1))
            for value in whole
        ]
        + [pl.BlockSpec(memory_space=pl.ANY)] * len(tokens),
        out_specs=[row_block(count) for count in columns],
        out_shape=[jax.ShapeDtypeStruct((rows, count), bf16) for count in columns],
        compiler_params=pltpu.CompilerParams(vmem_limit_bytes=52 * 1024 * 1024),
        cost_estimate=pl.CostEstimate(
            flops=flops, bytes_accessed=moved, transcendentals=transcendentals
        ),
    )(*rowed, *whole, *tokens)


def shifted_down(rows, step):
    return jnp.concatenate(
        [jnp.zeros((step, rows.shape[1]), rows.dtype), rows[:-step]], axis=0
    )


def shifted_up(rows, step):
    return jnp.concatenate(
        [rows[step:], jnp.zeros((step, rows.shape[1]), rows.dtype)], axis=0
    )


def inverse_rms(values):
    return lax.rsqrt(jnp.mean(values * values, axis=-1, keepdims=True) + EPSILON)


def norm_back(values, scale, weighted):
    return scale * weighted - values * (
        scale * scale * scale * jnp.mean(weighted * values, axis=-1, keepdims=True)
    )


def per_device(
    tokens,
    positions,
    cotangent,
    norm_gain,
    in_weight,
    conv_weight,
    out_weight,
    ffn_gain,
    gate_weight,
    up_weight,
    down_weight,
):
    shape = tokens.shape
    features = shape[2]
    rows = shape[0] * shape[1]
    share = in_weight.shape[0]
    hidden_share = down_weight.shape[0]
    hidden_width = gate_weight.shape[1]
    taps = conv_weight.shape[0]
    groups = lax.axis_size("g") * lax.axis_size("y")
    slots = lax.axis_size("s")
    chan_run = slots * share
    hid_run = slots * hidden_share
    chan = groups * chan_run
    hid = groups * hid_run

    def by_place(weight, parts, team, run):
        count = weight.shape[1] // (parts * team * run)
        split = weight.reshape(share, parts, count, team, run)
        return jnp.transpose(split, (3, 0, 1, 2, 4)).reshape(team, share, parts * count * run)

    def side_by_side(block, width):
        return jnp.concatenate(
            [block[..., j * share : (j + 1) * share, :width] for j in range(features // width)],
            axis=-1,
        )

    def stacked(block, width):
        return jnp.concatenate(
            [block[..., j * width : (j + 1) * width] for j in range(features // width)], axis=-2
        )

    in_blocks = by_place(in_weight, 3, TEAM, chan_run)
    in_mine = jnp.concatenate(exchange([in_blocks[j] for j in range(TEAM)]), axis=0)
    gains = jnp.concatenate([norm_gain, ffn_gain]).reshape(1, 2 * share)
    near_gains = team_rows(gains)
    gains_row = jnp.concatenate(reorder([near_gains[j : j + 1] for j in range(TEAM)]), axis=1)
    def as_row(values):
        return jnp.pad(values, ((0, 0), (0, features - values.shape[1])))

    first_pack = jnp.concatenate(
        [
            jnp.concatenate([in_mine, stacked(out_weight, chan)], axis=1),
            as_row(conv_weight.reshape(1, taps * share)),
            as_row(gains_row),
            jnp.zeros((EXTRA_ROWS - 2, features), bf16),
        ],
        axis=0,
    )
    tall = TEAM * share

    def first_unpack(block):
        return [
            block[:tall, : 3 * chan].reshape(TEAM, share, 3 * chan),
            side_by_side(block[:tall, 3 * chan :], chan),
            block[tall, : taps * share].reshape(taps, share),
            block[tall + 1, : 2 * tall].reshape(TEAM, 2, share),
        ]

    pair_blocks = jnp.concatenate(
        [by_place(gate_weight, 1, TEAM, hid_run), by_place(up_weight, 1, TEAM, hid_run)], axis=2
    )
    pair_mine = jnp.concatenate(exchange([pair_blocks[j] for j in range(TEAM)]), axis=0)

    first_all = lax.all_gather(first_pack, ("g", "y", "s"), axis=0, tiled=False)
    in_all, out_all, conv_all, gains_all = [
        part.reshape((groups, slots) + part.shape[1:]) for part in jax.vmap(first_unpack)(first_all)
    ]

    pair_all = lax.all_gather(pair_mine, ("g", "y", "s"), axis=0, tiled=False)
    down_full = lax.all_gather(down_weight, ("g", "y", "s"), axis=0, tiled=True)

    in_full = jnp.transpose(in_all, (0, 2, 1, 3, 4)).reshape(features, 3 * chan)
    out_full = out_all.reshape(chan, features)
    conv_full = jnp.transpose(conv_all, (2, 0, 1, 3)).reshape(taps, chan).astype(f32)
    gains_full = jnp.transpose(gains_all, (3, 0, 2, 1, 4)).reshape(2, features).astype(f32)
    norm_full, ffn_full = gains_full[0], gains_full[1]
    pair_full = jnp.transpose(
        pair_all.reshape(groups, slots, TEAM, share, 2 * hid), (0, 2, 1, 3, 4)
    ).reshape(features, 2 * hid)

    own_tokens = tokens.reshape(rows, features)
    places = positions.reshape(rows, 1)
    team_tokens = team_rows(own_tokens)
    team_places = team_rows(places)
    live = (places >= 0).astype(f32)
    upstream = cotangent.reshape(rows, features).astype(f32)
    ffn_pieces = team_pieces((live * upstream).astype(bf16))
    inputs = tokens.reshape(rows, features).astype(f32)

    values = team_tokens.astype(f32)
    early_full = after(norm_full, ffn_pieces[3][-1:])
    first_normed = (values * inverse_rms(values) * early_full).astype(bf16)
    projected = forward_dot(first_normed, in_full)
    b_part = projected[:, :chan]
    c_part = projected[:, chan : 2 * chan]
    x_part = projected[:, 2 * chan :]
    mixed = b_part * x_part
    mask_one = (team_places >= 1).astype(f32)
    mask_two = (team_places >= 2).astype(f32)
    mixed_one = mask_one * shifted_down(mixed, 1)
    mixed_two = mask_two * shifted_down(mixed, 2)
    convolved = conv_full[0] * mixed + conv_full[1] * mixed_one + conv_full[2] * mixed_two
    mixer_in = (c_part * convolved).astype(bf16)
    mixer_out = team_sum(forward_dot(mixer_in, out_full).astype(bf16))
    middle = inputs + live * mixer_out
    second_scale = inverse_rms(middle)
    second_pieces = team_pieces((middle * second_scale * ffn_full).astype(bf16))

    team_count = TEAM * rows
    unit = 2 * team_count * features * hid
    hidden, silu, slope, second_normed, ffn_grad = by_rows(
        forward_kernel,
        rows,
        TEAM,
        [],
        second_pieces + ffn_pieces + [pair_full],
        [],
        [hid] * 3 + [features] * 2,
        2 * unit,
        team_count * hid,
    )
    down_part = rows_dot(hidden, ffn_grad).astype(bf16)
    grad_down = scatter(down_part.reshape(groups, slots, hidden_share, features))
    pair_grad, normed_part, out_part = by_rows(
        backward_kernel,
        ROW_TILE,
        team_count // ROW_TILE,
        [ffn_grad, hidden, silu, slope],
        [pair_full, down_full],
        [down_part],
        [2 * hid, features, features],
        4 * unit,
        0,
    )

    def by_owner(grad, team):
        width = grad.shape[-1]
        count = features // (team * slots * share)
        split = grad.astype(bf16).reshape(count, team, slots, share, width)
        return jnp.transpose(split, (0, 2, 1, 3, 4)).reshape(count, slots, team * share, width)

    pair_part = by_owner(rows_dot(second_normed, pair_grad), TEAM)
    pair_sum = scatter(pair_part)
    normed_sum = team_sum(normed_part, pair_part[0, 0, :1])
    second_weighted = after(ffn_full, grad_down[:1]) * normed_sum
    middle_grad = upstream + norm_back(middle, second_scale, second_weighted)

    mixer_grad = team_rows((live * middle_grad).astype(bf16))
    mixer_in_grad = back_dot(mixer_grad, out_full)
    c_grad = mixer_in_grad * convolved
    conv_grad = mixer_in_grad * c_part
    mixed_grad = (
        conv_full[0] * conv_grad
        + conv_full[1] * shifted_up(mask_one * conv_grad, 1)
        + conv_full[2] * shifted_up(mask_two * conv_grad, 2)
    )
    projected_grad = jnp.concatenate(
        [mixed_grad * x_part, c_grad, mixed_grad * b_part], axis=1
    ).astype(bf16)
    grad_conv_part = jnp.stack(
        [
            jnp.sum(conv_grad * mixed, axis=0),
            jnp.sum(conv_grad * mixed_one, axis=0),
            jnp.sum(conv_grad * mixed_two, axis=0),
        ]
    )
    in_part = by_owner(rows_dot(first_normed, projected_grad), TEAM)
    out_grad_part = rows_dot(mixer_in, mixer_grad).astype(bf16)
    out_grad_part = stacked(out_grad_part.reshape(groups, slots, share, features), chan)
    conv_rows = jnp.transpose(
        grad_conv_part.reshape(taps, groups, slots, share), (1, 2, 0, 3)
    ).reshape(groups, slots, 1, taps * share)
    conv_rows = jnp.pad(
        conv_rows.astype(bf16),
        ((0, 0), (0, 0), (0, EXTRA_ROWS - 1), (0, features - taps * share)),
    )
    first_sum = scatter(
        jnp.concatenate(
            [jnp.concatenate([in_part, out_grad_part], axis=3), conv_rows], axis=2
        ),
        pair_sum[:1],
    )

    first_weighted = norm_full * team_sum(back_dot(projected_grad, in_full).astype(bf16))
    input_grad = middle_grad + norm_back(inputs, inverse_rms(inputs), first_weighted)
    input_grad = input_grad.astype(bf16)
    out_sum = team_sum(after(out_part, mixer_grad[-1:]))
    block_out = (middle + live * out_sum).astype(bf16)

    def own_rows(summed, parts, team, run):
        blocks = [summed[j * share : (j + 1) * share].astype(bf16) for j in range(team)]
        came = [block.reshape(share, parts, -1, 1, run) for block in exchange(blocks)]
        joined = jnp.concatenate(came, axis=3)
        return joined.reshape(share, -1).astype(f32)

    pair_rows = own_rows(pair_sum, 2, TEAM, hid_run)
    gate_rows = pair_rows[:, :hidden_width]
    up_rows = pair_rows[:, hidden_width:]
    in_rows = own_rows(first_sum[:tall, : 3 * chan], 3, TEAM, chan_run)
    grad_out = side_by_side(first_sum[:tall, 3 * chan :], chan).astype(f32)
    grad_conv = first_sum[tall, : taps * share].reshape(taps, share).astype(f32)
    grad_norm_gain = jnp.sum(in_weight.astype(f32) * in_rows, axis=1) / norm_gain.astype(f32)
    grad_ffn_gain = jnp.sum(
        gate_weight.astype(f32) * gate_rows + up_weight.astype(f32) * up_rows, axis=1
    ) / ffn_gain.astype(f32)
    return (
        block_out.reshape(shape),
        input_grad.reshape(shape),
        grad_norm_gain,
        in_rows,
        grad_conv,
        grad_out,
        grad_ffn_gain,
        gate_rows,
        up_rows,
        grad_down.astype(f32),
    )


def solution(mesh):
    every = ("g", "y", "x", "c", "s")
    outer = mesh.shape["dp"] // (2 * TEAM)
    teams = Mesh(mesh.devices.reshape(outer, 2, 2, 2, mesh.shape["shard"]), every)
    return jax.shard_map(
        per_device,
        mesh=teams,
        in_specs=(
            P(None, every, None),
            P(None, every),
            P(None, every, None),
            P(every),
            P(every, None),
            P(None, every),
            P(every, None),
            P(every),
            P(every, None),
            P(every, None),
            P(every, None),
        ),
        out_specs=(
            P(None, every, None),
            P(None, every, None),
            P(every),
            P(every, None),
            P(None, every),
            P(every, None),
            P(every),
            P(every, None),
            P(every, None),
            P(every, None),
        ),
        check_vma=False,
    )
```

```python
import jax
import jax.numpy as jnp
from jax import lax
from jax.experimental import pallas as pl
from jax.experimental.pallas import tpu as pltpu
from jax.sharding import Mesh, PartitionSpec as P

EPSILON = 1e-05
TEAM = 4
EXTRA_ROWS = 16
ROW_TILE = 512
bf16 = jnp.bfloat16
f32 = jnp.float32


def forward_dot(left_side, right_side):
    return jnp.dot(left_side, right_side, preferred_element_type=f32)


def rows_dot(left_side, right_side):
    return lax.dot_general(
        left_side, right_side, (((0,), (0,)), ((), ())), preferred_element_type=f32
    )


def back_dot(left_side, right_side):
    return lax.dot_general(
        left_side, right_side, (((1,), (1,)), ((), ())), preferred_element_type=f32
    )


def swap_core(values):
    return lax.ppermute(values, "c", [(0, 1), (1, 0)])


def swap_chip(values):
    return lax.ppermute(values, "x", [(0, 1), (1, 0)])


def swap_row(values):
    return lax.ppermute(values, "y", [(0, 1), (1, 0)])


def swap_far(values, distance):
    return lax.ppermute(values, ("x", "c"), [(i, i ^ distance) for i in range(TEAM)])


def after(values, token):
    return values + (token.ravel()[0] * 0).astype(values.dtype)


def reorder(blocks):
    blocks = list(blocks)
    for bit, axis in ((1, "c"), (2, "x")):
        odd = lax.axis_index(axis) == 1
        blocks = [jnp.where(odd, blocks[j ^ bit], blocks[j]) for j in range(len(blocks))]
    return blocks


def exchange(blocks):
    near = reorder(blocks)
    return reorder(near[:1] + [swap_far(near[j], j) for j in range(1, len(near))])


def team_pieces(rows):
    across = swap_chip(rows)
    return [rows, swap_core(rows), across, swap_core(across)]


def team_rows(rows):
    return jnp.concatenate(team_pieces(rows), axis=0)


def team_sum(terms, token=None):
    count = terms.shape[0] // TEAM
    sent = jnp.concatenate([terms[count : 2 * count], terms[3 * count :]], axis=0)
    came = swap_core(sent).astype(f32)
    own = terms[:count].astype(f32) + came[:count]
    other = terms[2 * count : 3 * count].astype(f32) + came[count:]
    other = other.astype(bf16)
    came = swap_chip(other).astype(f32)
    return own + (came if token is None else after(came, token)), other[:1, :1]


def take(blocks, index):
    return lax.dynamic_index_in_dim(blocks, index, axis=0, keepdims=False)


def scatter(part, *tokens):
    groups, slots = part.shape[:2]
    if groups == 2:
        row = lax.axis_index("y")
        came = swap_row(take(part, 1 - row)).astype(f32)
        for token in tokens:
            came = after(came, token)
        summed = (take(part, row).astype(f32) + came).astype(bf16)
        return lax.psum_scatter(summed, "s", scatter_dimension=0, tiled=False)
    flat = part.reshape((groups * slots,) + part.shape[2:]).astype(f32)
    return lax.psum_scatter(flat, ("g", "y", "s"), scatter_dimension=0, tiled=False)


def forward_kernel(*refs):
    pieces, pair_ref = refs[: 2 * TEAM], refs[2 * TEAM]
    hidden_ref, silu_ref, slope_ref, normed_ref, grad_ref = refs[2 * TEAM + 1 :]
    for k in range(TEAM):

        @pl.when(pl.program_id(0) == k)
        def _():
            normed_ref[...] = pieces[k][...]
            grad_ref[...] = pieces[TEAM + k][...]

    width = hidden_ref.shape[1]
    values = forward_dot(normed_ref[...], pair_ref[...])
    gate_value, up_value = values[:, :width], values[:, width:]
    sigmoid = jax.nn.sigmoid(gate_value)
    silu = gate_value * sigmoid
    hidden_ref[...] = (silu * up_value).astype(bf16)
    silu_ref[...] = silu.astype(bf16)
    slope_ref[...] = (up_value * (sigmoid * (1 + gate_value * (1 - sigmoid)))).astype(bf16)


def backward_kernel(
    grad_ref,
    hidden_ref,
    silu_ref,
    slope_ref,
    pair_ref,
    down_ref,
    token_ref,
    pair_grad_ref,
    normed_ref,
    out_ref,
):
    del token_ref
    width = hidden_ref.shape[1]
    hidden_grad = back_dot(grad_ref[...], down_ref[...])
    pair_grad_ref[:, :width] = (hidden_grad * slope_ref[...].astype(f32)).astype(bf16)
    pair_grad_ref[:, width:] = (hidden_grad * silu_ref[...].astype(f32)).astype(bf16)
    normed_ref[...] = back_dot(pair_grad_ref[...], pair_ref[...]).astype(bf16)
    out_ref[...] = forward_dot(hidden_ref[...], down_ref[...]).astype(bf16)


def by_rows(kernel, tile, steps, rowed, whole, tokens, columns, flops, transcendentals):
    rows = steps * tile

    def row_block(count):
        return pl.BlockSpec((tile, count), lambda i: (i, 0))

    moved = sum(2 * value.size for value in rowed + whole) + 2 * rows * sum(columns)
    return pl.pallas_call(
        kernel,
        grid=(steps,),
        in_specs=[row_block(value.shape[1]) for value in rowed]
        + [
            pl.BlockSpec(value.shape, lambda i: (0, 0), pipeline_mode=pl.Buffered(1))
            for value in whole
        ]
        + [pl.BlockSpec(memory_space=pl.ANY)] * len(tokens),
        out_specs=[row_block(count) for count in columns],
        out_shape=[jax.ShapeDtypeStruct((rows, count), bf16) for count in columns],
        compiler_params=pltpu.CompilerParams(vmem_limit_bytes=52 * 1024 * 1024),
        cost_estimate=pl.CostEstimate(
            flops=flops, bytes_accessed=moved, transcendentals=transcendentals
        ),
    )(*rowed, *whole, *tokens)


def shifted_down(rows, step):
    return jnp.concatenate(
        [jnp.zeros((step, rows.shape[1]), rows.dtype), rows[:-step]], axis=0
    )


def shifted_up(rows, step):
    return jnp.concatenate(
        [rows[step:], jnp.zeros((step, rows.shape[1]), rows.dtype)], axis=0
    )


def inverse_rms(values):
    return lax.rsqrt(jnp.mean(values * values, axis=-1, keepdims=True) + EPSILON)


def norm_back(values, scale, weighted):
    return scale * weighted - values * (
        scale * scale * scale * jnp.mean(weighted * values, axis=-1, keepdims=True)
    )


def per_device(
    tokens,
    positions,
    cotangent,
    norm_gain,
    in_weight,
    conv_weight,
    out_weight,
    ffn_gain,
    gate_weight,
    up_weight,
    down_weight,
):
    shape = tokens.shape
    features = shape[2]
    rows = shape[0] * shape[1]
    share = in_weight.shape[0]
    hidden_share = down_weight.shape[0]
    hidden_width = gate_weight.shape[1]
    taps = conv_weight.shape[0]
    groups = lax.axis_size("g") * lax.axis_size("y")
    slots = lax.axis_size("s")
    chan_run = slots * share
    hid_run = slots * hidden_share
    chan = groups * chan_run
    hid = groups * hid_run

    def by_place(weight, parts, team, run):
        count = weight.shape[1] // (parts * team * run)
        split = weight.reshape(share, parts, count, team, run)
        return jnp.transpose(split, (3, 0, 1, 2, 4)).reshape(team, share, parts * count * run)

    def side_by_side(block, width):
        return jnp.concatenate(
            [block[..., j * share : (j + 1) * share, :width] for j in range(features // width)],
            axis=-1,
        )

    def stacked(block, width):
        return jnp.concatenate(
            [block[..., j * width : (j + 1) * width] for j in range(features // width)], axis=-2
        )

    in_blocks = by_place(in_weight, 3, TEAM, chan_run)
    in_mine = jnp.concatenate(exchange([in_blocks[j] for j in range(TEAM)]), axis=0)
    gains = jnp.concatenate([norm_gain, ffn_gain]).reshape(1, 2 * share)
    near_gains = team_rows(gains)
    gains_row = jnp.concatenate(reorder([near_gains[j : j + 1] for j in range(TEAM)]), axis=1)
    def as_row(values):
        return jnp.pad(values, ((0, 0), (0, features - values.shape[1])))

    first_pack = jnp.concatenate(
        [
            jnp.concatenate([in_mine, stacked(out_weight, chan)], axis=1),
            as_row(conv_weight.reshape(1, taps * share)),
            as_row(gains_row),
            jnp.zeros((EXTRA_ROWS - 2, features), bf16),
        ],
        axis=0,
    )
    tall = TEAM * share

    def first_unpack(block):
        return [
            block[:tall, : 3 * chan].reshape(TEAM, share, 3 * chan),
            side_by_side(block[:tall, 3 * chan :], chan),
            block[tall, : taps * share].reshape(taps, share),
            block[tall + 1, : 2 * tall].reshape(TEAM, 2, share),
        ]

    pair_blocks = jnp.concatenate(
        [by_place(gate_weight, 1, TEAM, hid_run), by_place(up_weight, 1, TEAM, hid_run)], axis=2
    )
    pair_mine = jnp.concatenate(exchange([pair_blocks[j] for j in range(TEAM)]), axis=0)

    first_all = lax.all_gather(first_pack, ("g", "y", "s"), axis=0, tiled=False)
    in_all, out_all, conv_all, gains_all = [
        part.reshape((groups, slots) + part.shape[1:]) for part in jax.vmap(first_unpack)(first_all)
    ]

    pair_all = lax.all_gather(pair_mine, ("g", "y", "s"), axis=0, tiled=False)
    down_full = lax.all_gather(down_weight, ("g", "y", "s"), axis=0, tiled=True)

    in_full = jnp.transpose(in_all, (0, 2, 1, 3, 4)).reshape(features, 3 * chan)
    out_full = out_all.reshape(chan, features)
    conv_full = jnp.transpose(conv_all, (2, 0, 1, 3)).reshape(taps, chan).astype(f32)
    gains_full = jnp.transpose(gains_all, (3, 0, 2, 1, 4)).reshape(2, features).astype(f32)
    norm_full, ffn_full = gains_full[0], gains_full[1]
    pair_full = jnp.transpose(
        pair_all.reshape(groups, slots, TEAM, share, 2 * hid), (0, 2, 1, 3, 4)
    ).reshape(features, 2 * hid)

    own_tokens = tokens.reshape(rows, features)
    places = positions.reshape(rows, 1)
    team_tokens = team_rows(own_tokens)
    team_places = team_rows(places)
    live = (places >= 0).astype(f32)
    upstream = cotangent.reshape(rows, features).astype(f32)
    ffn_pieces = team_pieces((live * upstream).astype(bf16))
    inputs = tokens.reshape(rows, features).astype(f32)

    values = team_tokens.astype(f32)
    early_full = after(norm_full, ffn_pieces[3][-1:])
    first_normed = (values * inverse_rms(values) * early_full).astype(bf16)
    projected = forward_dot(first_normed, in_full)
    b_part = projected[:, :chan]
    c_part = projected[:, chan : 2 * chan]
    x_part = projected[:, 2 * chan :]
    mixed = b_part * x_part
    mask_one = (team_places >= 1).astype(f32)
    mask_two = (team_places >= 2).astype(f32)
    mixed_one = mask_one * shifted_down(mixed, 1)
    mixed_two = mask_two * shifted_down(mixed, 2)
    convolved = conv_full[0] * mixed + conv_full[1] * mixed_one + conv_full[2] * mixed_two
    mixer_in = (c_part * convolved).astype(bf16)
    mixer_out = team_sum(forward_dot(mixer_in, out_full).astype(bf16))
    middle = inputs + live * mixer_out[0]
    second_scale = inverse_rms(middle)
    second_pieces = team_pieces((middle * second_scale * ffn_full).astype(bf16))

    team_count = TEAM * rows
    unit = 2 * team_count * features * hid
    hidden, silu, slope, second_normed, ffn_grad = by_rows(
        forward_kernel,
        rows,
        TEAM,
        [],
        second_pieces + ffn_pieces + [pair_full],
        [],
        [hid] * 3 + [features] * 2,
        2 * unit,
        team_count * hid,
    )
    down_part = rows_dot(hidden, ffn_grad).astype(bf16)
    grad_down = scatter(down_part.reshape(groups, slots, hidden_share, features))
    pair_grad, normed_part, out_part = by_rows(
        backward_kernel,
        ROW_TILE,
        team_count // ROW_TILE,
        [ffn_grad, hidden, silu, slope],
        [pair_full, down_full],
        [down_part],
        [2 * hid, features, features],
        4 * unit,
        0,
    )

    def by_owner(grad, team):
        width = grad.shape[-1]
        count = features // (team * slots * share)
        split = grad.astype(bf16).reshape(count, team, slots, share, width)
        return jnp.transpose(split, (0, 2, 1, 3, 4)).reshape(count, slots, team * share, width)

    pair_part = by_owner(rows_dot(second_normed, pair_grad), TEAM)
    normed_sum, _ = team_sum(normed_part, pair_part[0, 0, :1])
    second_weighted = ffn_full * normed_sum
    middle_grad = upstream + norm_back(middle, second_scale, second_weighted)

    mixer_grad = team_rows((live * middle_grad).astype(bf16))
    mixer_in_grad = back_dot(mixer_grad, out_full)
    c_grad = mixer_in_grad * convolved
    conv_grad = mixer_in_grad * c_part
    conv_back = after(conv_full, grad_down[:1])
    mixed_grad = (
        conv_back[0] * conv_grad
        + conv_back[1] * shifted_up(mask_one * conv_grad, 1)
        + conv_back[2] * shifted_up(mask_two * conv_grad, 2)
    )
    projected_grad = jnp.concatenate(
        [mixed_grad * x_part, c_grad, mixed_grad * b_part], axis=1
    ).astype(bf16)
    grad_conv_part = jnp.stack(
        [
            jnp.sum(conv_grad * mixed, axis=0),
            jnp.sum(conv_grad * mixed_one, axis=0),
            jnp.sum(conv_grad * mixed_two, axis=0),
        ]
    )
    in_part = by_owner(rows_dot(first_normed, projected_grad), TEAM)
    out_grad_part = rows_dot(mixer_in, mixer_grad).astype(bf16)
    out_grad_part = stacked(out_grad_part.reshape(groups, slots, share, features), chan)
    conv_rows = jnp.transpose(
        grad_conv_part.reshape(taps, groups, slots, share), (1, 2, 0, 3)
    ).reshape(groups, slots, 1, taps * share)
    conv_rows = jnp.pad(
        conv_rows.astype(bf16),
        ((0, 0), (0, 0), (0, EXTRA_ROWS - 1), (0, features - taps * share)),
    )
    pair_sum = scatter(pair_part, projected_grad[-1:])
    first_weighted, first_sent = team_sum(back_dot(projected_grad, in_full).astype(bf16))
    input_grad = middle_grad + norm_back(inputs, inverse_rms(inputs), norm_full * first_weighted)
    input_grad = input_grad.astype(bf16)
    out_sum, _ = team_sum(after(out_part, mixer_grad[-1:]))
    block_out = (middle + live * out_sum).astype(bf16)
    first_sum = scatter(
        jnp.concatenate(
            [jnp.concatenate([in_part, out_grad_part], axis=3), conv_rows], axis=2
        ),
        pair_sum[:1],
        first_sent,
        block_out[:1],
    )

    def own_rows(summed, parts, team, run):
        blocks = [summed[j * share : (j + 1) * share].astype(bf16) for j in range(team)]
        came = [block.reshape(share, parts, -1, 1, run) for block in exchange(blocks)]
        joined = jnp.concatenate(came, axis=3)
        return joined.reshape(share, -1).astype(f32)

    pair_rows = own_rows(pair_sum, 2, TEAM, hid_run)
    gate_rows = pair_rows[:, :hidden_width]
    up_rows = pair_rows[:, hidden_width:]
    in_rows = own_rows(first_sum[:tall, : 3 * chan], 3, TEAM, chan_run)
    grad_out = side_by_side(first_sum[:tall, 3 * chan :], chan).astype(f32)
    grad_conv = first_sum[tall, : taps * share].reshape(taps, share).astype(f32)
    grad_norm_gain = jnp.sum(in_weight.astype(f32) * in_rows, axis=1) / norm_gain.astype(f32)
    grad_ffn_gain = jnp.sum(
        gate_weight.astype(f32) * gate_rows + up_weight.astype(f32) * up_rows, axis=1
    ) / ffn_gain.astype(f32)
    return (
        block_out.reshape(shape),
        input_grad.reshape(shape),
        grad_norm_gain,
        in_rows,
        grad_conv,
        grad_out,
        grad_ffn_gain,
        gate_rows,
        up_rows,
        grad_down.astype(f32),
    )


def solution(mesh):
    every = ("g", "y", "x", "c", "s")
    outer = mesh.shape["dp"] // (2 * TEAM)
    teams = Mesh(mesh.devices.reshape(outer, 2, 2, 2, mesh.shape["shard"]), every)
    return jax.shard_map(
        per_device,
        mesh=teams,
        in_specs=(
            P(None, every, None),
            P(None, every),
            P(None, every, None),
            P(every),
            P(every, None),
            P(None, every),
            P(every, None),
            P(every),
            P(every, None),
            P(every, None),
            P(every, None),
        ),
        out_specs=(
            P(None, every, None),
            P(None, every, None),
            P(every),
            P(every, None),
            P(None, every),
            P(every, None),
            P(every),
            P(every, None),
            P(every, None),
            P(every, None),
        ),
        check_vma=False,
    )
```

```python
import jax
import jax.numpy as jnp
from jax import lax
from jax.experimental import pallas as pl
from jax.experimental.pallas import tpu as pltpu
from jax.sharding import Mesh, PartitionSpec as P

EPSILON = 1e-05
TEAM = 4
EXTRA_ROWS = 16
ROW_TILE = 512
bf16 = jnp.bfloat16
f32 = jnp.float32


def forward_dot(left_side, right_side):
    return jnp.dot(left_side, right_side, preferred_element_type=f32)


def rows_dot(left_side, right_side):
    return lax.dot_general(
        left_side, right_side, (((0,), (0,)), ((), ())), preferred_element_type=f32
    )


def back_dot(left_side, right_side):
    return lax.dot_general(
        left_side, right_side, (((1,), (1,)), ((), ())), preferred_element_type=f32
    )


def swap_core(values):
    return lax.ppermute(values, "c", [(0, 1), (1, 0)])


def swap_chip(values):
    return lax.ppermute(values, "x", [(0, 1), (1, 0)])


def swap_row(values):
    return lax.ppermute(values, "y", [(0, 1), (1, 0)])


def swap_far(values, distance):
    return lax.ppermute(values, ("x", "c"), [(i, i ^ distance) for i in range(TEAM)])


def after(values, token):
    return values + (token.ravel()[0] * 0).astype(values.dtype)


def reorder(blocks):
    blocks = list(blocks)
    for bit, axis in ((1, "c"), (2, "x")):
        odd = lax.axis_index(axis) == 1
        blocks = [jnp.where(odd, blocks[j ^ bit], blocks[j]) for j in range(len(blocks))]
    return blocks


def exchange(blocks):
    near = reorder(blocks)
    return reorder(near[:1] + [swap_far(near[j], j) for j in range(1, len(near))])


def team_pieces(rows):
    across = swap_chip(rows)
    return [rows, swap_core(rows), across, swap_core(across)]


def team_rows(rows):
    return jnp.concatenate(team_pieces(rows), axis=0)


def team_sum(terms, token=None):
    count = terms.shape[0] // TEAM
    sent = jnp.concatenate([terms[count : 2 * count], terms[3 * count :]], axis=0)
    came = swap_core(sent).astype(f32)
    own = terms[:count].astype(f32) + came[:count]
    other = terms[2 * count : 3 * count].astype(f32) + came[count:]
    other = other.astype(bf16)
    came = swap_chip(other).astype(f32)
    return own + (came if token is None else after(came, token)), other[:1, :1]


def take(blocks, index):
    return lax.dynamic_index_in_dim(blocks, index, axis=0, keepdims=False)


def scatter(part, *tokens):
    groups, slots = part.shape[:2]
    if groups == 2:
        row = lax.axis_index("y")
        came = swap_row(take(part, 1 - row)).astype(f32)
        for token in tokens:
            came = after(came, token)
        summed = (take(part, row).astype(f32) + came).astype(bf16)
        return lax.psum_scatter(summed, "s", scatter_dimension=0, tiled=False)
    flat = part.reshape((groups * slots,) + part.shape[2:]).astype(f32)
    return lax.psum_scatter(flat, ("g", "y", "s"), scatter_dimension=0, tiled=False)


def scatter_plain(part):
    groups, slots = part.shape[:2]
    flat = part.reshape((groups * slots,) + part.shape[2:])
    if groups > 2:
        flat = flat.astype(f32)
    return lax.psum_scatter(flat, ("g", "y", "s"), scatter_dimension=0, tiled=False)


def forward_kernel(*refs):
    pieces, pair_ref = refs[: 2 * TEAM], refs[2 * TEAM]
    hidden_ref, silu_ref, slope_ref, normed_ref, grad_ref = refs[2 * TEAM + 1 :]
    for k in range(TEAM):

        @pl.when(pl.program_id(0) == k)
        def _():
            normed_ref[...] = pieces[k][...]
            grad_ref[...] = pieces[TEAM + k][...]

    width = hidden_ref.shape[1]
    values = forward_dot(normed_ref[...], pair_ref[...])
    gate_value, up_value = values[:, :width], values[:, width:]
    sigmoid = jax.nn.sigmoid(gate_value)
    silu = gate_value * sigmoid
    hidden_ref[...] = (silu * up_value).astype(bf16)
    silu_ref[...] = silu.astype(bf16)
    slope_ref[...] = (up_value * (sigmoid * (1 + gate_value * (1 - sigmoid)))).astype(bf16)


def backward_kernel(
    grad_ref,
    hidden_ref,
    silu_ref,
    slope_ref,
    pair_ref,
    down_ref,
    token_ref,
    pair_grad_ref,
    normed_ref,
    out_ref,
):
    del token_ref
    width = hidden_ref.shape[1]
    hidden_grad = back_dot(grad_ref[...], down_ref[...])
    pair_grad_ref[:, :width] = (hidden_grad * slope_ref[...].astype(f32)).astype(bf16)
    pair_grad_ref[:, width:] = (hidden_grad * silu_ref[...].astype(f32)).astype(bf16)
    normed_ref[...] = back_dot(pair_grad_ref[...], pair_ref[...]).astype(bf16)
    out_ref[...] = forward_dot(hidden_ref[...], down_ref[...]).astype(bf16)


def by_rows(kernel, tile, steps, rowed, whole, tokens, columns, flops, transcendentals):
    rows = steps * tile

    def row_block(count):
        return pl.BlockSpec((tile, count), lambda i: (i, 0))

    moved = sum(2 * value.size for value in rowed + whole) + 2 * rows * sum(columns)
    return pl.pallas_call(
        kernel,
        grid=(steps,),
        in_specs=[row_block(value.shape[1]) for value in rowed]
        + [
            pl.BlockSpec(value.shape, lambda i: (0, 0), pipeline_mode=pl.Buffered(1))
            for value in whole
        ]
        + [pl.BlockSpec(memory_space=pl.ANY)] * len(tokens),
        out_specs=[row_block(count) for count in columns],
        out_shape=[jax.ShapeDtypeStruct((rows, count), bf16) for count in columns],
        compiler_params=pltpu.CompilerParams(vmem_limit_bytes=52 * 1024 * 1024),
        cost_estimate=pl.CostEstimate(
            flops=flops, bytes_accessed=moved, transcendentals=transcendentals
        ),
    )(*rowed, *whole, *tokens)


def shifted_down(rows, step):
    return jnp.concatenate(
        [jnp.zeros((step, rows.shape[1]), rows.dtype), rows[:-step]], axis=0
    )


def shifted_up(rows, step):
    return jnp.concatenate(
        [rows[step:], jnp.zeros((step, rows.shape[1]), rows.dtype)], axis=0
    )


def inverse_rms(values):
    return lax.rsqrt(jnp.mean(values * values, axis=-1, keepdims=True) + EPSILON)


def norm_back(values, scale, weighted):
    return scale * weighted - values * (
        scale * scale * scale * jnp.mean(weighted * values, axis=-1, keepdims=True)
    )


def per_device(
    tokens,
    positions,
    cotangent,
    norm_gain,
    in_weight,
    conv_weight,
    out_weight,
    ffn_gain,
    gate_weight,
    up_weight,
    down_weight,
):
    shape = tokens.shape
    features = shape[2]
    rows = shape[0] * shape[1]
    share = in_weight.shape[0]
    hidden_share = down_weight.shape[0]
    hidden_width = gate_weight.shape[1]
    taps = conv_weight.shape[0]
    groups = lax.axis_size("g") * lax.axis_size("y")
    slots = lax.axis_size("s")
    chan_run = slots * share
    hid_run = slots * hidden_share
    chan = groups * chan_run
    hid = groups * hid_run

    def by_place(weight, parts, team, run):
        count = weight.shape[1] // (parts * team * run)
        split = weight.reshape(share, parts, count, team, run)
        return jnp.transpose(split, (3, 0, 1, 2, 4)).reshape(team, share, parts * count * run)

    def side_by_side(block, width):
        return jnp.concatenate(
            [block[..., j * share : (j + 1) * share, :width] for j in range(features // width)],
            axis=-1,
        )

    def stacked(block, width):
        return jnp.concatenate(
            [block[..., j * width : (j + 1) * width] for j in range(features // width)], axis=-2
        )

    in_blocks = by_place(in_weight, 3, TEAM, chan_run)
    in_mine = jnp.concatenate(exchange([in_blocks[j] for j in range(TEAM)]), axis=0)
    gains = jnp.concatenate([norm_gain, ffn_gain]).reshape(1, 2 * share)
    near_gains = team_rows(gains)
    gains_row = jnp.concatenate(reorder([near_gains[j : j + 1] for j in range(TEAM)]), axis=1)
    def as_row(values):
        return jnp.pad(values, ((0, 0), (0, features - values.shape[1])))

    first_pack = jnp.concatenate(
        [
            jnp.concatenate([in_mine, stacked(out_weight, chan)], axis=1),
            as_row(conv_weight.reshape(1, taps * share)),
            as_row(gains_row),
            jnp.zeros((EXTRA_ROWS - 2, features), bf16),
        ],
        axis=0,
    )
    tall = TEAM * share

    def first_unpack(block):
        return [
            block[:tall, : 3 * chan].reshape(TEAM, share, 3 * chan),
            side_by_side(block[:tall, 3 * chan :], chan),
            block[tall, : taps * share].reshape(taps, share),
            block[tall + 1, : 2 * tall].reshape(TEAM, 2, share),
        ]

    pair_blocks = jnp.concatenate(
        [by_place(gate_weight, 1, TEAM, hid_run), by_place(up_weight, 1, TEAM, hid_run)], axis=2
    )
    pair_mine = jnp.concatenate(exchange([pair_blocks[j] for j in range(TEAM)]), axis=0)

    first_all = lax.all_gather(first_pack, ("g", "y", "s"), axis=0, tiled=False)
    in_all, out_all, conv_all, gains_all = [
        part.reshape((groups, slots) + part.shape[1:]) for part in jax.vmap(first_unpack)(first_all)
    ]

    pair_all = lax.all_gather(pair_mine, ("g", "y", "s"), axis=0, tiled=False)
    down_full = lax.all_gather(down_weight, ("g", "y", "s"), axis=0, tiled=True)

    in_full = jnp.transpose(in_all, (0, 2, 1, 3, 4)).reshape(features, 3 * chan)
    out_full = out_all.reshape(chan, features)
    conv_full = jnp.transpose(conv_all, (2, 0, 1, 3)).reshape(taps, chan).astype(f32)
    gains_full = jnp.transpose(gains_all, (3, 0, 2, 1, 4)).reshape(2, features).astype(f32)
    norm_full, ffn_full = gains_full[0], gains_full[1]
    pair_full = jnp.transpose(
        pair_all.reshape(groups, slots, TEAM, share, 2 * hid), (0, 2, 1, 3, 4)
    ).reshape(features, 2 * hid)

    own_tokens = tokens.reshape(rows, features)
    places = positions.reshape(rows, 1)
    team_tokens = team_rows(own_tokens)
    team_places = team_rows(places)
    live = (places >= 0).astype(f32)
    upstream = cotangent.reshape(rows, features).astype(f32)
    ffn_pieces = team_pieces((live * upstream).astype(bf16))
    inputs = tokens.reshape(rows, features).astype(f32)

    values = team_tokens.astype(f32)
    early_full = after(norm_full, ffn_pieces[3][-1:])
    first_normed = (values * inverse_rms(values) * early_full).astype(bf16)
    projected = forward_dot(first_normed, in_full)
    b_part = projected[:, :chan]
    c_part = projected[:, chan : 2 * chan]
    x_part = projected[:, 2 * chan :]
    mixed = b_part * x_part
    mask_one = (team_places >= 1).astype(f32)
    mask_two = (team_places >= 2).astype(f32)
    mixed_one = mask_one * shifted_down(mixed, 1)
    mixed_two = mask_two * shifted_down(mixed, 2)
    convolved = conv_full[0] * mixed + conv_full[1] * mixed_one + conv_full[2] * mixed_two
    mixer_in = (c_part * convolved).astype(bf16)
    mixer_out = team_sum(forward_dot(mixer_in, out_full).astype(bf16))
    middle = inputs + live * mixer_out[0]
    second_scale = inverse_rms(middle)
    second_pieces = team_pieces((middle * second_scale * ffn_full).astype(bf16))

    team_count = TEAM * rows
    unit = 2 * team_count * features * hid
    hidden, silu, slope, second_normed, ffn_grad = by_rows(
        forward_kernel,
        rows,
        TEAM,
        [],
        second_pieces + ffn_pieces + [pair_full],
        [],
        [hid] * 3 + [features] * 2,
        2 * unit,
        team_count * hid,
    )
    down_part = rows_dot(hidden, ffn_grad).astype(bf16)
    pair_grad, normed_part, out_part = by_rows(
        backward_kernel,
        ROW_TILE,
        team_count // ROW_TILE,
        [ffn_grad, hidden, silu, slope],
        [pair_full, down_full],
        [down_part],
        [2 * hid, features, features],
        4 * unit,
        0,
    )

    def by_owner(grad, team):
        width = grad.shape[-1]
        count = features // (team * slots * share)
        split = grad.astype(bf16).reshape(count, team, slots, share, width)
        return jnp.transpose(split, (0, 2, 1, 3, 4)).reshape(count, slots, team * share, width)

    pair_part = by_owner(rows_dot(second_normed, pair_grad), TEAM)
    normed_sum, _ = team_sum(normed_part, pair_part[0, 0, :1])
    second_weighted = ffn_full * normed_sum
    middle_grad = upstream + norm_back(middle, second_scale, second_weighted)

    mixer_grad = team_rows((live * middle_grad).astype(bf16))
    mixer_in_grad = back_dot(mixer_grad, out_full)
    c_grad = mixer_in_grad * convolved
    conv_grad = mixer_in_grad * c_part
    mixed_grad = (
        conv_full[0] * conv_grad
        + conv_full[1] * shifted_up(mask_one * conv_grad, 1)
        + conv_full[2] * shifted_up(mask_two * conv_grad, 2)
    )
    projected_grad = jnp.concatenate(
        [mixed_grad * x_part, c_grad, mixed_grad * b_part], axis=1
    ).astype(bf16)
    grad_conv_part = jnp.stack(
        [
            jnp.sum(conv_grad * mixed, axis=0),
            jnp.sum(conv_grad * mixed_one, axis=0),
            jnp.sum(conv_grad * mixed_two, axis=0),
        ]
    )
    in_part = by_owner(rows_dot(first_normed, projected_grad), TEAM)
    out_grad_part = rows_dot(mixer_in, mixer_grad).astype(bf16)
    out_grad_part = stacked(out_grad_part.reshape(groups, slots, share, features), chan)
    conv_rows = jnp.transpose(
        grad_conv_part.reshape(taps, groups, slots, share), (1, 2, 0, 3)
    ).reshape(groups, slots, 1, taps * share)
    conv_rows = jnp.pad(
        conv_rows.astype(bf16),
        ((0, 0), (0, 0), (0, EXTRA_ROWS - 1), (0, features - taps * share)),
    )
    pair_sum = scatter_plain(pair_part)
    grad_down = scatter(
        down_part.reshape(groups, slots, hidden_share, features), pair_sum[:1]
    )
    first_weighted, first_sent = team_sum(back_dot(projected_grad, in_full).astype(bf16))
    input_grad = middle_grad + norm_back(inputs, inverse_rms(inputs), norm_full * first_weighted)
    input_grad = input_grad.astype(bf16)
    out_sum, _ = team_sum(after(out_part, mixer_grad[-1:]))
    block_out = (middle + live * out_sum).astype(bf16)
    first_sum = scatter(
        jnp.concatenate(
            [jnp.concatenate([in_part, out_grad_part], axis=3), conv_rows], axis=2
        ),
        pair_sum[:1],
        first_sent,
    )

    def own_rows(summed, parts, team, run):
        blocks = [summed[j * share : (j + 1) * share].astype(bf16) for j in range(team)]
        came = [block.reshape(share, parts, -1, 1, run) for block in exchange(blocks)]
        joined = jnp.concatenate(came, axis=3)
        return joined.reshape(share, -1).astype(f32)

    pair_rows = own_rows(pair_sum, 2, TEAM, hid_run)
    gate_rows = pair_rows[:, :hidden_width]
    up_rows = pair_rows[:, hidden_width:]
    in_rows = own_rows(first_sum[:tall, : 3 * chan], 3, TEAM, chan_run)
    grad_out = side_by_side(first_sum[:tall, 3 * chan :], chan).astype(f32)
    grad_conv = first_sum[tall, : taps * share].reshape(taps, share).astype(f32)
    grad_norm_gain = jnp.sum(in_weight.astype(f32) * in_rows, axis=1) / norm_gain.astype(f32)
    grad_ffn_gain = jnp.sum(
        gate_weight.astype(f32) * gate_rows + up_weight.astype(f32) * up_rows, axis=1
    ) / ffn_gain.astype(f32)
    return (
        block_out.reshape(shape),
        input_grad.reshape(shape),
        grad_norm_gain,
        in_rows,
        grad_conv,
        grad_out,
        grad_ffn_gain,
        gate_rows,
        up_rows,
        grad_down.astype(f32),
    )


def solution(mesh):
    every = ("g", "y", "x", "c", "s")
    outer = mesh.shape["dp"] // (2 * TEAM)
    teams = Mesh(mesh.devices.reshape(outer, 2, 2, 2, mesh.shape["shard"]), every)
    return jax.shard_map(
        per_device,
        mesh=teams,
        in_specs=(
            P(None, every, None),
            P(None, every),
            P(None, every, None),
            P(every),
            P(every, None),
            P(None, every),
            P(every, None),
            P(every),
            P(every, None),
            P(every, None),
            P(every, None),
        ),
        out_specs=(
            P(None, every, None),
            P(None, every, None),
            P(every),
            P(every, None),
            P(None, every),
            P(every, None),
            P(every),
            P(every, None),
            P(every, None),
            P(every, None),
        ),
        check_vma=False,
    )
```

```python
import jax
import jax.numpy as jnp
from jax import lax
from jax.experimental import pallas as pl
from jax.experimental.pallas import tpu as pltpu
from jax.sharding import Mesh, PartitionSpec as P

EPSILON = 1e-05
TEAM = 4
EXTRA_ROWS = 16
ROW_TILE = 512
bf16 = jnp.bfloat16
f32 = jnp.float32


def forward_dot(left_side, right_side):
    return jnp.dot(left_side, right_side, preferred_element_type=f32)


def rows_dot(left_side, right_side):
    return lax.dot_general(
        left_side, right_side, (((0,), (0,)), ((), ())), preferred_element_type=f32
    )


def back_dot(left_side, right_side):
    return lax.dot_general(
        left_side, right_side, (((1,), (1,)), ((), ())), preferred_element_type=f32
    )


def swap_core(values):
    return lax.ppermute(values, "c", [(0, 1), (1, 0)])


def swap_chip(values):
    return lax.ppermute(values, "x", [(0, 1), (1, 0)])


def swap_row(values):
    return lax.ppermute(values, "y", [(0, 1), (1, 0)])


def swap_far(values, distance):
    return lax.ppermute(values, ("x", "c"), [(i, i ^ distance) for i in range(TEAM)])


def after(values, token):
    return values + (token.ravel()[0] * 0).astype(values.dtype)


def reorder(blocks):
    blocks = list(blocks)
    for bit, axis in ((1, "c"), (2, "x")):
        odd = lax.axis_index(axis) == 1
        blocks = [jnp.where(odd, blocks[j ^ bit], blocks[j]) for j in range(len(blocks))]
    return blocks


def exchange(blocks):
    near = reorder(blocks)
    return reorder(near[:1] + [swap_far(near[j], j) for j in range(1, len(near))])


def team_pieces(rows):
    across = swap_chip(rows)
    return [rows, swap_core(rows), across, swap_core(across)]


def team_rows(rows):
    return jnp.concatenate(team_pieces(rows), axis=0)


def team_sum(terms, token=None):
    count = terms.shape[0] // TEAM
    sent = jnp.concatenate([terms[count : 2 * count], terms[3 * count :]], axis=0)
    came = swap_core(sent).astype(f32)
    own = terms[:count].astype(f32) + came[:count]
    other = terms[2 * count : 3 * count].astype(f32) + came[count:]
    other = other.astype(bf16)
    came = swap_chip(other).astype(f32)
    return own + (came if token is None else after(came, token)), other[:1, :1]


def take(blocks, index):
    return lax.dynamic_index_in_dim(blocks, index, axis=0, keepdims=False)


def scatter(part, *tokens):
    groups, slots = part.shape[:2]
    if groups == 2:
        row = lax.axis_index("y")
        came = swap_row(take(part, 1 - row)).astype(f32)
        for token in tokens:
            came = after(came, token)
        summed = (take(part, row).astype(f32) + came).astype(bf16)
        return lax.psum_scatter(summed, "s", scatter_dimension=0, tiled=False)
    flat = part.reshape((groups * slots,) + part.shape[2:]).astype(f32)
    return lax.psum_scatter(flat, ("g", "y", "s"), scatter_dimension=0, tiled=False)


def scatter_plain(part):
    groups, slots = part.shape[:2]
    flat = part.reshape((groups * slots,) + part.shape[2:])
    if groups > 2:
        flat = flat.astype(f32)
    return lax.psum_scatter(flat, ("g", "y", "s"), scatter_dimension=0, tiled=False)


def forward_kernel(*refs):
    pieces, pair_ref = refs[: 2 * TEAM], refs[2 * TEAM]
    hidden_ref, silu_ref, slope_ref, normed_ref, grad_ref = refs[2 * TEAM + 1 :]
    for k in range(TEAM):

        @pl.when(pl.program_id(0) == k)
        def _():
            normed_ref[...] = pieces[k][...]
            grad_ref[...] = pieces[TEAM + k][...]

    width = hidden_ref.shape[1]
    values = forward_dot(normed_ref[...], pair_ref[...])
    gate_value, up_value = values[:, :width], values[:, width:]
    sigmoid = jax.nn.sigmoid(gate_value)
    silu = gate_value * sigmoid
    hidden_ref[...] = (silu * up_value).astype(bf16)
    silu_ref[...] = silu.astype(bf16)
    slope_ref[...] = (up_value * (sigmoid * (1 + gate_value * (1 - sigmoid)))).astype(bf16)


def backward_kernel(
    grad_ref,
    hidden_ref,
    silu_ref,
    slope_ref,
    pair_ref,
    down_ref,
    token_ref,
    pair_grad_ref,
    normed_ref,
    out_ref,
):
    del token_ref
    width = hidden_ref.shape[1]
    hidden_grad = back_dot(grad_ref[...], down_ref[...])
    pair_grad_ref[:, :width] = (hidden_grad * slope_ref[...].astype(f32)).astype(bf16)
    pair_grad_ref[:, width:] = (hidden_grad * silu_ref[...].astype(f32)).astype(bf16)
    normed_ref[...] = back_dot(pair_grad_ref[...], pair_ref[...]).astype(bf16)
    out_ref[...] = forward_dot(hidden_ref[...], down_ref[...]).astype(bf16)


def by_rows(kernel, tile, steps, rowed, whole, tokens, columns, flops, transcendentals):
    rows = steps * tile

    def row_block(count):
        return pl.BlockSpec((tile, count), lambda i: (i, 0))

    moved = sum(2 * value.size for value in rowed + whole) + 2 * rows * sum(columns)
    return pl.pallas_call(
        kernel,
        grid=(steps,),
        in_specs=[row_block(value.shape[1]) for value in rowed]
        + [
            pl.BlockSpec(value.shape, lambda i: (0, 0), pipeline_mode=pl.Buffered(1))
            for value in whole
        ]
        + [pl.BlockSpec(memory_space=pl.ANY)] * len(tokens),
        out_specs=[row_block(count) for count in columns],
        out_shape=[jax.ShapeDtypeStruct((rows, count), bf16) for count in columns],
        compiler_params=pltpu.CompilerParams(vmem_limit_bytes=52 * 1024 * 1024),
        cost_estimate=pl.CostEstimate(
            flops=flops, bytes_accessed=moved, transcendentals=transcendentals
        ),
    )(*rowed, *whole, *tokens)


def shifted_down(rows, step):
    return jnp.concatenate(
        [jnp.zeros((step, rows.shape[1]), rows.dtype), rows[:-step]], axis=0
    )


def shifted_up(rows, step):
    return jnp.concatenate(
        [rows[step:], jnp.zeros((step, rows.shape[1]), rows.dtype)], axis=0
    )


def inverse_rms(values):
    return lax.rsqrt(jnp.mean(values * values, axis=-1, keepdims=True) + EPSILON)


def norm_back(values, scale, weighted):
    return scale * weighted - values * (
        scale * scale * scale * jnp.mean(weighted * values, axis=-1, keepdims=True)
    )


def per_device(
    tokens,
    positions,
    cotangent,
    norm_gain,
    in_weight,
    conv_weight,
    out_weight,
    ffn_gain,
    gate_weight,
    up_weight,
    down_weight,
):
    shape = tokens.shape
    features = shape[2]
    rows = shape[0] * shape[1]
    share = in_weight.shape[0]
    hidden_share = down_weight.shape[0]
    hidden_width = gate_weight.shape[1]
    taps = conv_weight.shape[0]
    groups = lax.axis_size("g") * lax.axis_size("y")
    slots = lax.axis_size("s")
    chan_run = slots * share
    hid_run = slots * hidden_share
    chan = groups * chan_run
    hid = groups * hid_run

    def by_place(weight, parts, team, run):
        count = weight.shape[1] // (parts * team * run)
        split = weight.reshape(share, parts, count, team, run)
        return jnp.transpose(split, (3, 0, 1, 2, 4)).reshape(team, share, parts * count * run)

    def side_by_side(block, width):
        return jnp.concatenate(
            [block[..., j * share : (j + 1) * share, :width] for j in range(features // width)],
            axis=-1,
        )

    def stacked(block, width):
        return jnp.concatenate(
            [block[..., j * width : (j + 1) * width] for j in range(features // width)], axis=-2
        )

    in_blocks = by_place(in_weight, 3, TEAM, chan_run)
    in_mine = jnp.concatenate(exchange([in_blocks[j] for j in range(TEAM)]), axis=0)
    gains = jnp.concatenate([norm_gain, ffn_gain]).reshape(1, 2 * share)
    near_gains = team_rows(gains)
    gains_row = jnp.concatenate(reorder([near_gains[j : j + 1] for j in range(TEAM)]), axis=1)
    def as_row(values):
        return jnp.pad(values, ((0, 0), (0, features - values.shape[1])))

    first_pack = jnp.concatenate(
        [
            jnp.concatenate([in_mine, stacked(out_weight, chan)], axis=1),
            as_row(conv_weight.reshape(1, taps * share)),
            as_row(gains_row),
            jnp.zeros((EXTRA_ROWS - 2, features), bf16),
        ],
        axis=0,
    )
    tall = TEAM * share

    def first_unpack(block):
        return [
            block[:tall, : 3 * chan].reshape(TEAM, share, 3 * chan),
            side_by_side(block[:tall, 3 * chan :], chan),
            block[tall, : taps * share].reshape(taps, share),
            block[tall + 1, : 2 * tall].reshape(TEAM, 2, share),
        ]

    pair_blocks = jnp.concatenate(
        [by_place(gate_weight, 1, TEAM, hid_run), by_place(up_weight, 1, TEAM, hid_run)], axis=2
    )
    pair_mine = jnp.concatenate(exchange([pair_blocks[j] for j in range(TEAM)]), axis=0)

    first_all = lax.all_gather(first_pack, ("g", "y", "s"), axis=0, tiled=False)
    in_all, out_all, conv_all, gains_all = [
        part.reshape((groups, slots) + part.shape[1:]) for part in jax.vmap(first_unpack)(first_all)
    ]

    pair_all = lax.all_gather(pair_mine, ("g", "y", "s"), axis=0, tiled=False)
    down_full = lax.all_gather(down_weight, ("g", "y", "s"), axis=0, tiled=True)

    in_full = jnp.transpose(in_all, (0, 2, 1, 3, 4)).reshape(features, 3 * chan)
    out_full = out_all.reshape(chan, features)
    conv_full = jnp.transpose(conv_all, (2, 0, 1, 3)).reshape(taps, chan).astype(f32)
    gains_full = jnp.transpose(gains_all, (3, 0, 2, 1, 4)).reshape(2, features).astype(f32)
    norm_full, ffn_full = gains_full[0], gains_full[1]
    pair_full = jnp.transpose(
        pair_all.reshape(groups, slots, TEAM, share, 2 * hid), (0, 2, 1, 3, 4)
    ).reshape(features, 2 * hid)

    own_tokens = tokens.reshape(rows, features)
    places = positions.reshape(rows, 1)
    team_tokens = team_rows(own_tokens)
    team_places = team_rows(places)
    live = (places >= 0).astype(f32)
    upstream = cotangent.reshape(rows, features).astype(f32)
    ffn_pieces = team_pieces((live * upstream).astype(bf16))
    inputs = tokens.reshape(rows, features).astype(f32)

    values = team_tokens.astype(f32)
    early_full = after(norm_full, ffn_pieces[3][-1:])
    first_normed = (values * inverse_rms(values) * early_full).astype(bf16)
    projected = forward_dot(first_normed, in_full)
    b_part = projected[:, :chan]
    c_part = projected[:, chan : 2 * chan]
    x_part = projected[:, 2 * chan :]
    mixed = b_part * x_part
    mask_one = (team_places >= 1).astype(f32)
    mask_two = (team_places >= 2).astype(f32)
    mixed_one = mask_one * shifted_down(mixed, 1)
    mixed_two = mask_two * shifted_down(mixed, 2)
    convolved = conv_full[0] * mixed + conv_full[1] * mixed_one + conv_full[2] * mixed_two
    mixer_in = (c_part * convolved).astype(bf16)
    mixer_out = team_sum(forward_dot(mixer_in, out_full).astype(bf16))
    middle = inputs + live * mixer_out[0]
    second_scale = inverse_rms(middle)
    second_pieces = team_pieces((middle * second_scale * ffn_full).astype(bf16))

    team_count = TEAM * rows
    unit = 2 * team_count * features * hid
    hidden, silu, slope, second_normed, ffn_grad = by_rows(
        forward_kernel,
        rows,
        TEAM,
        [],
        second_pieces + ffn_pieces + [pair_full],
        [],
        [hid] * 3 + [features] * 2,
        2 * unit,
        team_count * hid,
    )
    down_part = rows_dot(hidden, ffn_grad).astype(bf16)
    grad_down = scatter(down_part.reshape(groups, slots, hidden_share, features))
    pair_grad, normed_part, out_part = by_rows(
        backward_kernel,
        ROW_TILE,
        team_count // ROW_TILE,
        [ffn_grad, hidden, silu, slope],
        [pair_full, down_full],
        [down_part],
        [2 * hid, features, features],
        4 * unit,
        0,
    )

    def by_owner(grad, team):
        width = grad.shape[-1]
        count = features // (team * slots * share)
        split = grad.astype(bf16).reshape(count, team, slots, share, width)
        return jnp.transpose(split, (0, 2, 1, 3, 4)).reshape(count, slots, team * share, width)

    pair_part = by_owner(rows_dot(second_normed, pair_grad), TEAM)
    normed_sum, _ = team_sum(normed_part, pair_part[0, 0, :1])
    second_weighted = ffn_full * normed_sum
    middle_grad = upstream + norm_back(middle, second_scale, second_weighted)

    mixer_grad = team_rows((live * middle_grad).astype(bf16))
    mixer_in_grad = back_dot(mixer_grad, out_full)
    c_grad = mixer_in_grad * convolved
    conv_grad = mixer_in_grad * c_part
    conv_back = after(conv_full, grad_down[:1])
    mixed_grad = (
        conv_back[0] * conv_grad
        + conv_back[1] * shifted_up(mask_one * conv_grad, 1)
        + conv_back[2] * shifted_up(mask_two * conv_grad, 2)
    )
    projected_grad = jnp.concatenate(
        [mixed_grad * x_part, c_grad, mixed_grad * b_part], axis=1
    ).astype(bf16)
    grad_conv_part = jnp.stack(
        [
            jnp.sum(conv_grad * mixed, axis=0),
            jnp.sum(conv_grad * mixed_one, axis=0),
            jnp.sum(conv_grad * mixed_two, axis=0),
        ]
    )
    in_part = by_owner(rows_dot(first_normed, projected_grad), TEAM)
    out_grad_part = rows_dot(mixer_in, mixer_grad).astype(bf16)
    out_grad_part = stacked(out_grad_part.reshape(groups, slots, share, features), chan)
    conv_rows = jnp.transpose(
        grad_conv_part.reshape(taps, groups, slots, share), (1, 2, 0, 3)
    ).reshape(groups, slots, 1, taps * share)
    conv_rows = jnp.pad(
        conv_rows.astype(bf16),
        ((0, 0), (0, 0), (0, EXTRA_ROWS - 1), (0, features - taps * share)),
    )
    pair_sum = scatter_plain(pair_part)
    first_weighted, first_sent = team_sum(back_dot(projected_grad, in_full).astype(bf16))
    input_grad = middle_grad + norm_back(inputs, inverse_rms(inputs), norm_full * first_weighted)
    input_grad = input_grad.astype(bf16)
    out_sum, _ = team_sum(after(out_part, mixer_grad[-1:]))
    block_out = (middle + live * out_sum).astype(bf16)
    first_sum = scatter(
        jnp.concatenate(
            [jnp.concatenate([in_part, out_grad_part], axis=3), conv_rows], axis=2
        ),
        pair_sum[:1],
        first_sent,
    )

    def own_rows(summed, parts, team, run):
        blocks = [summed[j * share : (j + 1) * share].astype(bf16) for j in range(team)]
        came = [block.reshape(share, parts, -1, 1, run) for block in exchange(blocks)]
        joined = jnp.concatenate(came, axis=3)
        return joined.reshape(share, -1).astype(f32)

    pair_rows = own_rows(pair_sum, 2, TEAM, hid_run)
    gate_rows = pair_rows[:, :hidden_width]
    up_rows = pair_rows[:, hidden_width:]
    in_rows = own_rows(first_sum[:tall, : 3 * chan], 3, TEAM, chan_run)
    grad_out = side_by_side(first_sum[:tall, 3 * chan :], chan).astype(f32)
    grad_conv = first_sum[tall, : taps * share].reshape(taps, share).astype(f32)
    grad_norm_gain = jnp.sum(in_weight.astype(f32) * in_rows, axis=1) / norm_gain.astype(f32)
    grad_ffn_gain = jnp.sum(
        gate_weight.astype(f32) * gate_rows + up_weight.astype(f32) * up_rows, axis=1
    ) / ffn_gain.astype(f32)
    return (
        block_out.reshape(shape),
        input_grad.reshape(shape),
        grad_norm_gain,
        in_rows,
        grad_conv,
        grad_out,
        grad_ffn_gain,
        gate_rows,
        up_rows,
        grad_down.astype(f32),
    )


def solution(mesh):
    every = ("g", "y", "x", "c", "s")
    outer = mesh.shape["dp"] // (2 * TEAM)
    teams = Mesh(mesh.devices.reshape(outer, 2, 2, 2, mesh.shape["shard"]), every)
    return jax.shard_map(
        per_device,
        mesh=teams,
        in_specs=(
            P(None, every, None),
            P(None, every),
            P(None, every, None),
            P(every),
            P(every, None),
            P(None, every),
            P(every, None),
            P(every),
            P(every, None),
            P(every, None),
            P(every, None),
        ),
        out_specs=(
            P(None, every, None),
            P(None, every, None),
            P(every),
            P(every, None),
            P(None, every),
            P(every, None),
            P(every),
            P(every, None),
            P(every, None),
            P(every, None),
        ),
        check_vma=False,
    )
```

```python
import jax
import jax.numpy as jnp
from jax import lax
from jax.experimental import pallas as pl
from jax.experimental.pallas import tpu as pltpu
from jax.sharding import Mesh, PartitionSpec as P

EPSILON = 1e-05
TEAM = 4
EXTRA_ROWS = 16
ROW_TILE = 512
bf16 = jnp.bfloat16
f32 = jnp.float32


def forward_dot(left_side, right_side):
    return jnp.dot(left_side, right_side, preferred_element_type=f32)


def rows_dot(left_side, right_side):
    return lax.dot_general(
        left_side, right_side, (((0,), (0,)), ((), ())), preferred_element_type=f32
    )


def back_dot(left_side, right_side):
    return lax.dot_general(
        left_side, right_side, (((1,), (1,)), ((), ())), preferred_element_type=f32
    )


def swap_core(values):
    return lax.ppermute(values, "c", [(0, 1), (1, 0)])


def swap_chip(values):
    return lax.ppermute(values, "x", [(0, 1), (1, 0)])


def swap_row(values):
    return lax.ppermute(values, "y", [(0, 1), (1, 0)])


def swap_far(values, distance):
    return lax.ppermute(values, ("x", "c"), [(i, i ^ distance) for i in range(TEAM)])


def after(values, token):
    return values + (token.ravel()[0] * 0).astype(values.dtype)


def reorder(blocks):
    blocks = list(blocks)
    for bit, axis in ((1, "c"), (2, "x")):
        odd = lax.axis_index(axis) == 1
        blocks = [jnp.where(odd, blocks[j ^ bit], blocks[j]) for j in range(len(blocks))]
    return blocks


def exchange(blocks):
    near = reorder(blocks)
    return reorder(near[:1] + [swap_far(near[j], j) for j in range(1, len(near))])


def team_pieces(rows):
    across = swap_chip(rows)
    return [rows, swap_core(rows), across, swap_core(across)]


def team_rows(rows):
    return jnp.concatenate(team_pieces(rows), axis=0)


def team_sum(terms, token=None):
    count = terms.shape[0] // TEAM
    sent = jnp.concatenate([terms[count : 2 * count], terms[3 * count :]], axis=0)
    came = swap_core(sent).astype(f32)
    own = terms[:count].astype(f32) + came[:count]
    other = terms[2 * count : 3 * count].astype(f32) + came[count:]
    other = other.astype(bf16)
    came = swap_chip(other).astype(f32)
    return own + (came if token is None else after(came, token)), other[:1, :1]


def take(blocks, index):
    return lax.dynamic_index_in_dim(blocks, index, axis=0, keepdims=False)


def scatter(part, *tokens):
    groups, slots = part.shape[:2]
    if groups == 2:
        row = lax.axis_index("y")
        came = swap_row(take(part, 1 - row)).astype(f32)
        for token in tokens:
            came = after(came, token)
        summed = (take(part, row).astype(f32) + came).astype(bf16)
        return lax.psum_scatter(summed, "s", scatter_dimension=0, tiled=False)
    flat = part.reshape((groups * slots,) + part.shape[2:]).astype(f32)
    return lax.psum_scatter(flat, ("g", "y", "s"), scatter_dimension=0, tiled=False)


def forward_kernel(*refs):
    pieces, pair_ref = refs[: 2 * TEAM], refs[2 * TEAM]
    hidden_ref, silu_ref, slope_ref, normed_ref, grad_ref = refs[2 * TEAM + 1 :]
    for k in range(TEAM):

        @pl.when(pl.program_id(0) == k)
        def _():
            normed_ref[...] = pieces[k][...]
            grad_ref[...] = pieces[TEAM + k][...]

    width = hidden_ref.shape[1]
    values = forward_dot(normed_ref[...], pair_ref[...])
    gate_value, up_value = values[:, :width], values[:, width:]
    sigmoid = jax.nn.sigmoid(gate_value)
    silu = gate_value * sigmoid
    hidden_ref[...] = (silu * up_value).astype(bf16)
    silu_ref[...] = silu.astype(bf16)
    slope_ref[...] = (up_value * (sigmoid * (1 + gate_value * (1 - sigmoid)))).astype(bf16)


def backward_kernel(
    grad_ref, silu_ref, slope_ref, pair_ref, down_ref, token_ref, pair_grad_ref, normed_ref
):
    del token_ref
    width = silu_ref.shape[1]
    hidden_grad = back_dot(grad_ref[...], down_ref[...])
    pair_grad_ref[:, :width] = (hidden_grad * slope_ref[...].astype(f32)).astype(bf16)
    pair_grad_ref[:, width:] = (hidden_grad * silu_ref[...].astype(f32)).astype(bf16)
    normed_ref[...] = back_dot(pair_grad_ref[...], pair_ref[...]).astype(bf16)


def by_rows(kernel, tile, steps, rowed, whole, tokens, columns, flops, transcendentals):
    rows = steps * tile

    def row_block(count):
        return pl.BlockSpec((tile, count), lambda i: (i, 0))

    moved = sum(2 * value.size for value in rowed + whole) + 2 * rows * sum(columns)
    return pl.pallas_call(
        kernel,
        grid=(steps,),
        in_specs=[row_block(value.shape[1]) for value in rowed]
        + [
            pl.BlockSpec(value.shape, lambda i: (0, 0), pipeline_mode=pl.Buffered(1))
            for value in whole
        ]
        + [pl.BlockSpec(memory_space=pl.ANY)] * len(tokens),
        out_specs=[row_block(count) for count in columns],
        out_shape=[jax.ShapeDtypeStruct((rows, count), bf16) for count in columns],
        compiler_params=pltpu.CompilerParams(vmem_limit_bytes=52 * 1024 * 1024),
        cost_estimate=pl.CostEstimate(
            flops=flops, bytes_accessed=moved, transcendentals=transcendentals
        ),
    )(*rowed, *whole, *tokens)


def shifted_down(rows, step):
    return jnp.concatenate(
        [jnp.zeros((step, rows.shape[1]), rows.dtype), rows[:-step]], axis=0
    )


def shifted_up(rows, step):
    return jnp.concatenate(
        [rows[step:], jnp.zeros((step, rows.shape[1]), rows.dtype)], axis=0
    )


def inverse_rms(values):
    return lax.rsqrt(jnp.mean(values * values, axis=-1, keepdims=True) + EPSILON)


def norm_back(values, scale, weighted):
    return scale * weighted - values * (
        scale * scale * scale * jnp.mean(weighted * values, axis=-1, keepdims=True)
    )


def per_device(
    tokens,
    positions,
    cotangent,
    norm_gain,
    in_weight,
    conv_weight,
    out_weight,
    ffn_gain,
    gate_weight,
    up_weight,
    down_weight,
):
    shape = tokens.shape
    features = shape[2]
    rows = shape[0] * shape[1]
    share = in_weight.shape[0]
    hidden_share = down_weight.shape[0]
    hidden_width = gate_weight.shape[1]
    taps = conv_weight.shape[0]
    groups = lax.axis_size("g") * lax.axis_size("y")
    slots = lax.axis_size("s")
    chan_run = slots * share
    hid_run = slots * hidden_share
    chan = groups * chan_run
    hid = groups * hid_run

    def by_place(weight, parts, team, run):
        count = weight.shape[1] // (parts * team * run)
        split = weight.reshape(share, parts, count, team, run)
        return jnp.transpose(split, (3, 0, 1, 2, 4)).reshape(team, share, parts * count * run)

    def side_by_side(block, width):
        return jnp.concatenate(
            [block[..., j * share : (j + 1) * share, :width] for j in range(features // width)],
            axis=-1,
        )

    def stacked(block, width):
        return jnp.concatenate(
            [block[..., j * width : (j + 1) * width] for j in range(features // width)], axis=-2
        )

    in_blocks = by_place(in_weight, 3, TEAM, chan_run)
    in_mine = jnp.concatenate(exchange([in_blocks[j] for j in range(TEAM)]), axis=0)
    gains = jnp.concatenate([norm_gain, ffn_gain]).reshape(1, 2 * share)
    near_gains = team_rows(gains)
    gains_row = jnp.concatenate(reorder([near_gains[j : j + 1] for j in range(TEAM)]), axis=1)
    def as_row(values):
        return jnp.pad(values, ((0, 0), (0, features - values.shape[1])))

    first_pack = jnp.concatenate(
        [
            jnp.concatenate([in_mine, stacked(out_weight, chan)], axis=1),
            as_row(conv_weight.reshape(1, taps * share)),
            as_row(gains_row),
            jnp.zeros((EXTRA_ROWS - 2, features), bf16),
        ],
        axis=0,
    )
    tall = TEAM * share

    def first_unpack(block):
        return [
            block[:tall, : 3 * chan].reshape(TEAM, share, 3 * chan),
            side_by_side(block[:tall, 3 * chan :], chan),
            block[tall, : taps * share].reshape(taps, share),
            block[tall + 1, : 2 * tall].reshape(TEAM, 2, share),
        ]

    pair_blocks = jnp.concatenate(
        [by_place(gate_weight, 1, TEAM, hid_run), by_place(up_weight, 1, TEAM, hid_run)], axis=2
    )
    pair_mine = jnp.concatenate(exchange([pair_blocks[j] for j in range(TEAM)]), axis=0)

    first_all = lax.all_gather(first_pack, ("g", "y", "s"), axis=0, tiled=False)
    in_all, out_all, conv_all, gains_all = [
        part.reshape((groups, slots) + part.shape[1:]) for part in jax.vmap(first_unpack)(first_all)
    ]

    pair_all = lax.all_gather(pair_mine, ("g", "y", "s"), axis=0, tiled=False)
    down_full = lax.all_gather(down_weight, ("g", "y", "s"), axis=0, tiled=True)

    in_full = jnp.transpose(in_all, (0, 2, 1, 3, 4)).reshape(features, 3 * chan)
    out_full = out_all.reshape(chan, features)
    conv_full = jnp.transpose(conv_all, (2, 0, 1, 3)).reshape(taps, chan).astype(f32)
    gains_full = jnp.transpose(gains_all, (3, 0, 2, 1, 4)).reshape(2, features).astype(f32)
    norm_full, ffn_full = gains_full[0], gains_full[1]
    pair_full = jnp.transpose(
        pair_all.reshape(groups, slots, TEAM, share, 2 * hid), (0, 2, 1, 3, 4)
    ).reshape(features, 2 * hid)

    own_tokens = tokens.reshape(rows, features)
    places = positions.reshape(rows, 1)
    team_tokens = team_rows(own_tokens)
    team_places = team_rows(places)
    live = (places >= 0).astype(f32)
    upstream = cotangent.reshape(rows, features).astype(f32)
    ffn_pieces = team_pieces((live * upstream).astype(bf16))
    inputs = tokens.reshape(rows, features).astype(f32)

    values = team_tokens.astype(f32)
    early_full = after(norm_full, ffn_pieces[3][-1:])
    first_normed = (values * inverse_rms(values) * early_full).astype(bf16)
    projected = forward_dot(first_normed, in_full)
    b_part = projected[:, :chan]
    c_part = projected[:, chan : 2 * chan]
    x_part = projected[:, 2 * chan :]
    mixed = b_part * x_part
    mask_one = (team_places >= 1).astype(f32)
    mask_two = (team_places >= 2).astype(f32)
    mixed_one = mask_one * shifted_down(mixed, 1)
    mixed_two = mask_two * shifted_down(mixed, 2)
    convolved = conv_full[0] * mixed + conv_full[1] * mixed_one + conv_full[2] * mixed_two
    mixer_in = (c_part * convolved).astype(bf16)
    mixer_out = team_sum(forward_dot(mixer_in, out_full).astype(bf16))
    middle = inputs + live * mixer_out[0]
    second_scale = inverse_rms(middle)
    second_pieces = team_pieces((middle * second_scale * ffn_full).astype(bf16))

    team_count = TEAM * rows
    unit = 2 * team_count * features * hid
    hidden, silu, slope, second_normed, ffn_grad = by_rows(
        forward_kernel,
        rows,
        TEAM,
        [],
        second_pieces + ffn_pieces + [pair_full],
        [],
        [hid] * 3 + [features] * 2,
        2 * unit,
        team_count * hid,
    )
    down_part = rows_dot(hidden, ffn_grad).astype(bf16)
    grad_down = scatter(down_part.reshape(groups, slots, hidden_share, features))
    pair_grad, normed_part = by_rows(
        backward_kernel,
        ROW_TILE,
        team_count // ROW_TILE,
        [ffn_grad, silu, slope],
        [pair_full, down_full],
        [down_part],
        [2 * hid, features],
        3 * unit,
        0,
    )

    def by_owner(grad, team):
        width = grad.shape[-1]
        count = features // (team * slots * share)
        split = grad.astype(bf16).reshape(count, team, slots, share, width)
        return jnp.transpose(split, (0, 2, 1, 3, 4)).reshape(count, slots, team * share, width)

    pair_part = by_owner(rows_dot(second_normed, pair_grad), TEAM)
    normed_sum, _ = team_sum(normed_part, pair_part[0, 0, :1])
    second_weighted = ffn_full * normed_sum
    middle_grad = upstream + norm_back(middle, second_scale, second_weighted)

    mixer_grad = team_rows((live * middle_grad).astype(bf16))
    mixer_in_grad = back_dot(mixer_grad, out_full)
    c_grad = mixer_in_grad * convolved
    conv_grad = mixer_in_grad * c_part
    conv_back = after(conv_full, grad_down[:1])
    mixed_grad = (
        conv_back[0] * conv_grad
        + conv_back[1] * shifted_up(mask_one * conv_grad, 1)
        + conv_back[2] * shifted_up(mask_two * conv_grad, 2)
    )
    projected_grad = jnp.concatenate(
        [mixed_grad * x_part, c_grad, mixed_grad * b_part], axis=1
    ).astype(bf16)
    grad_conv_part = jnp.stack(
        [
            jnp.sum(conv_grad * mixed, axis=0),
            jnp.sum(conv_grad * mixed_one, axis=0),
            jnp.sum(conv_grad * mixed_two, axis=0),
        ]
    )
    in_part = by_owner(rows_dot(first_normed, projected_grad), TEAM)
    out_grad_part = rows_dot(mixer_in, mixer_grad).astype(bf16)
    out_grad_part = stacked(out_grad_part.reshape(groups, slots, share, features), chan)
    conv_rows = jnp.transpose(
        grad_conv_part.reshape(taps, groups, slots, share), (1, 2, 0, 3)
    ).reshape(groups, slots, 1, taps * share)
    conv_rows = jnp.pad(
        conv_rows.astype(bf16),
        ((0, 0), (0, 0), (0, EXTRA_ROWS - 1), (0, features - taps * share)),
    )
    pair_sum = scatter(pair_part)
    first_weighted, first_sent = team_sum(back_dot(projected_grad, in_full).astype(bf16))
    input_grad = middle_grad + norm_back(inputs, inverse_rms(inputs), norm_full * first_weighted)
    input_grad = input_grad.astype(bf16)
    out_part = forward_dot(hidden, down_full).astype(bf16)
    out_sum, _ = team_sum(after(out_part, mixer_grad[-1:]))
    block_out = (middle + live * out_sum).astype(bf16)
    first_sum = scatter(
        jnp.concatenate(
            [jnp.concatenate([in_part, out_grad_part], axis=3), conv_rows], axis=2
        ),
        pair_sum[:1],
        first_sent,
    )

    def own_rows(summed, parts, team, run):
        blocks = [summed[j * share : (j + 1) * share].astype(bf16) for j in range(team)]
        came = [block.reshape(share, parts, -1, 1, run) for block in exchange(blocks)]
        joined = jnp.concatenate(came, axis=3)
        return joined.reshape(share, -1).astype(f32)

    pair_rows = own_rows(pair_sum, 2, TEAM, hid_run)
    gate_rows = pair_rows[:, :hidden_width]
    up_rows = pair_rows[:, hidden_width:]
    in_rows = own_rows(first_sum[:tall, : 3 * chan], 3, TEAM, chan_run)
    grad_out = side_by_side(first_sum[:tall, 3 * chan :], chan).astype(f32)
    grad_conv = first_sum[tall, : taps * share].reshape(taps, share).astype(f32)
    grad_norm_gain = jnp.sum(in_weight.astype(f32) * in_rows, axis=1) / norm_gain.astype(f32)
    grad_ffn_gain = jnp.sum(
        gate_weight.astype(f32) * gate_rows + up_weight.astype(f32) * up_rows, axis=1
    ) / ffn_gain.astype(f32)
    return (
        block_out.reshape(shape),
        input_grad.reshape(shape),
        grad_norm_gain,
        in_rows,
        grad_conv,
        grad_out,
        grad_ffn_gain,
        gate_rows,
        up_rows,
        grad_down.astype(f32),
    )


def solution(mesh):
    every = ("g", "y", "x", "c", "s")
    outer = mesh.shape["dp"] // (2 * TEAM)
    teams = Mesh(mesh.devices.reshape(outer, 2, 2, 2, mesh.shape["shard"]), every)
    return jax.shard_map(
        per_device,
        mesh=teams,
        in_specs=(
            P(None, every, None),
            P(None, every),
            P(None, every, None),
            P(every),
            P(every, None),
            P(None, every),
            P(every, None),
            P(every),
            P(every, None),
            P(every, None),
            P(every, None),
        ),
        out_specs=(
            P(None, every, None),
            P(None, every, None),
            P(every),
            P(every, None),
            P(None, every),
            P(every, None),
            P(every),
            P(every, None),
            P(every, None),
            P(every, None),
        ),
        check_vma=False,
    )
```

```python
import jax
import jax.numpy as jnp
from jax import lax
from jax.experimental import pallas as pl
from jax.experimental.pallas import tpu as pltpu
from jax.sharding import Mesh, PartitionSpec as P

EPSILON = 1e-05
TEAM = 4
EXTRA_ROWS = 16
ROW_TILE = 512
bf16 = jnp.bfloat16
f32 = jnp.float32


def forward_dot(left_side, right_side):
    return jnp.dot(left_side, right_side, preferred_element_type=f32)


def rows_dot(left_side, right_side):
    return lax.dot_general(
        left_side, right_side, (((0,), (0,)), ((), ())), preferred_element_type=f32
    )


def back_dot(left_side, right_side):
    return lax.dot_general(
        left_side, right_side, (((1,), (1,)), ((), ())), preferred_element_type=f32
    )


def swap_core(values):
    return lax.ppermute(values, "c", [(0, 1), (1, 0)])


def swap_chip(values):
    return lax.ppermute(values, "x", [(0, 1), (1, 0)])


def swap_row(values):
    return lax.ppermute(values, "y", [(0, 1), (1, 0)])


def swap_far(values, distance):
    return lax.ppermute(values, ("x", "c"), [(i, i ^ distance) for i in range(TEAM)])


def after(values, token):
    return values + (token.ravel()[0] * 0).astype(values.dtype)


def reorder(blocks):
    blocks = list(blocks)
    for bit, axis in ((1, "c"), (2, "x")):
        odd = lax.axis_index(axis) == 1
        blocks = [jnp.where(odd, blocks[j ^ bit], blocks[j]) for j in range(len(blocks))]
    return blocks


def exchange(blocks):
    near = reorder(blocks)
    return reorder(near[:1] + [swap_far(near[j], j) for j in range(1, len(near))])


def team_pieces(rows):
    across = swap_chip(rows)
    return [rows, swap_core(rows), across, swap_core(across)]


def team_rows(rows):
    return jnp.concatenate(team_pieces(rows), axis=0)


def team_sum(terms, token=None):
    count = terms.shape[0] // TEAM
    sent = jnp.concatenate([terms[count : 2 * count], terms[3 * count :]], axis=0)
    came = swap_core(sent).astype(f32)
    own = terms[:count].astype(f32) + came[:count]
    other = terms[2 * count : 3 * count].astype(f32) + came[count:]
    other = other.astype(bf16)
    came = swap_chip(other).astype(f32)
    return own + (came if token is None else after(came, token)), other[:1, :1]


def take(blocks, index):
    return lax.dynamic_index_in_dim(blocks, index, axis=0, keepdims=False)


def scatter(part, *tokens):
    groups, slots = part.shape[:2]
    if groups == 2:
        row = lax.axis_index("y")
        came = swap_row(take(part, 1 - row)).astype(f32)
        for token in tokens:
            came = after(came, token)
        summed = (take(part, row).astype(f32) + came).astype(bf16)
        return lax.psum_scatter(summed, "s", scatter_dimension=0, tiled=False)
    flat = part.reshape((groups * slots,) + part.shape[2:]).astype(f32)
    return lax.psum_scatter(flat, ("g", "y", "s"), scatter_dimension=0, tiled=False)


def forward_kernel(*refs):
    pieces, pair_ref = refs[: 2 * TEAM], refs[2 * TEAM]
    hidden_ref, silu_ref, slope_ref, normed_ref, grad_ref = refs[2 * TEAM + 1 :]
    for k in range(TEAM):

        @pl.when(pl.program_id(0) == k)
        def _():
            normed_ref[...] = pieces[k][...]
            grad_ref[...] = pieces[TEAM + k][...]

    width = hidden_ref.shape[1]
    values = forward_dot(normed_ref[...], pair_ref[...])
    gate_value, up_value = values[:, :width], values[:, width:]
    sigmoid = jax.nn.sigmoid(gate_value)
    silu = gate_value * sigmoid
    hidden_ref[...] = (silu * up_value).astype(bf16)
    silu_ref[...] = silu.astype(bf16)
    slope_ref[...] = (up_value * (sigmoid * (1 + gate_value * (1 - sigmoid)))).astype(bf16)


def backward_kernel(
    grad_ref, silu_ref, slope_ref, pair_ref, down_ref, token_ref, pair_grad_ref, normed_ref
):
    del token_ref
    width = silu_ref.shape[1]
    hidden_grad = back_dot(grad_ref[...], down_ref[...])
    pair_grad_ref[:, :width] = (hidden_grad * slope_ref[...].astype(f32)).astype(bf16)
    pair_grad_ref[:, width:] = (hidden_grad * silu_ref[...].astype(f32)).astype(bf16)
    normed_ref[...] = back_dot(pair_grad_ref[...], pair_ref[...]).astype(bf16)


def by_rows(kernel, tile, steps, rowed, whole, tokens, columns, flops, transcendentals):
    rows = steps * tile

    def row_block(count):
        return pl.BlockSpec((tile, count), lambda i: (i, 0))

    moved = sum(2 * value.size for value in rowed + whole) + 2 * rows * sum(columns)
    return pl.pallas_call(
        kernel,
        grid=(steps,),
        in_specs=[row_block(value.shape[1]) for value in rowed]
        + [
            pl.BlockSpec(value.shape, lambda i: (0, 0), pipeline_mode=pl.Buffered(1))
            for value in whole
        ]
        + [pl.BlockSpec(memory_space=pl.ANY)] * len(tokens),
        out_specs=[row_block(count) for count in columns],
        out_shape=[jax.ShapeDtypeStruct((rows, count), bf16) for count in columns],
        compiler_params=pltpu.CompilerParams(vmem_limit_bytes=52 * 1024 * 1024),
        cost_estimate=pl.CostEstimate(
            flops=flops, bytes_accessed=moved, transcendentals=transcendentals
        ),
    )(*rowed, *whole, *tokens)


def shifted_down(rows, step):
    return jnp.concatenate(
        [jnp.zeros((step, rows.shape[1]), rows.dtype), rows[:-step]], axis=0
    )


def shifted_up(rows, step):
    return jnp.concatenate(
        [rows[step:], jnp.zeros((step, rows.shape[1]), rows.dtype)], axis=0
    )


def inverse_rms(values):
    return lax.rsqrt(jnp.mean(values * values, axis=-1, keepdims=True) + EPSILON)


def norm_back(values, scale, weighted):
    return scale * weighted - values * (
        scale * scale * scale * jnp.mean(weighted * values, axis=-1, keepdims=True)
    )


def per_device(
    tokens,
    positions,
    cotangent,
    norm_gain,
    in_weight,
    conv_weight,
    out_weight,
    ffn_gain,
    gate_weight,
    up_weight,
    down_weight,
):
    shape = tokens.shape
    features = shape[2]
    rows = shape[0] * shape[1]
    share = in_weight.shape[0]
    hidden_share = down_weight.shape[0]
    hidden_width = gate_weight.shape[1]
    taps = conv_weight.shape[0]
    groups = lax.axis_size("g") * lax.axis_size("y")
    slots = lax.axis_size("s")
    chan_run = slots * share
    hid_run = slots * hidden_share
    chan = groups * chan_run
    hid = groups * hid_run

    def by_place(weight, parts, team, run):
        count = weight.shape[1] // (parts * team * run)
        split = weight.reshape(share, parts, count, team, run)
        return jnp.transpose(split, (3, 0, 1, 2, 4)).reshape(team, share, parts * count * run)

    def side_by_side(block, width):
        return jnp.concatenate(
            [block[..., j * share : (j + 1) * share, :width] for j in range(features // width)],
            axis=-1,
        )

    def stacked(block, width):
        return jnp.concatenate(
            [block[..., j * width : (j + 1) * width] for j in range(features // width)], axis=-2
        )

    in_blocks = by_place(in_weight, 3, TEAM, chan_run)
    in_mine = jnp.concatenate(exchange([in_blocks[j] for j in range(TEAM)]), axis=0)
    gains = jnp.concatenate([norm_gain, ffn_gain]).reshape(1, 2 * share)
    near_gains = team_rows(gains)
    gains_row = jnp.concatenate(reorder([near_gains[j : j + 1] for j in range(TEAM)]), axis=1)
    def as_row(values):
        return jnp.pad(values, ((0, 0), (0, features - values.shape[1])))

    first_pack = jnp.concatenate(
        [
            jnp.concatenate([in_mine, stacked(out_weight, chan)], axis=1),
            as_row(conv_weight.reshape(1, taps * share)),
            as_row(gains_row),
            jnp.zeros((EXTRA_ROWS - 2, features), bf16),
        ],
        axis=0,
    )
    tall = TEAM * share

    def first_unpack(block):
        return [
            block[:tall, : 3 * chan].reshape(TEAM, share, 3 * chan),
            side_by_side(block[:tall, 3 * chan :], chan),
            block[tall, : taps * share].reshape(taps, share),
            block[tall + 1, : 2 * tall].reshape(TEAM, 2, share),
        ]

    pair_blocks = jnp.concatenate(
        [by_place(gate_weight, 1, TEAM, hid_run), by_place(up_weight, 1, TEAM, hid_run)], axis=2
    )
    pair_mine = jnp.concatenate(exchange([pair_blocks[j] for j in range(TEAM)]), axis=0)

    first_all = lax.all_gather(first_pack, ("g", "y", "s"), axis=0, tiled=False)
    in_all, out_all, conv_all, gains_all = [
        part.reshape((groups, slots) + part.shape[1:]) for part in jax.vmap(first_unpack)(first_all)
    ]

    pair_all = lax.all_gather(pair_mine, ("g", "y", "s"), axis=0, tiled=False)
    down_full = lax.all_gather(down_weight, ("g", "y", "s"), axis=0, tiled=True)

    in_full = jnp.transpose(in_all, (0, 2, 1, 3, 4)).reshape(features, 3 * chan)
    out_full = out_all.reshape(chan, features)
    conv_full = jnp.transpose(conv_all, (2, 0, 1, 3)).reshape(taps, chan).astype(f32)
    gains_full = jnp.transpose(gains_all, (3, 0, 2, 1, 4)).reshape(2, features).astype(f32)
    norm_full, ffn_full = gains_full[0], gains_full[1]
    pair_full = jnp.transpose(
        pair_all.reshape(groups, slots, TEAM, share, 2 * hid), (0, 2, 1, 3, 4)
    ).reshape(features, 2 * hid)

    own_tokens = tokens.reshape(rows, features)
    places = positions.reshape(rows, 1)
    team_tokens = team_rows(own_tokens)
    team_places = team_rows(places)
    live = (places >= 0).astype(f32)
    upstream = cotangent.reshape(rows, features).astype(f32)
    ffn_pieces = team_pieces((live * upstream).astype(bf16))
    inputs = tokens.reshape(rows, features).astype(f32)

    values = team_tokens.astype(f32)
    early_full = after(norm_full, ffn_pieces[3][-1:])
    first_normed = (values * inverse_rms(values) * early_full).astype(bf16)
    projected = forward_dot(first_normed, in_full)
    b_part = projected[:, :chan]
    c_part = projected[:, chan : 2 * chan]
    x_part = projected[:, 2 * chan :]
    mixed = b_part * x_part
    mask_one = (team_places >= 1).astype(f32)
    mask_two = (team_places >= 2).astype(f32)
    mixed_one = mask_one * shifted_down(mixed, 1)
    mixed_two = mask_two * shifted_down(mixed, 2)
    convolved = conv_full[0] * mixed + conv_full[1] * mixed_one + conv_full[2] * mixed_two
    mixer_in = (c_part * convolved).astype(bf16)
    mixer_out = team_sum(forward_dot(mixer_in, out_full).astype(bf16))
    middle = inputs + live * mixer_out[0]
    second_scale = inverse_rms(middle)
    second_pieces = team_pieces((middle * second_scale * ffn_full).astype(bf16))

    team_count = TEAM * rows
    unit = 2 * team_count * features * hid
    hidden, silu, slope, second_normed, ffn_grad = by_rows(
        forward_kernel,
        rows,
        TEAM,
        [],
        second_pieces + ffn_pieces + [pair_full],
        [],
        [hid] * 3 + [features] * 2,
        2 * unit,
        team_count * hid,
    )
    down_part = rows_dot(hidden, ffn_grad).astype(bf16)
    grad_down = scatter(down_part.reshape(groups, slots, hidden_share, features))
    pair_grad, normed_part = by_rows(
        backward_kernel,
        ROW_TILE,
        team_count // ROW_TILE,
        [ffn_grad, silu, slope],
        [pair_full, down_full],
        [down_part],
        [2 * hid, features],
        3 * unit,
        0,
    )

    def by_owner(grad, team):
        width = grad.shape[-1]
        count = features // (team * slots * share)
        split = grad.astype(bf16).reshape(count, team, slots, share, width)
        return jnp.transpose(split, (0, 2, 1, 3, 4)).reshape(count, slots, team * share, width)

    pair_part = by_owner(rows_dot(second_normed, pair_grad), TEAM)
    normed_sum, _ = team_sum(normed_part, pair_part[0, 0, :1])
    second_weighted = ffn_full * normed_sum
    middle_grad = upstream + norm_back(middle, second_scale, second_weighted)

    mixer_grad = team_rows((live * middle_grad).astype(bf16))
    mixer_in_grad = back_dot(mixer_grad, out_full)
    c_grad = mixer_in_grad * convolved
    conv_grad = mixer_in_grad * c_part
    conv_back = after(conv_full, grad_down[:1])
    mixed_grad = (
        conv_back[0] * conv_grad
        + conv_back[1] * shifted_up(mask_one * conv_grad, 1)
        + conv_back[2] * shifted_up(mask_two * conv_grad, 2)
    )
    projected_grad = jnp.concatenate(
        [mixed_grad * x_part, c_grad, mixed_grad * b_part], axis=1
    ).astype(bf16)
    grad_conv_part = jnp.stack(
        [
            jnp.sum(conv_grad * mixed, axis=0),
            jnp.sum(conv_grad * mixed_one, axis=0),
            jnp.sum(conv_grad * mixed_two, axis=0),
        ]
    )
    out_sum, _ = team_sum(forward_dot(hidden, down_full).astype(bf16))
    block_out = (middle + live * out_sum).astype(bf16)
    in_part = by_owner(rows_dot(first_normed, projected_grad), TEAM)
    out_grad_part = rows_dot(mixer_in, mixer_grad).astype(bf16)
    out_grad_part = stacked(out_grad_part.reshape(groups, slots, share, features), chan)
    conv_rows = jnp.transpose(
        grad_conv_part.reshape(taps, groups, slots, share), (1, 2, 0, 3)
    ).reshape(groups, slots, 1, taps * share)
    conv_rows = jnp.pad(
        after(conv_rows, block_out[:1]).astype(bf16),
        ((0, 0), (0, 0), (0, EXTRA_ROWS - 1), (0, features - taps * share)),
    )
    pair_sum = scatter(pair_part)
    first_weighted, first_sent = team_sum(back_dot(projected_grad, in_full).astype(bf16))
    input_grad = middle_grad + norm_back(inputs, inverse_rms(inputs), norm_full * first_weighted)
    input_grad = input_grad.astype(bf16)
    first_sum = scatter(
        jnp.concatenate(
            [jnp.concatenate([in_part, out_grad_part], axis=3), conv_rows], axis=2
        ),
        pair_sum[:1],
        first_sent,
    )

    def own_rows(summed, parts, team, run):
        blocks = [summed[j * share : (j + 1) * share].astype(bf16) for j in range(team)]
        came = [block.reshape(share, parts, -1, 1, run) for block in exchange(blocks)]
        joined = jnp.concatenate(came, axis=3)
        return joined.reshape(share, -1).astype(f32)

    pair_rows = own_rows(pair_sum, 2, TEAM, hid_run)
    gate_rows = pair_rows[:, :hidden_width]
    up_rows = pair_rows[:, hidden_width:]
    in_rows = own_rows(first_sum[:tall, : 3 * chan], 3, TEAM, chan_run)
    grad_out = side_by_side(first_sum[:tall, 3 * chan :], chan).astype(f32)
    grad_conv = first_sum[tall, : taps * share].reshape(taps, share).astype(f32)
    grad_norm_gain = jnp.sum(in_weight.astype(f32) * in_rows, axis=1) / norm_gain.astype(f32)
    grad_ffn_gain = jnp.sum(
        gate_weight.astype(f32) * gate_rows + up_weight.astype(f32) * up_rows, axis=1
    ) / ffn_gain.astype(f32)
    return (
        block_out.reshape(shape),
        input_grad.reshape(shape),
        grad_norm_gain,
        in_rows,
        grad_conv,
        grad_out,
        grad_ffn_gain,
        gate_rows,
        up_rows,
        grad_down.astype(f32),
    )


def solution(mesh):
    every = ("g", "y", "x", "c", "s")
    outer = mesh.shape["dp"] // (2 * TEAM)
    teams = Mesh(mesh.devices.reshape(outer, 2, 2, 2, mesh.shape["shard"]), every)
    return jax.shard_map(
        per_device,
        mesh=teams,
        in_specs=(
            P(None, every, None),
            P(None, every),
            P(None, every, None),
            P(every),
            P(every, None),
            P(None, every),
            P(every, None),
            P(every),
            P(every, None),
            P(every, None),
            P(every, None),
        ),
        out_specs=(
            P(None, every, None),
            P(None, every, None),
            P(every),
            P(every, None),
            P(None, every),
            P(every, None),
            P(every),
            P(every, None),
            P(every, None),
            P(every, None),
        ),
        check_vma=False,
    )
```

```python
import jax
import jax.numpy as jnp
from jax import lax
from jax.experimental import pallas as pl
from jax.experimental.pallas import tpu as pltpu
from jax.sharding import Mesh, PartitionSpec as P

EPSILON = 1e-05
TEAM = 4
EXTRA_ROWS = 16
ROW_TILE = 512
bf16 = jnp.bfloat16
f32 = jnp.float32


def forward_dot(left_side, right_side):
    return jnp.dot(left_side, right_side, preferred_element_type=f32)


def rows_dot(left_side, right_side):
    return lax.dot_general(
        left_side, right_side, (((0,), (0,)), ((), ())), preferred_element_type=f32
    )


def back_dot(left_side, right_side):
    return lax.dot_general(
        left_side, right_side, (((1,), (1,)), ((), ())), preferred_element_type=f32
    )


def swap_core(values):
    return lax.ppermute(values, "c", [(0, 1), (1, 0)])


def swap_chip(values):
    return lax.ppermute(values, "x", [(0, 1), (1, 0)])


def swap_row(values):
    return lax.ppermute(values, "y", [(0, 1), (1, 0)])


def swap_far(values, distance):
    return lax.ppermute(values, ("x", "c"), [(i, i ^ distance) for i in range(TEAM)])


def after(values, token):
    return values + (token.ravel()[0] * 0).astype(values.dtype)


def reorder(blocks):
    blocks = list(blocks)
    for bit, axis in ((1, "c"), (2, "x")):
        odd = lax.axis_index(axis) == 1
        blocks = [jnp.where(odd, blocks[j ^ bit], blocks[j]) for j in range(len(blocks))]
    return blocks


def exchange(blocks):
    near = reorder(blocks)
    return reorder(near[:1] + [swap_far(near[j], j) for j in range(1, len(near))])


def team_pieces(rows):
    across = swap_chip(rows)
    return [rows, swap_core(rows), across, swap_core(across)]


def team_rows(rows):
    return jnp.concatenate(team_pieces(rows), axis=0)


def team_sum(terms, token=None, gate=None):
    count = terms.shape[0] // TEAM
    sent = jnp.concatenate([terms[count : 2 * count], terms[3 * count :]], axis=0)
    came = swap_core(sent).astype(f32)
    own = terms[:count].astype(f32) + came[:count]
    other = terms[2 * count : 3 * count].astype(f32) + came[count:]
    other = (other if gate is None else after(other, gate)).astype(bf16)
    came = swap_chip(other).astype(f32)
    return own + (came if token is None else after(came, token)), other[:1, :1]


def take(blocks, index):
    return lax.dynamic_index_in_dim(blocks, index, axis=0, keepdims=False)


def scatter(part, *tokens):
    groups, slots = part.shape[:2]
    if groups == 2:
        row = lax.axis_index("y")
        came = swap_row(take(part, 1 - row)).astype(f32)
        for token in tokens:
            came = after(came, token)
        summed = (take(part, row).astype(f32) + came).astype(bf16)
        return lax.psum_scatter(summed, "s", scatter_dimension=0, tiled=False)
    flat = part.reshape((groups * slots,) + part.shape[2:]).astype(f32)
    return lax.psum_scatter(flat, ("g", "y", "s"), scatter_dimension=0, tiled=False)


def forward_kernel(*refs):
    pieces, pair_ref = refs[: 2 * TEAM], refs[2 * TEAM]
    hidden_ref, silu_ref, slope_ref, normed_ref, grad_ref = refs[2 * TEAM + 1 :]
    for k in range(TEAM):

        @pl.when(pl.program_id(0) == k)
        def _():
            normed_ref[...] = pieces[k][...]
            grad_ref[...] = pieces[TEAM + k][...]

    width = hidden_ref.shape[1]
    values = forward_dot(normed_ref[...], pair_ref[...])
    gate_value, up_value = values[:, :width], values[:, width:]
    sigmoid = jax.nn.sigmoid(gate_value)
    silu = gate_value * sigmoid
    hidden_ref[...] = (silu * up_value).astype(bf16)
    silu_ref[...] = silu.astype(bf16)
    slope_ref[...] = (up_value * (sigmoid * (1 + gate_value * (1 - sigmoid)))).astype(bf16)


def backward_kernel(
    grad_ref, silu_ref, slope_ref, pair_ref, down_ref, token_ref, pair_grad_ref, normed_ref
):
    del token_ref
    width = silu_ref.shape[1]
    hidden_grad = back_dot(grad_ref[...], down_ref[...])
    pair_grad_ref[:, :width] = (hidden_grad * slope_ref[...].astype(f32)).astype(bf16)
    pair_grad_ref[:, width:] = (hidden_grad * silu_ref[...].astype(f32)).astype(bf16)
    normed_ref[...] = back_dot(pair_grad_ref[...], pair_ref[...]).astype(bf16)


def by_rows(kernel, tile, steps, rowed, whole, tokens, columns, flops, transcendentals):
    rows = steps * tile

    def row_block(count):
        return pl.BlockSpec((tile, count), lambda i: (i, 0))

    moved = sum(2 * value.size for value in rowed + whole) + 2 * rows * sum(columns)
    return pl.pallas_call(
        kernel,
        grid=(steps,),
        in_specs=[row_block(value.shape[1]) for value in rowed]
        + [
            pl.BlockSpec(value.shape, lambda i: (0, 0), pipeline_mode=pl.Buffered(1))
            for value in whole
        ]
        + [pl.BlockSpec(memory_space=pl.ANY)] * len(tokens),
        out_specs=[row_block(count) for count in columns],
        out_shape=[jax.ShapeDtypeStruct((rows, count), bf16) for count in columns],
        compiler_params=pltpu.CompilerParams(vmem_limit_bytes=52 * 1024 * 1024),
        cost_estimate=pl.CostEstimate(
            flops=flops, bytes_accessed=moved, transcendentals=transcendentals
        ),
    )(*rowed, *whole, *tokens)


def shifted_down(rows, step):
    return jnp.concatenate(
        [jnp.zeros((step, rows.shape[1]), rows.dtype), rows[:-step]], axis=0
    )


def shifted_up(rows, step):
    return jnp.concatenate(
        [rows[step:], jnp.zeros((step, rows.shape[1]), rows.dtype)], axis=0
    )


def inverse_rms(values):
    return lax.rsqrt(jnp.mean(values * values, axis=-1, keepdims=True) + EPSILON)


def norm_back(values, scale, weighted):
    return scale * weighted - values * (
        scale * scale * scale * jnp.mean(weighted * values, axis=-1, keepdims=True)
    )


def per_device(
    tokens,
    positions,
    cotangent,
    norm_gain,
    in_weight,
    conv_weight,
    out_weight,
    ffn_gain,
    gate_weight,
    up_weight,
    down_weight,
):
    shape = tokens.shape
    features = shape[2]
    rows = shape[0] * shape[1]
    share = in_weight.shape[0]
    hidden_share = down_weight.shape[0]
    hidden_width = gate_weight.shape[1]
    taps = conv_weight.shape[0]
    groups = lax.axis_size("g") * lax.axis_size("y")
    slots = lax.axis_size("s")
    chan_run = slots * share
    hid_run = slots * hidden_share
    chan = groups * chan_run
    hid = groups * hid_run

    def by_place(weight, parts, team, run):
        count = weight.shape[1] // (parts * team * run)
        split = weight.reshape(share, parts, count, team, run)
        return jnp.transpose(split, (3, 0, 1, 2, 4)).reshape(team, share, parts * count * run)

    def side_by_side(block, width):
        return jnp.concatenate(
            [block[..., j * share : (j + 1) * share, :width] for j in range(features // width)],
            axis=-1,
        )

    def stacked(block, width):
        return jnp.concatenate(
            [block[..., j * width : (j + 1) * width] for j in range(features // width)], axis=-2
        )

    in_blocks = by_place(in_weight, 3, TEAM, chan_run)
    in_mine = jnp.concatenate(exchange([in_blocks[j] for j in range(TEAM)]), axis=0)
    gains = jnp.concatenate([norm_gain, ffn_gain]).reshape(1, 2 * share)
    near_gains = team_rows(gains)
    gains_row = jnp.concatenate(reorder([near_gains[j : j + 1] for j in range(TEAM)]), axis=1)
    def as_row(values):
        return jnp.pad(values, ((0, 0), (0, features - values.shape[1])))

    first_pack = jnp.concatenate(
        [
            jnp.concatenate([in_mine, stacked(out_weight, chan)], axis=1),
            as_row(conv_weight.reshape(1, taps * share)),
            as_row(gains_row),
            jnp.zeros((EXTRA_ROWS - 2, features), bf16),
        ],
        axis=0,
    )
    tall = TEAM * share

    def first_unpack(block):
        return [
            block[:tall, : 3 * chan].reshape(TEAM, share, 3 * chan),
            side_by_side(block[:tall, 3 * chan :], chan),
            block[tall, : taps * share].reshape(taps, share),
            block[tall + 1, : 2 * tall].reshape(TEAM, 2, share),
        ]

    pair_blocks = jnp.concatenate(
        [by_place(gate_weight, 1, TEAM, hid_run), by_place(up_weight, 1, TEAM, hid_run)], axis=2
    )
    pair_mine = jnp.concatenate(exchange([pair_blocks[j] for j in range(TEAM)]), axis=0)

    first_all = lax.all_gather(first_pack, ("g", "y", "s"), axis=0, tiled=False)
    in_all, out_all, conv_all, gains_all = [
        part.reshape((groups, slots) + part.shape[1:]) for part in jax.vmap(first_unpack)(first_all)
    ]

    pair_all = lax.all_gather(pair_mine, ("g", "y", "s"), axis=0, tiled=False)
    down_full = lax.all_gather(down_weight, ("g", "y", "s"), axis=0, tiled=True)

    in_full = jnp.transpose(in_all, (0, 2, 1, 3, 4)).reshape(features, 3 * chan)
    out_full = out_all.reshape(chan, features)
    conv_full = jnp.transpose(conv_all, (2, 0, 1, 3)).reshape(taps, chan).astype(f32)
    gains_full = jnp.transpose(gains_all, (3, 0, 2, 1, 4)).reshape(2, features).astype(f32)
    norm_full, ffn_full = gains_full[0], gains_full[1]
    pair_full = jnp.transpose(
        pair_all.reshape(groups, slots, TEAM, share, 2 * hid), (0, 2, 1, 3, 4)
    ).reshape(features, 2 * hid)

    own_tokens = tokens.reshape(rows, features)
    places = positions.reshape(rows, 1)
    team_tokens = team_rows(own_tokens)
    team_places = team_rows(places)
    live = (places >= 0).astype(f32)
    upstream = cotangent.reshape(rows, features).astype(f32)
    ffn_pieces = team_pieces((live * upstream).astype(bf16))
    inputs = tokens.reshape(rows, features).astype(f32)

    values = team_tokens.astype(f32)
    early_full = after(norm_full, ffn_pieces[3][-1:])
    first_normed = (values * inverse_rms(values) * early_full).astype(bf16)
    projected = forward_dot(first_normed, in_full)
    b_part = projected[:, :chan]
    c_part = projected[:, chan : 2 * chan]
    x_part = projected[:, 2 * chan :]
    mixed = b_part * x_part
    mask_one = (team_places >= 1).astype(f32)
    mask_two = (team_places >= 2).astype(f32)
    mixed_one = mask_one * shifted_down(mixed, 1)
    mixed_two = mask_two * shifted_down(mixed, 2)
    convolved = conv_full[0] * mixed + conv_full[1] * mixed_one + conv_full[2] * mixed_two
    mixer_in = (c_part * convolved).astype(bf16)
    mixer_out = team_sum(forward_dot(mixer_in, out_full).astype(bf16))
    middle = inputs + live * mixer_out[0]
    second_scale = inverse_rms(middle)
    second_pieces = team_pieces((middle * second_scale * ffn_full).astype(bf16))

    team_count = TEAM * rows
    unit = 2 * team_count * features * hid
    hidden, silu, slope, second_normed, ffn_grad = by_rows(
        forward_kernel,
        rows,
        TEAM,
        [],
        second_pieces + ffn_pieces + [pair_full],
        [],
        [hid] * 3 + [features] * 2,
        2 * unit,
        team_count * hid,
    )
    down_part = rows_dot(hidden, ffn_grad).astype(bf16)
    grad_down = scatter(down_part.reshape(groups, slots, hidden_share, features))
    pair_grad, normed_part = by_rows(
        backward_kernel,
        ROW_TILE,
        team_count // ROW_TILE,
        [ffn_grad, silu, slope],
        [pair_full, down_full],
        [down_part],
        [2 * hid, features],
        3 * unit,
        0,
    )

    def by_owner(grad, team):
        width = grad.shape[-1]
        count = features // (team * slots * share)
        split = grad.astype(bf16).reshape(count, team, slots, share, width)
        return jnp.transpose(split, (0, 2, 1, 3, 4)).reshape(count, slots, team * share, width)

    pair_part = by_owner(rows_dot(second_normed, pair_grad), TEAM)
    normed_sum, _ = team_sum(normed_part, pair_part[0, 0, :1])
    second_weighted = ffn_full * normed_sum
    middle_grad = upstream + norm_back(middle, second_scale, second_weighted)

    mixer_grad = team_rows((live * middle_grad).astype(bf16))
    mixer_in_grad = back_dot(mixer_grad, out_full)
    c_grad = mixer_in_grad * convolved
    conv_grad = mixer_in_grad * c_part
    conv_back = after(conv_full, grad_down[:1])
    mixed_grad = (
        conv_back[0] * conv_grad
        + conv_back[1] * shifted_up(mask_one * conv_grad, 1)
        + conv_back[2] * shifted_up(mask_two * conv_grad, 2)
    )
    projected_grad = jnp.concatenate(
        [mixed_grad * x_part, c_grad, mixed_grad * b_part], axis=1
    ).astype(bf16)
    grad_conv_part = jnp.stack(
        [
            jnp.sum(conv_grad * mixed, axis=0),
            jnp.sum(conv_grad * mixed_one, axis=0),
            jnp.sum(conv_grad * mixed_two, axis=0),
        ]
    )
    out_sum, _ = team_sum(
        forward_dot(hidden, down_full).astype(bf16), gate=mixer_grad[-1:]
    )
    block_out = (middle + live * out_sum).astype(bf16)
    in_part = by_owner(rows_dot(first_normed, projected_grad), TEAM)
    out_grad_part = rows_dot(mixer_in, mixer_grad).astype(bf16)
    out_grad_part = stacked(out_grad_part.reshape(groups, slots, share, features), chan)
    conv_rows = jnp.transpose(
        grad_conv_part.reshape(taps, groups, slots, share), (1, 2, 0, 3)
    ).reshape(groups, slots, 1, taps * share)
    conv_rows = jnp.pad(
        after(conv_rows, block_out[:1]).astype(bf16),
        ((0, 0), (0, 0), (0, EXTRA_ROWS - 1), (0, features - taps * share)),
    )
    pair_sum = scatter(pair_part)
    first_weighted, first_sent = team_sum(back_dot(projected_grad, in_full).astype(bf16))
    input_grad = middle_grad + norm_back(inputs, inverse_rms(inputs), norm_full * first_weighted)
    input_grad = input_grad.astype(bf16)
    first_sum = scatter(
        jnp.concatenate(
            [jnp.concatenate([in_part, out_grad_part], axis=3), conv_rows], axis=2
        ),
        pair_sum[:1],
        first_sent,
    )

    def own_rows(summed, parts, team, run):
        blocks = [summed[j * share : (j + 1) * share].astype(bf16) for j in range(team)]
        came = [block.reshape(share, parts, -1, 1, run) for block in exchange(blocks)]
        joined = jnp.concatenate(came, axis=3)
        return joined.reshape(share, -1).astype(f32)

    pair_rows = own_rows(pair_sum, 2, TEAM, hid_run)
    gate_rows = pair_rows[:, :hidden_width]
    up_rows = pair_rows[:, hidden_width:]
    in_rows = own_rows(first_sum[:tall, : 3 * chan], 3, TEAM, chan_run)
    grad_out = side_by_side(first_sum[:tall, 3 * chan :], chan).astype(f32)
    grad_conv = first_sum[tall, : taps * share].reshape(taps, share).astype(f32)
    grad_norm_gain = jnp.sum(in_weight.astype(f32) * in_rows, axis=1) / norm_gain.astype(f32)
    grad_ffn_gain = jnp.sum(
        gate_weight.astype(f32) * gate_rows + up_weight.astype(f32) * up_rows, axis=1
    ) / ffn_gain.astype(f32)
    return (
        block_out.reshape(shape),
        input_grad.reshape(shape),
        grad_norm_gain,
        in_rows,
        grad_conv,
        grad_out,
        grad_ffn_gain,
        gate_rows,
        up_rows,
        grad_down.astype(f32),
    )


def solution(mesh):
    every = ("g", "y", "x", "c", "s")
    outer = mesh.shape["dp"] // (2 * TEAM)
    teams = Mesh(mesh.devices.reshape(outer, 2, 2, 2, mesh.shape["shard"]), every)
    return jax.shard_map(
        per_device,
        mesh=teams,
        in_specs=(
            P(None, every, None),
            P(None, every),
            P(None, every, None),
            P(every),
            P(every, None),
            P(None, every),
            P(every, None),
            P(every),
            P(every, None),
            P(every, None),
            P(every, None),
        ),
        out_specs=(
            P(None, every, None),
            P(None, every, None),
            P(every),
            P(every, None),
            P(None, every),
            P(every, None),
            P(every),
            P(every, None),
            P(every, None),
            P(every, None),
        ),
        check_vma=False,
    )
```
